128 devices in a mesh: dp: 32 (over y, z, core), ctx: 4 (over x).
Axes of the slice: x: 4, y: 4, z: 4, core: 2. Of those that a mesh axis runs over, the one named last changes fastest.
Arguments:
- tokens: bfloat16 [16384, 1024], P(('dp', 'ctx')), may hold values from -6 to 6
- cotangent: bfloat16 [16384, 1024], P(('dp', 'ctx')), may hold values from -6 to 6
- packed_pos: int32 [16384], P(('dp', 'ctx')), may hold values from 0 to 16383, as said below
- segment_ids: int32 [32, 512], P('dp'), may hold values from 0 to 7, never falling along the last dimension, each value on 1 to 256 neighbouring positions
- w_proj: bfloat16 [1024, 16, 256], P(None, 'ctx'), may hold values from -0.1875 to 0.1875
- w_out: bfloat16 [1024, 1024], replicated, may hold values from -0.1875 to 0.1875
Outputs:
- layer_out: bfloat16 [16384, 1024], P(('dp', 'ctx'))
- input_grad: bfloat16 [16384, 1024], P(('dp', 'ctx'))
- proj_grad: float32 [1024, 16, 256], P(None, 'ctx')
- out_grad: float32 [1024, 1024], P('ctx')
The draws below stay inside these ranges and needn't reach their ends.
Inputs may be any that keep to these rules, and one draw needn't show every extreme that they name: packed_pos is a permutation that keeps each row's index of ctx; the rows of one device go to every index of dp, at most 6 rows to any one of them, and every device receives 128 rows.
All inputs are finite; a program needn't handle non-finite values.
Results may differ from the reference program's by a relative error of at most 0.02.
Values may be sent and summed in bfloat16 or wider, within the bound.
A program may use at most 128 MiB of HBM per device.

```python
import math
import jax
import jax.numpy as jnp
import numpy as np
from jax import lax

D = 1024
H = 16
DH = 64
HISTS = 8
TOK_DEV = 128
GROUP = 512
TOKENS = 16384
N_DP = 32
N_CTX = 4


def draw_packed_pos(key, part):
    key = jax.random.fold_in(key, 11)
    unit = TOK_DEV // (2 * N_DP)
    half = N_DP // 2
    row_index = jnp.arange(TOK_DEV, dtype=jnp.int32)
    piece = jnp.where(row_index < half * 3 * unit, row_index // (3 * unit), half + (row_index - half * 3 * unit) // unit)
    sources = jnp.arange(N_DP, dtype=jnp.int32)
    columns = []
    for column in range(N_CTX):
        column_key = jax.random.fold_in(key, column)
        first_key, second_key = jax.random.split(column_key)
        offsets = jax.random.permutation(first_key, N_DP).astype(jnp.int32)
        orders = jax.vmap(lambda inner: jax.random.permutation(inner, TOK_DEV))(jax.random.split(second_key, N_DP)).astype(jnp.int32)
        target = (sources[:, None] + offsets[piece][None, :]) % N_DP
        target_row = orders[target, row_index[None, :]]
        columns.append(target * (N_CTX * TOK_DEV) + column * TOK_DEV + target_row)
    whole = jnp.stack(columns, axis=1)
    return whole.reshape(-1).astype(jnp.int32)


def steps_of(rng, shape, cuts, least, largest):
    gain, own = 1.0, jax.random.fold_in(rng, 6)
    for axis_at, parts in cuts:
        heights = jnp.exp(jax.random.uniform(jax.random.fold_in(own, axis_at), (parts,), jnp.float32, least / len(cuts), largest / len(cuts)))
        gain = gain * jnp.repeat(heights, shape[axis_at] // parts).reshape([-1 if axis == axis_at else 1 for axis in range(len(shape))])
    return gain


def length_profile(amount, total, bound, slope):
    loads = [(1 << 20) // math.isqrt(rank ** slope) + 1 for rank in range(2, amount + 1)]
    rest, holding = total - bound - (amount - 1), [1] * (amount - 1)
    while rest > 0:
        free = [i for i in range(amount - 1) if holding[i] < bound]
        mass, budget = sum([loads[i] for i in free]), rest
        for i in free:
            more = min(bound - holding[i], max(1, budget * loads[i] // mass), rest)
            holding[i] = holding[i] + more
            rest = rest - more
    return np.array([bound] + holding)


def uneven(key, number_of, total, reach, lean):
    if number_of == 2:
        one = jax.random.randint(key, (), max(1, total - reach), min(reach, total - 1) + 1)
        return jnp.stack([one, total - one])
    lengths = jnp.asarray(length_profile(number_of, total, reach, lean), jnp.int32)
    pairs = (number_of - 1) // 2
    donor, receiver = lengths[1:1 + 2 * pairs:2], lengths[2:2 + 2 * pairs:2]
    margin = jnp.minimum(donor - 1, reach - receiver)
    passed = jax.random.randint(jax.random.fold_in(key, 1), (pairs,), 0, 1 << 20) % (margin + 1)
    lengths = lengths.at[1:1 + 2 * pairs:2].set(donor - passed).at[2:2 + 2 * pairs:2].set(receiver + passed)
    return lengths[jax.random.permutation(jax.random.fold_in(key, 2), number_of)]


def gaussian(rng, dims, width, bound, pieces=(), held_as=jnp.bfloat16):
    array = jax.random.normal(rng, dims, jnp.float32) * width
    if len(pieces) > 0:
        array = steps_of(rng, dims, pieces, -0.22, 0.18) * array
    return jnp.clip(array, min=-bound, max=bound).astype(held_as)


def setup_inputs(seed: int = 0) -> dict:
    seeds = jax.random.split(jax.random.key(seed), 7)
    tokens = gaussian(seeds[0], (TOKENS, D), 1.0, 6.0, ((0, 128),))
    cotangent = gaussian(seeds[1], (TOKENS, D), 1.0, 6.0, ((0, 128),))
    packed_pos = draw_packed_pos(jax.random.fold_in(seeds[6], 71), 0)
    segment_ids = jax.vmap(lambda own: jnp.searchsorted(jnp.cumsum(uneven(own, HISTS, GROUP, GROUP // 2, 1)), jnp.arange(GROUP), side="right"))(jax.random.split(seeds[3], N_DP)).reshape((N_DP, GROUP)).astype(jnp.int32)
    w_proj = gaussian(seeds[4], (D, H, 4 * DH), D ** -0.5, 0.1875, ((1, 4),))
    w_out = gaussian(seeds[5], (H * DH, D), (H * DH) ** -0.5, 0.1875)
    return dict(tokens=tokens, cotangent=cotangent, packed_pos=packed_pos, segment_ids=segment_ids, w_proj=w_proj, w_out=w_out)


EPS = 1e-05

def silu_slope(t):
    sig = jax.nn.sigmoid(t)
    return sig * (1.0 + t * (1.0 - sig))

def block_mask(seg, start, block):
    rows_here = start + jnp.arange(block, dtype=jnp.int32)
    keys_all = jnp.arange(seg.shape[0], dtype=jnp.int32)
    seg_here = lax.dynamic_slice_in_dim(seg, start, block, 0)
    return (seg_here[:, None] == seg[None, :]) & (keys_all[None, :] <= rows_here[:, None])

def attend(query, keys, values, seg, alpha, block):
    count = query.shape[0] // block

    def one_block(index):
        start = (index * block).astype(jnp.int32)
        q_here = lax.dynamic_slice_in_dim(query, start, block, 0).astype(jnp.float32)
        score = alpha * jnp.einsum('ihd,jhd->hij', q_here, keys.astype(jnp.float32))
        mask = block_mask(seg, start, block)
        weight = jnp.where(mask[None], jax.nn.silu(score), 0.0).astype(jnp.bfloat16)
        return jnp.einsum('hij,jhd->ihd', weight.astype(jnp.float32), values.astype(jnp.float32))
    outs = lax.map(one_block, jnp.arange(count, dtype=jnp.int32))
    return outs.reshape(query.shape)

def attend_grad(query, keys, values, d_out, seg, alpha, block):
    count = query.shape[0] // block
    keys_f = keys.astype(jnp.float32)
    values_f = values.astype(jnp.float32)

    def one_block(carry, index):
        d_keys, d_values = carry
        start = (index * block).astype(jnp.int32)
        q_here = lax.dynamic_slice_in_dim(query, start, block, 0).astype(jnp.float32)
        g_here = lax.dynamic_slice_in_dim(d_out, start, block, 0).astype(jnp.float32)
        score = alpha * jnp.einsum('ihd,jhd->hij', q_here, keys_f)
        mask = block_mask(seg, start, block)[None]
        weight = jnp.where(mask, jax.nn.silu(score), 0.0).astype(jnp.bfloat16).astype(jnp.float32)
        d_weight = jnp.einsum('ihd,jhd->hij', g_here, values_f)
        d_values = d_values + jnp.einsum('hij,ihd->jhd', weight, g_here)
        d_score = jnp.where(mask, d_weight * silu_slope(score) * alpha, 0.0).astype(jnp.bfloat16).astype(jnp.float32)
        d_query = jnp.einsum('hij,jhd->ihd', d_score, keys_f)
        d_keys = d_keys + jnp.einsum('hij,ihd->jhd', d_score, q_here)
        return ((d_keys, d_values), d_query)
    zeros = jnp.zeros(query.shape, jnp.float32)
    (d_keys, d_values), d_query = lax.scan(one_block, (zeros, zeros), jnp.arange(count, dtype=jnp.int32))
    return (d_query.reshape(query.shape), d_keys, d_values)

def one_group(x_group, group_out_gradient, seg, w_proj, w_out):
    block = 512 if GROUP % 512 == 0 else GROUP
    alpha = DH ** (-0.5)
    rows = x_group.shape[0]
    input_float = x_group.astype(jnp.float32)
    first_mean1 = lax.optimization_barrier(jnp.mean(input_float, axis=1, keepdims=True))
    inverse_deviation = lax.rsqrt(lax.optimization_barrier(jnp.mean((input_float - first_mean1) ** 2, axis=1, keepdims=True)) + EPS)
    centered_scaled_input = (input_float - first_mean1) * inverse_deviation
    layer_normalized = centered_scaled_input.astype(jnp.bfloat16)
    w_flat = w_proj.reshape(D, H * 4 * DH)
    pre = jnp.dot(layer_normalized, w_flat, preferred_element_type=jnp.float32)
    act = jax.nn.silu(pre).astype(jnp.bfloat16).reshape(rows, H, 4, DH)
    gate_u, val, query, keys = (act[:, :, 0], act[:, :, 1], act[:, :, 2], act[:, :, 3])
    attn = attend(query, keys, val, seg, alpha, block).astype(jnp.bfloat16).reshape(rows, H * DH)
    a_f = attn.astype(jnp.float32)
    mean2 = lax.optimization_barrier(jnp.mean(a_f, axis=1, keepdims=True))
    r_two = lax.rsqrt(lax.optimization_barrier(jnp.mean((a_f - mean2) ** 2, axis=1, keepdims=True)) + EPS)
    onorm = (a_f - mean2) * r_two
    u_f = gate_u.reshape(rows, H * DH).astype(jnp.float32)
    gated = (onorm * u_f).astype(jnp.bfloat16)
    y_group = (input_float + jnp.dot(gated, w_out, preferred_element_type=jnp.float32)).astype(jnp.bfloat16)
    d_wout = jnp.dot(gated.T, group_out_gradient, preferred_element_type=jnp.float32)
    dgated = jnp.dot(group_out_gradient, w_out.T, preferred_element_type=jnp.float32)
    d_gate = (dgated * onorm).astype(jnp.bfloat16)
    e_term = dgated * u_f
    d_attn = (r_two * (e_term - lax.optimization_barrier(jnp.mean(e_term, axis=1, keepdims=True)) - onorm * lax.optimization_barrier(jnp.mean(e_term * onorm, axis=1, keepdims=True)))).astype(jnp.bfloat16)
    d_query, d_keys, d_values = attend_grad(query, keys, val, d_attn.reshape(rows, H, DH), seg, alpha, block)
    d_act = jnp.stack([d_gate.reshape(rows, H, DH).astype(jnp.float32), d_values, d_query, d_keys], axis=2)
    d_pre = (d_act.reshape(rows, H * 4 * DH) * silu_slope(pre)).astype(jnp.bfloat16)
    d_wproj = jnp.dot(layer_normalized.T, d_pre, preferred_element_type=jnp.float32)
    normalized_gradient = jnp.dot(d_pre, w_flat.T, preferred_element_type=jnp.float32)
    group_input_gradient = (group_out_gradient.astype(jnp.float32) + inverse_deviation * (normalized_gradient - lax.optimization_barrier(jnp.mean(normalized_gradient, axis=1, keepdims=True)) - centered_scaled_input * lax.optimization_barrier(jnp.mean(normalized_gradient * centered_scaled_input, axis=1, keepdims=True)))).astype(jnp.bfloat16)
    return (y_group, group_input_gradient, d_wproj, d_wout)

def reference(tokens, cotangent, packed_pos, segment_ids, w_proj, w_out):
    x_packed = jnp.zeros_like(tokens).at[packed_pos].set(tokens)
    g_packed = jnp.zeros_like(cotangent).at[packed_pos].set(cotangent)
    x_groups = x_packed.reshape(N_DP, GROUP, D)
    g_groups = g_packed.reshape(N_DP, GROUP, D)

    def step(carry, items):
        x_group, group_out_gradient, seg = items
        y_group, group_input_gradient, d_wproj, d_wout = one_group(x_group, group_out_gradient, seg, w_proj, w_out)
        return ((carry[0] + d_wproj, carry[1] + d_wout), (y_group, group_input_gradient))
    start = (jnp.zeros((D, H * 4 * DH), jnp.float32), jnp.zeros((H * DH, D), jnp.float32))
    (sum_proj, sum_out), (y_all, dx_all) = lax.scan(step, start, (x_groups, g_groups, segment_ids))
    scale = TOKENS ** (-0.5)
    y_packed = y_all.reshape(TOKENS, D)
    dx_packed = dx_all.reshape(TOKENS, D)
    return (y_packed[packed_pos], dx_packed[packed_pos], (sum_proj * scale).reshape(D, H, 4 * DH), sum_out * scale)
```

```python
import functools
import jax
import jax.numpy as jnp
from jax import lax
from jax.experimental import pallas as pl
from jax.experimental.pallas import tpu as pltpu
from jax.sharding import PartitionSpec as P

EPS = 1e-05
MESH = pl.DeviceIdType.MESH
bf16, f32, i32 = jnp.bfloat16, jnp.float32, jnp.int32
ROWS, WIDTH, GROUP, SLOTS = 128, 1024, 512, 16
CAP = 6
COMBOS = [(L, c) for L in range(3) for c in range(8) if c * CAP < 16 * L + 16 and c * CAP + CAP > 16 * L]
PIECES = 5


def dot(a, b):
    return lax.dot_general(a, b, (((1,), (0,)), ((), ())), preferred_element_type=f32)


def dot_nt(a, b):
    return lax.dot_general(a, b, (((1,), (1,)), ((), ())), preferred_element_type=f32)


def dot_tn(a, b):
    return lax.dot_general(a, b, (((0,), (0,)), ((), ())), preferred_element_type=f32)


def sigmoid(t):
    return 0.5 * jnp.tanh(0.5 * t) + 0.5


def iota(shape, axis):
    return lax.broadcasted_iota(i32, shape, axis)


def one(cond):
    return jnp.where(cond, 1.0, 0.0).astype(bf16)


def chunk(c):
    return pl.ds(c * 128, 128)


def kernel(
    n_dp, stop,
    tok, cot, pos_ref, seg_ref, w, wo,
    y_out, dx_out, ar_f,
    send_x, recv_x, send_g, recv_g, send_y, recv_y, send_d, recv_d,
    meta_t, rank_s, xp, xhat, rstd_ref, nrm, nrm_t, gbuf,
    msk, slope, uv, qk, kq, qz, p_ref, sl_ref, ds_ref, dq_ref,
    attn_ref, u_ref, dg_ref, st_all, cmb, gated, gfull, dout, du_ref, dpre,
    yd, ar_src, ar_c, ar_h, ar_r, rs_send, rs_own, rs1, rs2,
    a2a_s, a2a_r, ag_s, ag_r, st_s, st_r, gt_s, gt_r, s1_s, s1_r, s2_s, s2_r, s3_s, s3_r, s4_s, s4_r, rs_s, rs_r,
):
    me, cx = lax.axis_index("dp"), lax.axis_index("ctx")
    core, chip = lax.rem(me, 2), lax.div(me, 2)
    other = 1 - core
    n_chip = n_dp // 2
    right, left, opp = lax.rem(cx + 1, 4), lax.rem(cx + 3, 4), lax.rem(cx + 2, 4)
    sends = []

    def rc(src, dst, ss, rs, dev):
        return pltpu.make_async_remote_copy(
            src_ref=src, dst_ref=dst, send_sem=ss, recv_sem=rs, device_id=dev, device_id_type=MESH
        )

    def wait_bytes(ref, ss, rs):
        return rc(ref, ref, ss, rs, {"ctx": right})

    def al(i, m):
        return pl.multiple_of(i * m, m)

    bar = pltpu.get_barrier_semaphore()

    @pl.loop(1, n_dp)
    def _(o):
        pl.semaphore_signal(bar, inc=1, device_id={"dp": lax.rem(me + o, n_dp)}, device_id_type=MESH)

    for o in range(1, 4):
        pl.semaphore_signal(bar, inc=1, device_id={"ctx": lax.rem(cx + o, 4)}, device_id_type=MESH)

    pos_l = jnp.broadcast_to(pos_ref[...], (ROWS, ROWS))
    pos_s = jnp.transpose(pos_l.astype(f32)).astype(i32)
    tgt_l, tgt_s = lax.shift_right_logical(pos_l, 9), lax.shift_right_logical(pos_s, 9)
    ii, jj = iota((ROWS, ROWS), 0), iota((ROWS, ROWS), 1)
    same = tgt_l == tgt_s
    rank_l = jnp.sum(jnp.where(same & (ii < jj), 1.0, 0.0), axis=0, keepdims=True).astype(i32)
    rank_c = jnp.sum(jnp.where(same & (jj < ii), 1.0, 0.0), axis=1, keepdims=True).astype(i32)
    tgt_row = tgt_l[:1] * SLOTS
    rank_s[...] = jnp.where(jj == 0, rank_c, tgt_s * SLOTS)
    row_no = (pos_s & (ROWS - 1)) + 1

    def pack_out(src, dst, with_meta):
        @pl.loop(0, 4)
        def _(rb):
            rows = pl.ds(al(rb, 128), 128)
            here = iota((128, ROWS), 0) + rb * 128
            meta = jnp.zeros((128, 128), f32)
            for L in range(3):
                acc = jnp.zeros((128, 128), f32)
                every = jnp.zeros((128, 128), f32)
                for c in [c for (l, c) in COMBOS if l == L]:
                    v = rank_l + (c * CAP - 16 * L)
                    idx = jnp.where((v >= 0) & (v < 16), tgt_row + v, -1)
                    hit = jnp.where(here == idx, 1.0, 0.0)
                    acc = acc + dot(hit.astype(bf16), src[:, c * 128:c * 128 + 128])
                    every = every + hit
                dst[rows, L * 128:L * 128 + 128] = acc.astype(bf16)
                if with_meta:
                    meta = meta + dot(every.astype(bf16), jnp.where(jj == L, row_no, 0).astype(f32).astype(bf16))
            if with_meta:
                dst[rows, 384:512] = meta.astype(bf16)

    def a2a_start(k, src, dst):
        mine = pl.ds(al(me, SLOTS), SLOTS)
        dst[mine, :] = src[mine, :]

        @pl.loop(1, n_dp)
        def _(o):
            t = lax.rem(me + o, n_dp)
            rc(src.at[pl.ds(al(t, SLOTS), SLOTS)], dst.at[mine], a2a_s.at[k], a2a_r.at[k], {"dp": t}).start()

        part = src.at[pl.ds(0, (n_dp - 1) * SLOTS)]
        sends.append(lambda: wait_bytes(part, a2a_s.at[k], a2a_r.at[k]).wait_send())

    def a2a_wait(k, dst):
        wait_bytes(dst.at[pl.ds(0, (n_dp - 1) * SLOTS)], a2a_s.at[k], a2a_r.at[k]).wait_recv()

    def unpack_arrived(src, dst, rows):
        unit = iota((ROWS, 512), 1) & 15
        for c in range(8):
            acc = jnp.zeros((ROWS, 128), f32)
            for L in [l for (l, d) in COMBOS if d == c]:
                lo = c * CAP - 16 * L
                hit = (meta_t[L:L + 1, :] == (iota((ROWS, 512), 0) + 1).astype(f32)) & (unit >= lo) & (unit < lo + CAP)
                acc = acc + dot(one(hit), src[:, L * 128:L * 128 + 128])
            dst[rows, c * 128:c * 128 + 128] = acc.astype(bf16)

    def pack_back(src, dst):
        @pl.loop(0, 4)
        def _(rb):
            rows = pl.ds(al(rb, 128), 128)
            meta = recv_x[rows, 384:512].astype(f32)
            unit = iota((128, ROWS), 0) & 15
            lane = (iota((128, ROWS), 1) + 1).astype(f32)
            for L in range(3):
                acc = jnp.zeros((128, 128), f32)
                mine = meta[:, L:L + 1] == lane
                for c in [c for (l, c) in COMBOS if l == L]:
                    lo = c * CAP - 16 * L
                    acc = acc + dot(one(mine & (unit >= lo) & (unit < lo + CAP)), src[:, c * 128:c * 128 + 128])
                dst[rows, L * 128:L * 128 + 128] = acc.astype(bf16)

    def unpack_home(src, dst):
        rank, base = rank_s[:, 0:1], rank_s[:, 1:2]
        lanes = iota((ROWS, 512), 1)
        for c in range(8):
            acc = jnp.zeros((ROWS, 128), f32)
            for L in [l for (l, d) in COMBOS if d == c]:
                v = rank + (c * CAP - 16 * L)
                idx = jnp.where((v >= 0) & (v < 16), base + v, -1)
                acc = acc + dot(one(lanes == idx), src[:, L * 128:L * 128 + 128])
            dst[:, c * 128:c * 128 + 128] = acc.astype(bf16)

    def finish():
        for f in sends:
            f()

    pack_out(tok, send_x, True)
    pl.semaphore_wait(bar, n_dp - 1 + 3)
    a2a_start(0, send_x, recv_x)
    pack_out(cot, send_g, False)
    a2a_start(1, send_g, recv_g)

    seg_row = seg_ref[...]
    seg_col = jnp.transpose(jnp.broadcast_to(seg_row.astype(f32), (128, GROUP))).astype(i32)
    for b in range(4):
        sc = seg_col[b * 128:b * 128 + 128, 0:1]
        ok = (sc == seg_row) & (iota((128, GROUP), 1) <= iota((128, GROUP), 0) + b * 128)
        msk[b * 128:b * 128 + 128, :] = jnp.where(ok, 1.0, 0.0)
    cmb[...] = jnp.zeros_like(cmb)

    own = pl.ds(al(cx, 128), 128)
    a2a_wait(0, recv_x)
    meta_t[...] = jnp.transpose(recv_x[:, 384:512].astype(f32))[:8]
    unpack_arrived(recv_x, xp, pl.ds(0, 128))
    xf = xp[...].astype(f32)
    mean = jnp.mean(xf, axis=1, keepdims=True)
    rstd = lax.rsqrt(jnp.mean((xf - mean) ** 2, axis=1, keepdims=True) + EPS)
    xh = (xf - mean) * rstd
    xhat[...] = xh
    rstd_ref[...] = jnp.broadcast_to(rstd, (ROWS, 128))
    nrm[own, :] = xh.astype(bf16)

    def half(b, k):
        return pl.ds(pl.multiple_of(b * 128 + k * 64, 64), 64)

    def ag(k, buf):
        def to(block, h, way, slot):
            ref = buf.at[half(block, h)]
            return rc(ref, ref, ag_s.at[k], ag_r.at[k, slot], {"ctx": way})

        def start():
            to(cx, 0, right, 0).start()
            to(cx, 1, left, 1).start()
            to(cx, 1, right, 2).start()
            to(cx, 0, left, 3).start()

        def forward():
            to(left, 0, right, 0).wait_recv()
            to(left, 0, right, 4).start()
            to(right, 1, left, 1).wait_recv()
            to(right, 1, left, 5).start()
            sends.append(lambda: wait_bytes(buf.at[pl.ds(0, 384)], ag_s.at[k], ag_r.at[k, 0]).wait_send())

        def near():
            to(left, 1, right, 2).wait_recv()
            to(right, 0, left, 3).wait_recv()

        def far():
            to(opp, 0, right, 4).wait_recv()
            to(opp, 1, left, 5).wait_recv()

        return start, forward, near, far

    lane_lo = iota((128, 128), 1) < 64

    def project(block):
        rows = pl.ds(al(block, 128), 128)
        nT = jnp.transpose(nrm[rows, :].astype(f32)).astype(bf16)
        nrm_t[block] = nT

        @pl.loop(0, 4)
        def _(h):
            pre = dot(nrm[rows, :], w[h])
            sig = sigmoid(pre)
            act = pre * sig
            slope[h, rows, :] = sig * (1.0 + pre * (1.0 - sig))
            uv[h, rows, :] = act[:, :128].astype(bf16)
            b = act[:, 128:].astype(bf16)
            qk[h, rows, :] = b
            bf = b.astype(f32)
            kq[h, rows, :] = pltpu.roll(bf, 64, 1).astype(bf16)
            qz[h, rows, :] = jnp.where(lane_lo, bf * 0.125, 0.0).astype(bf16)

    n_start, n_forward, n_near, n_far = ag(0, nrm)
    g_start, g_forward, g_near, g_far = ag(1, gbuf)
    n_start()
    a2a_wait(1, recv_g)
    unpack_arrived(recv_g, gbuf, own)
    project(cx)
    n_forward()
    g_start()
    n_near()
    project(left)
    project(right)
    g_forward()
    n_far()
    project(opp)

    for j in range(2):
        for half_j in range(2):
            h = 2 * j + half_j
            for b in range(4):
                r, n = slice(b * 128, b * 128 + 128), (b + 1) * 128
                t = dot_nt(qz[h, r, :], kq[h, :n, :])
                sig = sigmoid(t)
                m = msk[r, :n]
                pw = t * sig
                p = (pw * m).astype(bf16)
                p_ref[h, r, :n] = p
                sl_ref[h, r, :n] = ((sig + pw * (1.0 - sig)) * (m * 0.125)).astype(bf16)
                pv = dot(p, uv[h, :n, :]).astype(bf16).astype(f32)
                u_here = uv[h, r, :].astype(f32)
                if half_j == 0:
                    attn_ref[r, j * 128:j * 128 + 128] = pltpu.roll(pv, 64, 1)
                    u_ref[r, j * 128:j * 128 + 128] = u_here
                else:
                    attn_ref[r, j * 128:j * 128 + 128] = jnp.where(lane_lo, attn_ref[r, j * 128:j * 128 + 128], pv)
                    u_ref[r, j * 128:j * 128 + 128] = jnp.where(
                        lane_lo, u_ref[r, j * 128:j * 128 + 128], pltpu.roll(u_here, 64, 1)
                    )

    g_near()
    g_far()
    wo_mine = pl.ds(al(cx, 256), 256)

    @pl.loop(0, 4)
    def _(b):
        r = pl.ds(al(b, 128), 128)
        dg = dot_nt(gbuf[r, :], wo[wo_mine, :])
        dg_ref[r, :] = dg
        a = attn_ref[r, :]
        m = jnp.mean(a, axis=1, keepdims=True)
        ac = a - m
        e = dg * u_ref[r, :]
        lane = iota((128, 128), 1)
        st = jnp.where(lane == 0, m, jnp.sum(ac * ac, axis=1, keepdims=True))
        st = jnp.where(lane == 2, jnp.sum(e, axis=1, keepdims=True), st)
        st = jnp.where(lane == 3, jnp.sum(e * ac, axis=1, keepdims=True), st)
        st_all[cx, :, pl.ds(al(b, 128), 128)] = jnp.transpose(st)[:8]

    for o in range(1, 4):
        rc(st_all.at[cx], st_all.at[cx], st_s, st_r, {"ctx": lax.rem(cx + o, 4)}).start()
    sends.append(lambda: wait_bytes(st_all.at[pl.ds(0, 3)], st_s, st_r).wait_send())
    wait_bytes(st_all.at[pl.ds(0, 3)], st_s, st_r).wait_recv()
    ms = [st_all[l, 0:1, :] for l in range(4)]
    m2 = (ms[0] + ms[1] + ms[2] + ms[3]) * 0.25
    sq, se, seo = 0.0, 0.0, 0.0
    for l in range(4):
        d = ms[l] - m2
        sq = sq + st_all[l, 1:2, :] + 256.0 * d * d
        se = se + st_all[l, 2:3, :]
        seo = seo + st_all[l, 3:4, :] + d * st_all[l, 2:3, :]
    r2 = lax.rsqrt(sq * (1.0 / WIDTH) + EPS)
    cmb[0:1, :] = m2
    cmb[1:2, :] = r2
    cmb[2:3, :] = se * (1.0 / WIDTH)
    cmb[3:4, :] = r2 * seo * (1.0 / WIDTH)

    for b in range(4):
        r = slice(b * 128, b * 128 + 128)
        tr = jnp.transpose(cmb[:, r])
        r2c = tr[:, 1:2]
        onorm = (attn_ref[r, :] - tr[:, 0:1]) * r2c
        u, dg = u_ref[r, :], dg_ref[r, :]
        gated[r, :] = (onorm * u).astype(bf16)
        du = (dg * onorm).astype(bf16).astype(f32)
        da = r2c * (dg * u - tr[:, 2:3] - onorm * tr[:, 3:4])
        for j in range(2):
            s = slice(j * 128, j * 128 + 128)
            dout[2 * j, r, :] = jnp.where(lane_lo, 0.0, pltpu.roll(da[:, s], 64, 1)).astype(bf16)
            dout[2 * j + 1, r, :] = jnp.where(lane_lo, 0.0, da[:, s]).astype(bf16)
            du_ref[2 * j, r, :] = du[:, s]
            du_ref[2 * j + 1, r, :] = pltpu.roll(du[:, s], 64, 1)

    for o in (2, 1, 3):
        t = lax.rem(cx + o, 4)
        rc(gated.at[pl.ds(al(t, 128), 128)], gfull.at[own], gt_s, gt_r, {"ctx": t}).start()
    sends.append(lambda: wait_bytes(gated.at[pl.ds(0, 384)], gt_s, gt_r).wait_send())
    gfull[own, :] = gated[own, :]

    half_rows = 512
    unit_rows = half_rows // n_chip

    def ar1(p):
        c = rc(ar_src.at[p, pl.ds(al(other, half_rows), half_rows)], ar_c.at[p], s1_s.at[p], s1_r.at[p], {"dp": chip * 2 + other})
        c.start()
        sends.append(c.wait_send)

    def ar2(p):
        wait_bytes(ar_c.at[p], s1_s.at[p], s1_r.at[p]).wait_recv()
        mine = pl.ds(al(chip, unit_rows), unit_rows)

        @pl.loop(0, 4)
        def _(b):
            r = pl.ds(al(b, 128), 128)
            a = ar_src[p, pl.ds(pl.multiple_of(core * half_rows + b * 128, 128), 128), :].astype(f32)
            ar_h[p, r, :] = (a + ar_c[p, r, :].astype(f32)).astype(bf16)

        ar_r[p, mine, :] = ar_h[p, mine, :]

        @pl.loop(1, n_chip)
        def _(o):
            t = lax.rem(chip + o, n_chip)
            rc(ar_h.at[p, pl.ds(al(t, unit_rows), unit_rows)], ar_r.at[p, mine], s2_s.at[p], s2_r.at[p], {"dp": t * 2 + core}).start()

        sends.append(lambda: wait_bytes(ar_h.at[p, pl.ds(0, unit_rows * (n_chip - 1))], s2_s.at[p], s2_r.at[p]).wait_send())

    def ar3(p):
        part = ar_r.at[p, pl.ds(0, unit_rows * (n_chip - 1))]
        wait_bytes(part, s2_s.at[p], s2_r.at[p]).wait_recv()
        acc = jnp.zeros((unit_rows, 256), f32)
        for k in range(n_chip):
            acc = acc + ar_r[p, k * unit_rows:(k + 1) * unit_rows, :].astype(f32)
        mine = pl.ds(pl.multiple_of(core * half_rows + chip * unit_rows, unit_rows), unit_rows)
        ar_f[p, mine, :] = acc.astype(bf16)
        ref = ar_f.at[p, mine]

        @pl.loop(1, n_chip)
        def _(o):
            rc(ref, ref, s3_s.at[p], s3_r.at[p], {"dp": lax.rem(chip + o, n_chip) * 2 + core}).start()

        sends.append(lambda: wait_bytes(part, s3_s.at[p], s3_r.at[p]).wait_send())

    def ar4(p):
        wait_bytes(ar_f.at[p, pl.ds(0, unit_rows * (n_chip - 1))], s3_s.at[p], s3_r.at[p]).wait_recv()
        ref = ar_f.at[p, pl.ds(al(core, half_rows), half_rows)]
        c = rc(ref, ref, s4_s.at[p], s4_r.at[p], {"dp": chip * 2 + other})
        c.start()
        sends.append(c.wait_send)

    def ar5(p):
        ref = ar_f.at[p, pl.ds(al(other, half_rows), half_rows)]
        wait_bytes(ref, s4_s.at[p], s4_r.at[p]).wait_recv()

    for cb in range(4):
        ar_src[0, cb * 256:cb * 256 + 256, :] = dot_tn(gated[...], gbuf[:, cb * 256:cb * 256 + 256]).astype(bf16)
    ar1(0)

    wait_bytes(gfull.at[pl.ds(0, 384)], gt_s, gt_r).wait_recv()
    for cb in range(4):
        s = slice(cb * 256, cb * 256 + 256)
        acc = xp[:, s].astype(f32)
        for c in range(4):
            acc = acc + dot(gfull[c * 128:c * 128 + 128, :], wo[c * 256:c * 256 + 256, s])
        yd[:, s] = acc.astype(bf16)
    pack_back(yd, send_y)
    a2a_start(2, send_y, recv_y)

    def backward(h):
        for b in range(4):
            r, n = slice(b * 128, b * 128 + 128), (b + 1) * 128
            dw = dot_nt(dout[h, r, :], uv[h, :n, :])
            ds = (dw * sl_ref[h, r, :n].astype(f32)).astype(bf16)
            ds_ref[r, :n] = ds
            dq_ref[r, :] = dot(ds, qk[h, :n, :])
        for b in range(4):
            r, c = slice(b * 128, b * 128 + 128), slice(b * 128, 512)
            dv = dot_tn(p_ref[h, c, r], dout[h, c, :])
            dk = dot_tn(ds_ref[c, r], qk[h, c, :])
            d1 = jnp.where(lane_lo, du_ref[h, r, :], dv)
            d2 = pltpu.roll(jnp.where(lane_lo, dk, dq_ref[r, :]), 64, 1)
            dpre[h, r, 0:128] = (d1 * slope[h, r, 0:128]).astype(bf16)
            dpre[h, r, 128:256] = (d2 * slope[h, r, 128:256]).astype(bf16)

    def piece(h):
        @pl.loop(0, 4)
        def _(q):
            acc = jnp.zeros((256, 256), f32)
            for b in range(4):
                acc = acc + dot(nrm_t[b, pl.ds(al(q, 256), 256), :], dpre[h, b * 128:b * 128 + 128, :])
            ar_src[h + 1, pl.ds(al(q, 256), 256), :] = acc.astype(bf16)

        ar1(h + 1)

    backward(0)
    piece(0)
    ar2(0)
    backward(1)
    piece(1)
    ar2(1)
    ar3(0)
    backward(2)
    piece(2)
    ar2(2)
    ar3(1)
    ar4(0)
    backward(3)

    def dnorm(block, dst):
        rows = pl.ds(al(block, 128), 128)

        @pl.loop(0, 4)
        def _(cb):
            acc = jnp.zeros((128, 256), f32)
            for h in range(4):
                acc = acc + dot_nt(dpre[h, rows, :], w[h, pl.ds(al(cb, 256), 256), :])
            dst[:, pl.ds(al(cb, 256), 256)] = acc.astype(dst.dtype)

    lo, hi = pl.ds(0, 64), pl.ds(64, 64)

    def rs_go(src, dst, k, way):
        c = rc(src, dst, rs_s.at[k], rs_r.at[k], {"ctx": way})
        c.start()
        sends.append(c.wait_send)

    def rs_wait(dst, k):
        wait_bytes(dst, rs_s.at[k], rs_r.at[k]).wait_recv()

    to_far, to_right, to_left = rs_send.at[0], rs_send.at[1], rs_send.at[2]
    dnorm(opp, to_far)
    rs_go(to_far.at[lo], rs1.at[0], 0, right)
    rs_go(to_far.at[hi], rs1.at[1], 1, left)
    dnorm(right, to_right)
    rs_go(to_right.at[hi], rs2.at[0, hi], 2, right)
    dnorm(left, to_left)
    rs_go(to_left.at[lo], rs2.at[1, lo], 3, left)
    piece(3)
    dnorm(cx, rs_own)
    rs_wait(rs1.at[0], 0)
    to_right[lo, :] = (to_right[lo, :].astype(f32) + rs1[0].astype(f32)).astype(bf16)
    rs_go(to_right.at[lo], rs2.at[0, lo], 4, right)
    rs_wait(rs1.at[1], 1)
    to_left[hi, :] = (to_left[hi, :].astype(f32) + rs1[1].astype(f32)).astype(bf16)
    rs_go(to_left.at[hi], rs2.at[1, hi], 5, left)
    ar2(3)
    ar3(2)
    ar4(1)
    ar2(4)
    ar3(3)
    ar4(2)
    a2a_wait(2, recv_y)
    unpack_home(recv_y, y_out)
    rs_wait(rs2.at[0, hi], 2)
    rs_wait(rs2.at[1, lo], 3)
    rs_wait(rs2.at[0, lo], 4)
    rs_wait(rs2.at[1, hi], 5)
    dn = rs_own[...] + rs2[0].astype(f32) + rs2[1].astype(f32)
    xh2 = xhat[...]
    mean_d = jnp.mean(dn, axis=1, keepdims=True)
    mean_dx = jnp.mean(dn * xh2, axis=1, keepdims=True)
    dx = gbuf[own, :].astype(f32) + rstd_ref[:, 0:1] * (dn - mean_d - xh2 * mean_dx)
    yd[...] = dx.astype(bf16)
    pack_back(yd, send_d)
    a2a_start(3, send_d, recv_d)
    ar3(4)
    ar4(3)
    ar4(4)
    a2a_wait(3, recv_d)
    unpack_home(recv_d, dx_out)
    for p in range(PIECES):
        ar5(p)
    finish()


def shards(stop, tokens, cotangent, packed_pos, segment_ids, w_proj, w_out):
    n_dp = lax.axis_size("dp")
    vmem, sem = pltpu.VMEM, pltpu.SemaphoreType.DMA
    scratch = [
        vmem((512, 512), bf16), vmem((512, 512), bf16),
        vmem((512, 384), bf16), vmem((512, 384), bf16),
        vmem((512, 384), bf16), vmem((512, 384), bf16),
        vmem((512, 384), bf16), vmem((512, 384), bf16),
        vmem((8, 512), f32), vmem((128, 128), i32),
        vmem((128, 1024), bf16), vmem((128, 1024), f32), vmem((128, 128), f32),
        vmem((512, 1024), bf16), vmem((4, 1024, 128), bf16), vmem((512, 1024), bf16),
        vmem((512, 512), f32), vmem((4, 512, 256), f32),
        vmem((4, 512, 128), bf16), vmem((4, 512, 128), bf16),
        vmem((4, 512, 128), bf16), vmem((4, 512, 128), bf16),
        vmem((4, 512, 512), bf16), vmem((4, 512, 512), bf16),
        vmem((512, 512), bf16), vmem((512, 128), f32),
        vmem((512, 256), f32), vmem((512, 256), f32), vmem((512, 256), f32),
        vmem((4, 8, 512), f32), vmem((128, 512), f32),
        vmem((512, 256), bf16), vmem((512, 256), bf16),
        vmem((4, 512, 128), bf16), vmem((4, 512, 128), f32), vmem((4, 512, 256), bf16),
        vmem((128, 1024), bf16),
        vmem((PIECES, 1024, 256), bf16), vmem((PIECES, 512, 256), bf16),
        vmem((PIECES, 512, 256), bf16), vmem((PIECES, 512, 256), bf16),
        vmem((3, 128, 1024), bf16), vmem((128, 1024), f32),
        vmem((2, 64, 1024), bf16), vmem((2, 128, 1024), bf16),
        sem((4,)), sem((4,)), sem((2,)), sem((2, 6)), sem, sem, sem, sem,
        sem((PIECES,)), sem((PIECES,)), sem((PIECES,)), sem((PIECES,)),
        sem((PIECES,)), sem((PIECES,)), sem((PIECES,)), sem((PIECES,)), sem((6,)), sem((6,)),
    ]
    spec = pl.BlockSpec(memory_space=pltpu.VMEM)
    y, dx, ar = pl.pallas_call(
        functools.partial(kernel, n_dp, stop),
        out_shape=[
            jax.ShapeDtypeStruct((ROWS, WIDTH), bf16),
            jax.ShapeDtypeStruct((ROWS, WIDTH), bf16),
            jax.ShapeDtypeStruct((PIECES, 1024, 256), bf16),
        ],
        in_specs=[spec] * 6,
        out_specs=[spec] * 3,
        scratch_shapes=scratch,
        compiler_params=pltpu.CompilerParams(
            collective_id=0, has_side_effects=True, vmem_limit_bytes=60 * 1024 * 1024
        ),
        cost_estimate=pl.CostEstimate(flops=6 * 10**9, bytes_accessed=12 * 10**6, transcendentals=3 * 10**6),
    )(
        tokens,
        cotangent,
        packed_pos.reshape(1, ROWS),
        segment_ids,
        jnp.transpose(w_proj, (1, 0, 2)),
        w_out,
    )
    scale = (ROWS * 4 * n_dp) ** (-0.5)
    proj = jnp.transpose(ar[1:], (1, 0, 2)).astype(f32) * scale
    out = jnp.transpose(ar[0].reshape(4, 256, 256), (1, 0, 2)).reshape(256, WIDTH).astype(f32) * scale
    return y, dx, proj, out


def solution(mesh, stop=99):
    return jax.shard_map(
        functools.partial(shards, stop),
        mesh=mesh,
        in_specs=(
            P(("dp", "ctx"), None),
            P(("dp", "ctx"), None),
            P(("dp", "ctx")),
            P("dp", None),
            P(None, "ctx", None),
            P(),
        ),
        out_specs=(
            P(("dp", "ctx"), None),
            P(("dp", "ctx"), None),
            P(None, "ctx", None),
            P("ctx", None),
        ),
        check_vma=False,
    )
```

```python
import functools
import jax
import jax.numpy as jnp
from jax import lax
from jax.experimental import pallas as pl
from jax.experimental.pallas import tpu as pltpu
from jax.sharding import PartitionSpec as P

EPS = 1e-05
MESH = pl.DeviceIdType.MESH
bf16, f32, i32 = jnp.bfloat16, jnp.float32, jnp.int32
ROWS, WIDTH, GROUP, SLOTS = 128, 1024, 512, 16
CAP = 6
COMBOS = [(L, c) for L in range(3) for c in range(8) if c * CAP < 16 * L + 16 and c * CAP + CAP > 16 * L]
PIECES = 5


def dot(a, b):
    return lax.dot_general(a, b, (((1,), (0,)), ((), ())), preferred_element_type=f32)


def dot_nt(a, b):
    return lax.dot_general(a, b, (((1,), (1,)), ((), ())), preferred_element_type=f32)


def dot_tn(a, b):
    return lax.dot_general(a, b, (((0,), (0,)), ((), ())), preferred_element_type=f32)


def sigmoid(t):
    return 0.5 * jnp.tanh(0.5 * t) + 0.5


def iota(shape, axis):
    return lax.broadcasted_iota(i32, shape, axis)


def one(cond):
    return jnp.where(cond, 1.0, 0.0).astype(bf16)


def chunk(c):
    return pl.ds(c * 128, 128)


def kernel(
    n_dp,
    tok_h, cot_h, pos_ref, seg_ref, w_h, wo_h,
    y_out, recv_d, ar_f,
    tok, cot, w, wo, in_s,
    send_x, recv_x, send_g, recv_g, send_y, recv_y, send_d,
    meta_t, rank_s, xp, xhat, rstd_ref, nrm, nrm_t, gbuf,
    msk, slope, uv, qk, kq, qz, p_ref, sl_ref, ds_ref, dq_ref,
    attn_ref, u_ref, dg_ref, st_all, cmb, gated, gfull, dout, du_ref, dpre, dg_send,
    yd, ar_src, ar_c, ar_h, ar_r, rs_send, rs_own, rs1, rs2,
    a2a_s, a2a_r, ag_s, ag_r, st_s, st_r, gt_s, gt_r, dg_s, dg_r, s1_s, s1_r, s2_s, s2_r, s3_s, s3_r, s4_s, s4_r, rs_s, rs_r,
):
    me, cx = lax.axis_index("dp"), lax.axis_index("ctx")
    core, chip = lax.rem(me, 2), lax.div(me, 2)
    other = 1 - core
    n_chip = n_dp // 2
    right, left, opp = lax.rem(cx + 1, 4), lax.rem(cx + 3, 4), lax.rem(cx + 2, 4)
    sends, flight = [], {}

    def rc(src, dst, ss, rs, dev):
        return pltpu.make_async_remote_copy(
            src_ref=src, dst_ref=dst, send_sem=ss, recv_sem=rs, device_id=dev, device_id_type=MESH
        )

    def wait_bytes(ref, ss, rs):
        return rc(ref, ref, ss, rs, {"ctx": right})

    def arrive(*keys):
        for key in keys:
            flight.pop(key)()

    def al(i, m):
        return pl.multiple_of(i * m, m)

    loads = [pltpu.make_async_copy(a, b, in_s.at[i]) for i, (a, b) in enumerate([(tok_h, tok), (cot_h, cot), (w_h, w), (wo_h, wo)])]
    for c in loads:
        c.start()

    bar = pltpu.get_barrier_semaphore()

    @pl.loop(1, n_dp)
    def _(o):
        pl.semaphore_signal(bar, inc=1, device_id={"dp": lax.rem(me + o, n_dp)}, device_id_type=MESH)

    for o in range(1, 4):
        pl.semaphore_signal(bar, inc=1, device_id={"ctx": lax.rem(cx + o, 4)}, device_id_type=MESH)

    pos_l = jnp.broadcast_to(pos_ref[...], (ROWS, ROWS))
    pos_s = jnp.transpose(pos_l.astype(f32)).astype(i32)
    tgt_l, tgt_s = lax.shift_right_logical(pos_l, 9), lax.shift_right_logical(pos_s, 9)
    ii, jj = iota((ROWS, ROWS), 0), iota((ROWS, ROWS), 1)
    same = tgt_l == tgt_s
    rank_l = jnp.sum(jnp.where(same & (ii < jj), 1.0, 0.0), axis=0, keepdims=True).astype(i32)
    rank_c = jnp.sum(jnp.where(same & (jj < ii), 1.0, 0.0), axis=1, keepdims=True).astype(i32)
    tgt_row = tgt_l[:1] * SLOTS
    rank_s[...] = jnp.where(jj == 0, rank_c, tgt_s * SLOTS)
    row_no = (pos_s & (ROWS - 1)) + 1

    def pack_out(src, dst, with_meta):
        @pl.loop(0, 4)
        def _(rb):
            rows = pl.ds(al(rb, 128), 128)
            here = iota((128, ROWS), 0) + rb * 128
            meta = jnp.zeros((128, 128), f32)
            for L in range(3):
                acc = jnp.zeros((128, 128), f32)
                every = jnp.zeros((128, 128), f32)
                for c in [c for (l, c) in COMBOS if l == L]:
                    v = rank_l + (c * CAP - 16 * L)
                    idx = jnp.where((v >= 0) & (v < 16), tgt_row + v, -1)
                    hit = jnp.where(here == idx, 1.0, 0.0)
                    acc = acc + dot(hit.astype(bf16), src[:, c * 128:c * 128 + 128])
                    every = every + hit
                dst[rows, L * 128:L * 128 + 128] = acc.astype(bf16)
                if with_meta:
                    meta = meta + dot(every.astype(bf16), jnp.where(jj == L, row_no, 0).astype(f32).astype(bf16))
            if with_meta:
                dst[rows, 384:512] = meta.astype(bf16)

    def a2a_start(k, src, dst):
        mine = pl.ds(al(me, SLOTS), SLOTS)
        dst[mine, :] = src[mine, :]

        @pl.loop(1, n_dp)
        def _(o):
            t = lax.rem(me + o, n_dp)
            rc(src.at[pl.ds(al(t, SLOTS), SLOTS)], dst.at[mine], a2a_s.at[k], a2a_r.at[k], {"dp": t}).start()

        part = src.at[pl.ds(0, (n_dp - 1) * SLOTS)]
        sends.append(lambda: wait_bytes(part, a2a_s.at[k], a2a_r.at[k]).wait_send())
        come = dst.at[pl.ds(0, (n_dp - 1) * SLOTS)]
        flight["a2a", k] = lambda: wait_bytes(come, a2a_s.at[k], a2a_r.at[k]).wait_recv()

    def unpack_arrived(src, dst, rows):
        unit = iota((ROWS, 512), 1) & 15
        for c in range(8):
            acc = jnp.zeros((ROWS, 128), f32)
            for L in [l for (l, d) in COMBOS if d == c]:
                lo = c * CAP - 16 * L
                hit = (meta_t[L:L + 1, :] == (iota((ROWS, 512), 0) + 1).astype(f32)) & (unit >= lo) & (unit < lo + CAP)
                acc = acc + dot(one(hit), src[:, L * 128:L * 128 + 128])
            dst[rows, c * 128:c * 128 + 128] = acc.astype(bf16)

    def pack_back(src, dst):
        @pl.loop(0, 4)
        def _(rb):
            rows = pl.ds(al(rb, 128), 128)
            meta = recv_x[rows, 384:512].astype(f32)
            unit = iota((128, ROWS), 0) & 15
            lane = (iota((128, ROWS), 1) + 1).astype(f32)
            for L in range(3):
                acc = jnp.zeros((128, 128), f32)
                mine = meta[:, L:L + 1] == lane
                for c in [c for (l, c) in COMBOS if l == L]:
                    lo = c * CAP - 16 * L
                    acc = acc + dot(one(mine & (unit >= lo) & (unit < lo + CAP)), src[:, c * 128:c * 128 + 128])
                dst[rows, L * 128:L * 128 + 128] = acc.astype(bf16)

    def unpack_home(src, dst):
        rank, base = rank_s[:, 0:1], rank_s[:, 1:2]
        lanes = iota((ROWS, 512), 1)
        for c in range(8):
            acc = jnp.zeros((ROWS, 128), f32)
            for L in [l for (l, d) in COMBOS if d == c]:
                v = rank + (c * CAP - 16 * L)
                idx = jnp.where((v >= 0) & (v < 16), base + v, -1)
                acc = acc + dot(one(lanes == idx), src[:, L * 128:L * 128 + 128])
            dst[:, c * 128:c * 128 + 128] = acc.astype(bf16)

    def finish():
        for f in sends:
            f()

    loads[0].wait()
    pack_out(tok, send_x, True)
    pl.semaphore_wait(bar, n_dp - 1 + 3)
    a2a_start(0, send_x, recv_x)
    loads[1].wait()
    pack_out(cot, send_g, False)
    a2a_start(1, send_g, recv_g)

    seg_row = seg_ref[...]
    seg_col = jnp.transpose(jnp.broadcast_to(seg_row.astype(f32), (128, GROUP))).astype(i32)
    for b in range(4):
        sc = seg_col[b * 128:b * 128 + 128, 0:1]
        ok = (sc == seg_row) & (iota((128, GROUP), 1) <= iota((128, GROUP), 0) + b * 128)
        msk[b * 128:b * 128 + 128, :] = jnp.where(ok, 1.0, 0.0)
    cmb[...] = jnp.zeros_like(cmb)

    own = pl.ds(al(cx, 128), 128)
    loads[2].wait()
    loads[3].wait()
    arrive(("a2a", 0))
    meta_t[...] = jnp.transpose(recv_x[:, 384:512].astype(f32))[:8]
    unpack_arrived(recv_x, xp, pl.ds(0, 128))
    xf = xp[...].astype(f32)
    mean = jnp.mean(xf, axis=1, keepdims=True)
    rstd = lax.rsqrt(jnp.mean((xf - mean) ** 2, axis=1, keepdims=True) + EPS)
    xh = (xf - mean) * rstd
    xhat[...] = xh
    rstd_ref[...] = jnp.broadcast_to(rstd, (ROWS, 128))
    nrm[own, :] = xh.astype(bf16)

    def half(b, k):
        return pl.ds(pl.multiple_of(b * 128 + k * 64, 64), 64)

    def ag(k, buf):
        def to(block, h, way, slot):
            ref = buf.at[half(block, h)]
            return rc(ref, ref, ag_s.at[k], ag_r.at[k, slot], {"ctx": way})

        def go(block, h, way, slot, source):
            to(block, h, way, slot).start()
            sends.append(to(block, h, way, slot).wait_send)
            flight["ag", k, slot] = to(source, h, way, slot).wait_recv

        def start():
            go(cx, 0, right, 0, left)
            go(cx, 1, left, 1, right)
            go(cx, 1, right, 2, left)
            go(cx, 0, left, 3, right)

        def forward():
            arrive(("ag", k, 0))
            go(left, 0, right, 4, opp)
            arrive(("ag", k, 1))
            go(right, 1, left, 5, opp)

        def near():
            arrive(("ag", k, 2), ("ag", k, 3))

        def far():
            arrive(("ag", k, 4), ("ag", k, 5))

        return start, forward, near, far

    lane_lo = iota((128, 128), 1) < 64

    def project(block):
        rows = pl.ds(al(block, 128), 128)
        nT = jnp.transpose(nrm[rows, :].astype(f32)).astype(bf16)
        nrm_t[block] = nT

        @pl.loop(0, 4)
        def _(h):
            pre = dot(nrm[rows, :], w[h])
            sig = sigmoid(pre)
            act = pre * sig
            slope[h, rows, :] = sig * (1.0 + pre * (1.0 - sig))
            uv[h, rows, :] = act[:, :128].astype(bf16)
            b = act[:, 128:].astype(bf16)
            qk[h, rows, :] = b
            bf = b.astype(f32)
            kq[h, rows, :] = pltpu.roll(bf, 64, 1).astype(bf16)
            qz[h, rows, :] = jnp.where(lane_lo, bf * 0.125, 0.0).astype(bf16)

    n_start, n_forward, n_near, n_far = ag(0, nrm)
    g_start, g_forward, g_near, g_far = ag(1, gbuf)
    n_start()
    arrive(("a2a", 1))
    unpack_arrived(recv_g, gbuf, own)
    n_forward()
    for t in range(4):
        dg_send[t] = dot_nt(gbuf[own, :], wo[t * 256:t * 256 + 256, :]).astype(bf16)
    for o in (2, 1, 3):
        t = lax.rem(cx + o, 4)
        rc(dg_send.at[t], dg_ref.at[own], dg_s, dg_r, {"ctx": t}).start()
    sends.append(lambda: wait_bytes(dg_ref.at[pl.ds(0, 384)], dg_s, dg_r).wait_send())
    flight["dg"] = lambda: wait_bytes(dg_ref.at[pl.ds(0, 384)], dg_s, dg_r).wait_recv()
    dg_ref[own, :] = dg_send[cx]
    project(cx)
    n_near()
    project(left)
    project(right)
    n_far()
    g_start()
    project(opp)

    for j in range(2):
        for half_j in range(2):
            h = 2 * j + half_j
            for b in range(4):
                r, n = slice(b * 128, b * 128 + 128), (b + 1) * 128
                t = dot_nt(qz[h, r, :], kq[h, :n, :])
                sig = sigmoid(t)
                m = msk[r, :n]
                pw = t * sig
                p = (pw * m).astype(bf16)
                p_ref[h, r, :n] = p
                sl_ref[h, r, :n] = ((sig + pw * (1.0 - sig)) * (m * 0.125)).astype(bf16)
                pv = dot(p, uv[h, :n, :]).astype(bf16).astype(f32)
                u_here = uv[h, r, :].astype(f32)
                if half_j == 0:
                    attn_ref[r, j * 128:j * 128 + 128] = pltpu.roll(pv, 64, 1)
                    u_ref[r, j * 128:j * 128 + 128] = u_here
                else:
                    attn_ref[r, j * 128:j * 128 + 128] = jnp.where(lane_lo, attn_ref[r, j * 128:j * 128 + 128], pv)
                    u_ref[r, j * 128:j * 128 + 128] = jnp.where(
                        lane_lo, u_ref[r, j * 128:j * 128 + 128], pltpu.roll(u_here, 64, 1)
                    )

    g_forward()
    arrive("dg")

    @pl.loop(0, 4)
    def _(b):
        r = pl.ds(al(b, 128), 128)
        dg = dg_ref[r, :].astype(f32)
        a = attn_ref[r, :]
        m = jnp.mean(a, axis=1, keepdims=True)
        ac = a - m
        e = dg * u_ref[r, :]
        lane = iota((128, 128), 1)
        st = jnp.where(lane == 0, m, jnp.sum(ac * ac, axis=1, keepdims=True))
        st = jnp.where(lane == 2, jnp.sum(e, axis=1, keepdims=True), st)
        st = jnp.where(lane == 3, jnp.sum(e * ac, axis=1, keepdims=True), st)
        st_all[cx, :, pl.ds(al(b, 128), 128)] = jnp.transpose(st)[:8]

    for o in range(1, 4):
        rc(st_all.at[cx], st_all.at[cx], st_s, st_r, {"ctx": lax.rem(cx + o, 4)}).start()
    sends.append(lambda: wait_bytes(st_all.at[pl.ds(0, 3)], st_s, st_r).wait_send())
    flight["st"] = lambda: wait_bytes(st_all.at[pl.ds(0, 3)], st_s, st_r).wait_recv()
    arrive("st")
    ms = [st_all[l, 0:1, :] for l in range(4)]
    m2 = (ms[0] + ms[1] + ms[2] + ms[3]) * 0.25
    sq, se, seo = 0.0, 0.0, 0.0
    for l in range(4):
        d = ms[l] - m2
        sq = sq + st_all[l, 1:2, :] + 256.0 * d * d
        se = se + st_all[l, 2:3, :]
        seo = seo + st_all[l, 3:4, :] + d * st_all[l, 2:3, :]
    r2 = lax.rsqrt(sq * (1.0 / WIDTH) + EPS)
    cmb[0:1, :] = m2
    cmb[1:2, :] = r2
    cmb[2:3, :] = se * (1.0 / WIDTH)
    cmb[3:4, :] = r2 * seo * (1.0 / WIDTH)

    for b in range(4):
        r = slice(b * 128, b * 128 + 128)
        tr = jnp.transpose(cmb[:, r])
        r2c = tr[:, 1:2]
        onorm = (attn_ref[r, :] - tr[:, 0:1]) * r2c
        u, dg = u_ref[r, :], dg_ref[r, :].astype(f32)
        gated[r, :] = (onorm * u).astype(bf16)
        du = (dg * onorm).astype(bf16).astype(f32)
        da = r2c * (dg * u - tr[:, 2:3] - onorm * tr[:, 3:4])
        for j in range(2):
            s = slice(j * 128, j * 128 + 128)
            dout[2 * j, r, :] = jnp.where(lane_lo, 0.0, pltpu.roll(da[:, s], 64, 1)).astype(bf16)
            dout[2 * j + 1, r, :] = jnp.where(lane_lo, 0.0, da[:, s]).astype(bf16)
            du_ref[2 * j, r, :] = du[:, s]
            du_ref[2 * j + 1, r, :] = pltpu.roll(du[:, s], 64, 1)

    for o in (2, 1, 3):
        t = lax.rem(cx + o, 4)
        rc(gated.at[pl.ds(al(t, 128), 128)], gfull.at[own], gt_s, gt_r, {"ctx": t}).start()
    sends.append(lambda: wait_bytes(gated.at[pl.ds(0, 384)], gt_s, gt_r).wait_send())
    flight["gt"] = lambda: wait_bytes(gfull.at[pl.ds(0, 384)], gt_s, gt_r).wait_recv()
    gfull[own, :] = gated[own, :]

    half_rows = 512
    unit_rows = half_rows // n_chip

    def ar1(p):
        c = rc(ar_src.at[p, pl.ds(al(other, half_rows), half_rows)], ar_c.at[p], s1_s.at[p], s1_r.at[p], {"dp": chip * 2 + other})
        c.start()
        sends.append(c.wait_send)
        flight["s1", p] = lambda: wait_bytes(ar_c.at[p], s1_s.at[p], s1_r.at[p]).wait_recv()

    def ar2(p):
        arrive(("s1", p))
        mine = pl.ds(al(chip, unit_rows), unit_rows)

        @pl.loop(0, 4)
        def _(b):
            r = pl.ds(al(b, 128), 128)
            a = ar_src[p, pl.ds(pl.multiple_of(core * half_rows + b * 128, 128), 128), :].astype(f32)
            ar_h[p, r, :] = (a + ar_c[p, r, :].astype(f32)).astype(bf16)

        ar_r[p, mine, :] = ar_h[p, mine, :]

        @pl.loop(1, n_chip)
        def _(o):
            t = lax.rem(chip + o, n_chip)
            rc(ar_h.at[p, pl.ds(al(t, unit_rows), unit_rows)], ar_r.at[p, mine], s2_s.at[p], s2_r.at[p], {"dp": t * 2 + core}).start()

        sends.append(lambda: wait_bytes(ar_h.at[p, pl.ds(0, unit_rows * (n_chip - 1))], s2_s.at[p], s2_r.at[p]).wait_send())
        part = ar_r.at[p, pl.ds(0, unit_rows * (n_chip - 1))]
        flight["s2", p] = lambda: wait_bytes(part, s2_s.at[p], s2_r.at[p]).wait_recv()

    def ar3(p):
        arrive(("s2", p))
        acc = jnp.zeros((unit_rows, 256), f32)
        for k in range(n_chip):
            acc = acc + ar_r[p, k * unit_rows:(k + 1) * unit_rows, :].astype(f32)
        mine = pl.ds(pl.multiple_of(core * half_rows + chip * unit_rows, unit_rows), unit_rows)
        ar_f[p, mine, :] = acc.astype(bf16)
        ref = ar_f.at[p, mine]

        @pl.loop(1, n_chip)
        def _(o):
            rc(ref, ref, s3_s.at[p], s3_r.at[p], {"dp": lax.rem(chip + o, n_chip) * 2 + core}).start()

        part = ar_f.at[p, pl.ds(0, unit_rows * (n_chip - 1))]
        sends.append(lambda: wait_bytes(part, s3_s.at[p], s3_r.at[p]).wait_send())
        flight["s3", p] = lambda: wait_bytes(part, s3_s.at[p], s3_r.at[p]).wait_recv()

    def ar4(p):
        arrive(("s3", p))
        ref = ar_f.at[p, pl.ds(al(core, half_rows), half_rows)]
        c = rc(ref, ref, s4_s.at[p], s4_r.at[p], {"dp": chip * 2 + other})
        c.start()
        sends.append(c.wait_send)
        flight["s4", p] = lambda: wait_bytes(ref, s4_s.at[p], s4_r.at[p]).wait_recv()

    def ar5(p):
        arrive(("s4", p))

    def backward(h):
        for b in range(4):
            r, n = slice(b * 128, b * 128 + 128), (b + 1) * 128
            dw = dot_nt(dout[h, r, :], uv[h, :n, :])
            ds = (dw * sl_ref[h, r, :n].astype(f32)).astype(bf16)
            ds_ref[r, :n] = ds
            dq_ref[r, :] = dot(ds, qk[h, :n, :])
        for b in range(4):
            r, c = slice(b * 128, b * 128 + 128), slice(b * 128, 512)
            dv = dot_tn(p_ref[h, c, r], dout[h, c, :])
            dk = dot_tn(ds_ref[c, r], qk[h, c, :])
            d1 = jnp.where(lane_lo, du_ref[h, r, :], dv)
            d2 = pltpu.roll(jnp.where(lane_lo, dk, dq_ref[r, :]), 64, 1)
            dpre[h, r, 0:128] = (d1 * slope[h, r, 0:128]).astype(bf16)
            dpre[h, r, 128:256] = (d2 * slope[h, r, 128:256]).astype(bf16)

    def piece(h):
        @pl.loop(0, 4)
        def _(q):
            acc = jnp.zeros((256, 256), f32)
            for b in range(4):
                acc = acc + dot(nrm_t[b, pl.ds(al(q, 256), 256), :], dpre[h, b * 128:b * 128 + 128, :])
            ar_src[h + 1, pl.ds(al(q, 256), 256), :] = acc.astype(bf16)

        ar1(h + 1)

    def dnorm(block, dst):
        rows = pl.ds(al(block, 128), 128)

        @pl.loop(0, 4)
        def _(cb):
            acc = jnp.zeros((128, 256), f32)
            for h in range(4):
                acc = acc + dot_nt(dpre[h, rows, :], w[h, pl.ds(al(cb, 256), 256), :])
            dst[:, pl.ds(al(cb, 256), 256)] = acc.astype(dst.dtype)

    lo, hi = pl.ds(0, 64), pl.ds(64, 64)

    def rs_go(src, dst, k, way):
        c = rc(src, dst, rs_s.at[k], rs_r.at[k], {"ctx": way})
        c.start()
        sends.append(c.wait_send)
        flight["rs", k] = c.wait_recv

    backward(0)
    piece(0)
    g_near()
    g_far()
    for cb in range(4):
        ar_src[0, cb * 256:cb * 256 + 256, :] = dot_tn(gated[...], gbuf[:, cb * 256:cb * 256 + 256]).astype(bf16)
    ar1(0)
    backward(1)
    piece(1)
    ar2(1)
    arrive("gt")
    for cb in range(4):
        s = slice(cb * 256, cb * 256 + 256)
        acc = xp[:, s].astype(f32)
        for c in range(4):
            acc = acc + dot(gfull[c * 128:c * 128 + 128, :], wo[c * 256:c * 256 + 256, s])
        yd[:, s] = acc.astype(bf16)
    pack_back(yd, send_y)
    a2a_start(2, send_y, recv_y)

    ar2(0)
    backward(2)
    piece(2)
    ar2(2)
    ar3(1)
    backward(3)

    to_far, to_right, to_left = rs_send.at[0], rs_send.at[1], rs_send.at[2]
    dnorm(opp, to_far)
    rs_go(to_far.at[lo], rs1.at[0], 0, right)
    rs_go(to_far.at[hi], rs1.at[1], 1, left)
    dnorm(right, to_right)
    rs_go(to_right.at[hi], rs2.at[0, hi], 2, right)
    dnorm(left, to_left)
    rs_go(to_left.at[lo], rs2.at[1, lo], 3, left)
    piece(3)
    ar2(3)
    ar3(0)
    arrive(("rs", 0))
    to_right[lo, :] = (to_right[lo, :].astype(f32) + rs1[0].astype(f32)).astype(bf16)
    rs_go(to_right.at[lo], rs2.at[0, lo], 4, right)
    arrive(("rs", 1))
    to_left[hi, :] = (to_left[hi, :].astype(f32) + rs1[1].astype(f32)).astype(bf16)
    rs_go(to_left.at[hi], rs2.at[1, hi], 5, left)
    dnorm(cx, rs_own)
    ar2(4)
    ar3(2)
    ar4(1)
    arrive(("rs", 2), ("rs", 3), ("rs", 4), ("rs", 5))
    dn = rs_own[...] + rs2[0].astype(f32) + rs2[1].astype(f32)
    xh2 = xhat[...]
    mean_d = jnp.mean(dn, axis=1, keepdims=True)
    mean_dx = jnp.mean(dn * xh2, axis=1, keepdims=True)
    dx = gbuf[own, :].astype(f32) + rstd_ref[:, 0:1] * (dn - mean_d - xh2 * mean_dx)
    yd[...] = dx.astype(bf16)
    pack_back(yd, send_d)
    a2a_start(3, send_d, recv_d)
    ar3(3)
    ar4(0)
    ar4(2)
    ar3(4)
    ar4(3)
    arrive(("a2a", 2))
    unpack_home(recv_y, y_out)
    ar4(4)
    arrive(("a2a", 3))
    for p in range(PIECES):
        ar5(p)
    finish()


def last(scale, y, recv, pos_ref, ar, y_out, dx_out, proj, out):
    c = pl.program_id(0)
    y_out[...] = y[...]
    pos_l = jnp.broadcast_to(pos_ref[...], (ROWS, ROWS))
    pos_s = jnp.transpose(pos_l.astype(f32)).astype(i32)
    tgt_l, tgt_s = lax.shift_right_logical(pos_l, 9), lax.shift_right_logical(pos_s, 9)
    before = (tgt_l == tgt_s) & (iota((ROWS, ROWS), 1) < iota((ROWS, ROWS), 0))
    rank = jnp.sum(jnp.where(before, 1.0, 0.0), axis=1, keepdims=True).astype(i32)
    base = tgt_s[:, 0:1] * SLOTS
    lanes = iota((ROWS, 512), 1)
    acc = jnp.zeros((ROWS, 128), f32)
    for L in range(3):
        v = rank + (c * CAP - 16 * L)
        idx = jnp.where((v >= 0) & (v < 16), base + v, -1)
        acc = acc + dot(one(lanes == idx), recv[:, L * 128:L * 128 + 128])
    dx_out[...] = acc.astype(bf16)
    out[...] = ar[0].astype(f32) * scale
    for h in range(4):
        proj[:, h, :] = ar[h + 1].astype(f32) * scale


def shards(tokens, cotangent, packed_pos, segment_ids, w_proj, w_out):
    n_dp = lax.axis_size("dp")
    vmem, sem = pltpu.VMEM, pltpu.SemaphoreType.DMA
    scratch = [
        vmem((128, 1024), bf16), vmem((128, 1024), bf16), vmem((4, 1024, 256), bf16), vmem((1024, 1024), bf16), sem((4,)),
        vmem((512, 512), bf16), vmem((512, 512), bf16),
        vmem((512, 384), bf16), vmem((512, 384), bf16),
        vmem((512, 384), bf16), vmem((512, 384), bf16),
        vmem((512, 384), bf16),
        vmem((8, 512), f32), vmem((128, 128), i32),
        vmem((128, 1024), bf16), vmem((128, 1024), f32), vmem((128, 128), f32),
        vmem((512, 1024), bf16), vmem((4, 1024, 128), bf16), vmem((512, 1024), bf16),
        vmem((512, 512), f32), vmem((4, 512, 256), f32),
        vmem((4, 512, 128), bf16), vmem((4, 512, 128), bf16),
        vmem((4, 512, 128), bf16), vmem((4, 512, 128), bf16),
        vmem((4, 512, 512), bf16), vmem((4, 512, 512), bf16),
        vmem((512, 512), bf16), vmem((512, 128), f32),
        vmem((512, 256), f32), vmem((512, 256), f32), vmem((512, 256), bf16),
        vmem((4, 8, 512), f32), vmem((128, 512), f32),
        vmem((512, 256), bf16), vmem((512, 256), bf16),
        vmem((4, 512, 128), bf16), vmem((4, 512, 128), f32), vmem((4, 512, 256), bf16),
        vmem((4, 128, 256), bf16),
        vmem((128, 1024), bf16),
        vmem((PIECES, 1024, 256), bf16), vmem((PIECES, 512, 256), bf16),
        vmem((PIECES, 512, 256), bf16), vmem((PIECES, 512, 256), bf16),
        vmem((3, 128, 1024), bf16), vmem((128, 1024), f32),
        vmem((2, 64, 1024), bf16), vmem((2, 128, 1024), bf16),
        sem((4,)), sem((4,)), sem((2,)), sem((2, 6)), sem, sem, sem, sem, sem, sem,
        sem((PIECES,)), sem((PIECES,)), sem((PIECES,)), sem((PIECES,)),
        sem((PIECES,)), sem((PIECES,)), sem((PIECES,)), sem((PIECES,)), sem((6,)), sem((6,)),
    ]
    spec, free = pl.BlockSpec(memory_space=pltpu.VMEM), pl.BlockSpec(memory_space=pl.ANY)
    pos = packed_pos.reshape(1, ROWS)
    y, dx, ar = pl.pallas_call(
        functools.partial(kernel, n_dp),
        out_shape=[
            jax.ShapeDtypeStruct((ROWS, WIDTH), bf16),
            jax.ShapeDtypeStruct((512, 384), bf16),
            jax.ShapeDtypeStruct((PIECES, 1024, 256), bf16),
        ],
        in_specs=[free, free, spec, spec, free, free],
        out_specs=[spec] * 3,
        scratch_shapes=scratch,
        compiler_params=pltpu.CompilerParams(
            collective_id=0, has_side_effects=True, vmem_limit_bytes=60 * 1024 * 1024
        ),
        cost_estimate=pl.CostEstimate(flops=6 * 10**9, bytes_accessed=12 * 10**6, transcendentals=3 * 10**6),
    )(tokens, cotangent, pos, segment_ids, jnp.transpose(w_proj, (1, 0, 2)), w_out)
    scale = (ROWS * 4 * n_dp) ** (-0.5)
    return pl.pallas_call(
        functools.partial(last, scale),
        grid=(8,),
        out_shape=[
            jax.ShapeDtypeStruct((ROWS, WIDTH), bf16),
            jax.ShapeDtypeStruct((ROWS, WIDTH), bf16),
            jax.ShapeDtypeStruct((1024, 4, 256), f32),
            jax.ShapeDtypeStruct((256, WIDTH), f32),
        ],
        in_specs=[
            pl.BlockSpec((16, WIDTH), lambda i: (i, 0)),
            pl.BlockSpec((512, 384), lambda i: (0, 0)),
            pl.BlockSpec((1, ROWS), lambda i: (0, 0)),
            pl.BlockSpec((PIECES, 128, 256), lambda i: (0, i, 0)),
        ],
        out_specs=[
            pl.BlockSpec((16, WIDTH), lambda i: (i, 0)),
            pl.BlockSpec((ROWS, 128), lambda i: (0, i)),
            pl.BlockSpec((128, 4, 256), lambda i: (i, 0, 0)),
            pl.BlockSpec((128, 256), lambda i: (i % 2, i // 2)),
        ],
        cost_estimate=pl.CostEstimate(flops=10**8, bytes_accessed=10 * 10**6, transcendentals=0),
    )(y, dx, pos, ar)


def solution(mesh):
    return jax.shard_map(
        shards,
        mesh=mesh,
        in_specs=(
            P(("dp", "ctx"), None),
            P(("dp", "ctx"), None),
            P(("dp", "ctx")),
            P("dp", None),
            P(None, "ctx", None),
            P(),
        ),
        out_specs=(
            P(("dp", "ctx"), None),
            P(("dp", "ctx"), None),
            P(None, "ctx", None),
            P("ctx", None),
        ),
        check_vma=False,
    )
```

```python
import functools
import jax
import jax.numpy as jnp
from jax import lax
from jax.experimental import pallas as pl
from jax.experimental.pallas import tpu as pltpu
from jax.sharding import PartitionSpec as P

EPS = 1e-05
MESH = pl.DeviceIdType.MESH
bf16, f32, i32 = jnp.bfloat16, jnp.float32, jnp.int32
ROWS, WIDTH, GROUP, SLOTS = 128, 1024, 512, 16
CAP = 6
COMBOS = [(L, c) for L in range(3) for c in range(8) if c * CAP < 16 * L + 16 and c * CAP + CAP > 16 * L]
PIECES = 5


def dot(a, b):
    return lax.dot_general(a, b, (((1,), (0,)), ((), ())), preferred_element_type=f32)


def dot_nt(a, b):
    return lax.dot_general(a, b, (((1,), (1,)), ((), ())), preferred_element_type=f32)


def dot_tn(a, b):
    return lax.dot_general(a, b, (((0,), (0,)), ((), ())), preferred_element_type=f32)


def sigmoid(t):
    return 0.5 * jnp.tanh(0.5 * t) + 0.5


def iota(shape, axis):
    return lax.broadcasted_iota(i32, shape, axis)


def one(cond):
    return jnp.where(cond, 1.0, 0.0).astype(bf16)


def chunk(c):
    return pl.ds(c * 128, 128)


def kernel(
    n_dp,
    tok_h, cot_h, pos_ref, seg_ref, w_h, wo_h,
    y_out, recv_d, ar_f,
    tok, cot, w_raw, w, wo, in_s,
    send_x, recv_x, send_g, recv_g, send_y, recv_y, send_d,
    meta_t, rank_s, xp, xhat, rstd_ref, nrm, nrm_t, gbuf,
    msk, slope, uv, qk, kq, qz, p_ref, sl_ref, ds_ref, dq_ref,
    attn_ref, u_ref, dg_ref, st_all, cmb, gated, gfull, dout, du_ref, dpre, dg_send,
    yd, ar_src, ar_c, ar_h, ar_r, ar_q, ar_b, rs_send, rs_own, rs1, rs2,
    a2a_s, a2a_r, ag_s, ag_r, st_s, st_r, gt_s, gt_r, dg_s, dg_r, ar_ss, ar_rs, rs_s, rs_r,
):
    me, cx = lax.axis_index("dp"), lax.axis_index("ctx")
    core, chip = lax.rem(me, 2), lax.div(me, 2)
    other = 1 - core
    right, left, opp = lax.rem(cx + 1, 4), lax.rem(cx + 3, 4), lax.rem(cx + 2, 4)
    sends, flight = [], {}

    def rc(src, dst, ss, rs, dev):
        return pltpu.make_async_remote_copy(
            src_ref=src, dst_ref=dst, send_sem=ss, recv_sem=rs, device_id=dev, device_id_type=MESH
        )

    def wait_bytes(ref, ss, rs):
        return rc(ref, ref, ss, rs, {"ctx": right})

    def arrive(*keys):
        for key in keys:
            flight.pop(key)()

    def al(i, m):
        return pl.multiple_of(i * m, m)

    loads = [pltpu.make_async_copy(a, b, in_s.at[i]) for i, (a, b) in enumerate([(tok_h, tok), (cot_h, cot), (w_h, w_raw), (wo_h, wo)])]
    for c in loads:
        c.start()

    bar = pltpu.get_barrier_semaphore()

    @pl.loop(1, n_dp)
    def _(o):
        pl.semaphore_signal(bar, inc=1, device_id={"dp": lax.rem(me + o, n_dp)}, device_id_type=MESH)

    for o in range(1, 4):
        pl.semaphore_signal(bar, inc=1, device_id={"ctx": lax.rem(cx + o, 4)}, device_id_type=MESH)

    pos_l = jnp.broadcast_to(pos_ref[...], (ROWS, ROWS))
    pos_s = jnp.transpose(pos_l.astype(f32)).astype(i32)
    tgt_l, tgt_s = lax.shift_right_logical(pos_l, 9), lax.shift_right_logical(pos_s, 9)
    ii, jj = iota((ROWS, ROWS), 0), iota((ROWS, ROWS), 1)
    same = tgt_l == tgt_s
    rank_l = jnp.sum(jnp.where(same & (ii < jj), 1.0, 0.0), axis=0, keepdims=True).astype(i32)
    rank_c = jnp.sum(jnp.where(same & (jj < ii), 1.0, 0.0), axis=1, keepdims=True).astype(i32)
    tgt_row = tgt_l[:1] * SLOTS
    rank_s[...] = jnp.where(jj == 0, rank_c, tgt_s * SLOTS)
    row_no = (pos_s & (ROWS - 1)) + 1

    def pack_out(src, dst, with_meta):
        @pl.loop(0, 4)
        def _(rb):
            rows = pl.ds(al(rb, 128), 128)
            here = iota((128, ROWS), 0) + rb * 128
            meta = jnp.zeros((128, 128), f32)
            for L in range(3):
                acc = jnp.zeros((128, 128), f32)
                every = jnp.zeros((128, 128), f32)
                for c in [c for (l, c) in COMBOS if l == L]:
                    v = rank_l + (c * CAP - 16 * L)
                    idx = jnp.where((v >= 0) & (v < 16), tgt_row + v, -1)
                    hit = jnp.where(here == idx, 1.0, 0.0)
                    acc = acc + dot(hit.astype(bf16), src[:, c * 128:c * 128 + 128])
                    every = every + hit
                dst[rows, L * 128:L * 128 + 128] = acc.astype(bf16)
                if with_meta:
                    meta = meta + dot(every.astype(bf16), jnp.where(jj == L, row_no, 0).astype(f32).astype(bf16))
            if with_meta:
                dst[rows, 384:512] = meta.astype(bf16)

    def a2a_start(k, src, dst):
        mine = pl.ds(al(me, SLOTS), SLOTS)
        dst[mine, :] = src[mine, :]

        @pl.loop(1, n_dp)
        def _(o):
            t = lax.rem(me + o, n_dp)
            rc(src.at[pl.ds(al(t, SLOTS), SLOTS)], dst.at[mine], a2a_s.at[k], a2a_r.at[k], {"dp": t}).start()

        part = src.at[pl.ds(0, (n_dp - 1) * SLOTS)]
        sends.append(lambda: wait_bytes(part, a2a_s.at[k], a2a_r.at[k]).wait_send())
        come = dst.at[pl.ds(0, (n_dp - 1) * SLOTS)]
        flight["a2a", k] = lambda: wait_bytes(come, a2a_s.at[k], a2a_r.at[k]).wait_recv()

    def unpack_arrived(src, dst, rows):
        unit = iota((ROWS, 512), 1) & 15
        for c in range(8):
            acc = jnp.zeros((ROWS, 128), f32)
            for L in [l for (l, d) in COMBOS if d == c]:
                lo = c * CAP - 16 * L
                hit = (meta_t[L:L + 1, :] == (iota((ROWS, 512), 0) + 1).astype(f32)) & (unit >= lo) & (unit < lo + CAP)
                acc = acc + dot(one(hit), src[:, L * 128:L * 128 + 128])
            dst[rows, c * 128:c * 128 + 128] = acc.astype(bf16)

    def pack_back(src, dst):
        @pl.loop(0, 4)
        def _(rb):
            rows = pl.ds(al(rb, 128), 128)
            meta = recv_x[rows, 384:512].astype(f32)
            unit = iota((128, ROWS), 0) & 15
            lane = (iota((128, ROWS), 1) + 1).astype(f32)
            for L in range(3):
                acc = jnp.zeros((128, 128), f32)
                mine = meta[:, L:L + 1] == lane
                for c in [c for (l, c) in COMBOS if l == L]:
                    lo = c * CAP - 16 * L
                    acc = acc + dot(one(mine & (unit >= lo) & (unit < lo + CAP)), src[:, c * 128:c * 128 + 128])
                dst[rows, L * 128:L * 128 + 128] = acc.astype(bf16)

    def unpack_home(src, dst):
        rank, base = rank_s[:, 0:1], rank_s[:, 1:2]
        lanes = iota((ROWS, 512), 1)
        for c in range(8):
            acc = jnp.zeros((ROWS, 128), f32)
            for L in [l for (l, d) in COMBOS if d == c]:
                v = rank + (c * CAP - 16 * L)
                idx = jnp.where((v >= 0) & (v < 16), base + v, -1)
                acc = acc + dot(one(lanes == idx), src[:, L * 128:L * 128 + 128])
            dst[:, c * 128:c * 128 + 128] = acc.astype(bf16)

    def finish():
        for f in sends:
            f()

    loads[0].wait()
    pack_out(tok, send_x, True)
    pl.semaphore_wait(bar, n_dp - 1 + 3)
    a2a_start(0, send_x, recv_x)
    loads[1].wait()
    pack_out(cot, send_g, False)
    a2a_start(1, send_g, recv_g)

    seg_row = seg_ref[...]
    seg_col = jnp.transpose(jnp.broadcast_to(seg_row.astype(f32), (128, GROUP))).astype(i32)
    for b in range(4):
        sc = seg_col[b * 128:b * 128 + 128, 0:1]
        ok = (sc == seg_row) & (iota((128, GROUP), 1) <= iota((128, GROUP), 0) + b * 128)
        msk[b * 128:b * 128 + 128, :] = jnp.where(ok, 1.0, 0.0)
    cmb[...] = jnp.zeros_like(cmb)

    own = pl.ds(al(cx, 128), 128)
    loads[2].wait()

    @pl.loop(0, 16)
    def _(i):
        rows = pl.ds(al(i, 64), 64)
        w[:, rows, :] = jnp.swapaxes(w_raw[rows].astype(f32), 0, 1).astype(bf16)

    loads[3].wait()
    arrive(("a2a", 0))
    meta_t[...] = jnp.transpose(recv_x[:, 384:512].astype(f32))[:8]
    unpack_arrived(recv_x, xp, pl.ds(0, 128))
    xf = xp[...].astype(f32)
    mean = jnp.mean(xf, axis=1, keepdims=True)
    rstd = lax.rsqrt(jnp.mean((xf - mean) ** 2, axis=1, keepdims=True) + EPS)
    xh = (xf - mean) * rstd
    xhat[...] = xh
    rstd_ref[...] = jnp.broadcast_to(rstd, (ROWS, 128))
    nrm[own, :] = xh.astype(bf16)

    def half(b, k):
        return pl.ds(pl.multiple_of(b * 128 + k * 64, 64), 64)

    def ag(k, buf):
        def to(block, h, way, slot):
            ref = buf.at[half(block, h)]
            return rc(ref, ref, ag_s.at[k], ag_r.at[k, slot], {"ctx": way})

        def go(block, h, way, slot, source):
            to(block, h, way, slot).start()
            sends.append(to(block, h, way, slot).wait_send)
            flight["ag", k, slot] = to(source, h, way, slot).wait_recv

        def start():
            go(cx, 0, right, 0, left)
            go(cx, 1, left, 1, right)
            go(cx, 1, right, 2, left)
            go(cx, 0, left, 3, right)

        def forward():
            arrive(("ag", k, 0))
            go(left, 0, right, 4, opp)
            arrive(("ag", k, 1))
            go(right, 1, left, 5, opp)

        def near():
            arrive(("ag", k, 2), ("ag", k, 3))

        def far():
            arrive(("ag", k, 4), ("ag", k, 5))

        return start, forward, near, far

    lane_lo = iota((128, 128), 1) < 64

    def project(block):
        rows = pl.ds(al(block, 128), 128)
        nT = jnp.transpose(nrm[rows, :].astype(f32)).astype(bf16)
        nrm_t[block] = nT

        @pl.loop(0, 4)
        def _(h):
            pre = dot(nrm[rows, :], w[h])
            sig = sigmoid(pre)
            act = pre * sig
            slope[h, rows, :] = sig * (1.0 + pre * (1.0 - sig))
            uv[h, rows, :] = act[:, :128].astype(bf16)
            b = act[:, 128:].astype(bf16)
            qk[h, rows, :] = b
            bf = b.astype(f32)
            kq[h, rows, :] = pltpu.roll(bf, 64, 1).astype(bf16)
            qz[h, rows, :] = jnp.where(lane_lo, bf * 0.125, 0.0).astype(bf16)

    n_start, n_forward, n_near, n_far = ag(0, nrm)
    g_start, g_forward, g_near, g_far = ag(1, gbuf)
    n_start()
    arrive(("a2a", 1))
    unpack_arrived(recv_g, gbuf, own)
    n_forward()
    for t in range(4):
        dg_send[t] = dot_nt(gbuf[own, :], wo[t * 256:t * 256 + 256, :]).astype(bf16)
    for o in (2, 1, 3):
        t = lax.rem(cx + o, 4)
        rc(dg_send.at[t], dg_ref.at[own], dg_s, dg_r, {"ctx": t}).start()
    sends.append(lambda: wait_bytes(dg_ref.at[pl.ds(0, 384)], dg_s, dg_r).wait_send())
    flight["dg"] = lambda: wait_bytes(dg_ref.at[pl.ds(0, 384)], dg_s, dg_r).wait_recv()
    dg_ref[own, :] = dg_send[cx]
    project(cx)
    n_near()
    project(left)
    project(right)
    n_far()
    g_start()
    project(opp)

    for j in range(2):
        for half_j in range(2):
            h = 2 * j + half_j
            for b in range(4):
                r, n = slice(b * 128, b * 128 + 128), (b + 1) * 128
                t = dot_nt(qz[h, r, :], kq[h, :n, :])
                sig = sigmoid(t)
                m = msk[r, :n]
                pw = t * sig
                p = (pw * m).astype(bf16)
                p_ref[h, r, :n] = p
                sl_ref[h, r, :n] = ((sig + pw * (1.0 - sig)) * (m * 0.125)).astype(bf16)
                pv = dot(p, uv[h, :n, :]).astype(bf16).astype(f32)
                u_here = uv[h, r, :].astype(f32)
                if half_j == 0:
                    attn_ref[r, j * 128:j * 128 + 128] = pltpu.roll(pv, 64, 1)
                    u_ref[r, j * 128:j * 128 + 128] = u_here
                else:
                    attn_ref[r, j * 128:j * 128 + 128] = jnp.where(lane_lo, attn_ref[r, j * 128:j * 128 + 128], pv)
                    u_ref[r, j * 128:j * 128 + 128] = jnp.where(
                        lane_lo, u_ref[r, j * 128:j * 128 + 128], pltpu.roll(u_here, 64, 1)
                    )

    g_forward()
    arrive("dg")

    @pl.loop(0, 4)
    def _(b):
        r = pl.ds(al(b, 128), 128)
        dg = dg_ref[r, :].astype(f32)
        a = attn_ref[r, :]
        m = jnp.mean(a, axis=1, keepdims=True)
        ac = a - m
        e = dg * u_ref[r, :]
        lane = iota((128, 128), 1)
        st = jnp.where(lane == 0, m, jnp.sum(ac * ac, axis=1, keepdims=True))
        st = jnp.where(lane == 2, jnp.sum(e, axis=1, keepdims=True), st)
        st = jnp.where(lane == 3, jnp.sum(e * ac, axis=1, keepdims=True), st)
        st_all[cx, :, pl.ds(al(b, 128), 128)] = jnp.transpose(st)[:8]

    for o in range(1, 4):
        rc(st_all.at[cx], st_all.at[cx], st_s, st_r, {"ctx": lax.rem(cx + o, 4)}).start()
    sends.append(lambda: wait_bytes(st_all.at[pl.ds(0, 3)], st_s, st_r).wait_send())
    flight["st"] = lambda: wait_bytes(st_all.at[pl.ds(0, 3)], st_s, st_r).wait_recv()
    arrive("st")
    ms = [st_all[l, 0:1, :] for l in range(4)]
    m2 = (ms[0] + ms[1] + ms[2] + ms[3]) * 0.25
    sq, se, seo = 0.0, 0.0, 0.0
    for l in range(4):
        d = ms[l] - m2
        sq = sq + st_all[l, 1:2, :] + 256.0 * d * d
        se = se + st_all[l, 2:3, :]
        seo = seo + st_all[l, 3:4, :] + d * st_all[l, 2:3, :]
    r2 = lax.rsqrt(sq * (1.0 / WIDTH) + EPS)
    cmb[0:1, :] = m2
    cmb[1:2, :] = r2
    cmb[2:3, :] = se * (1.0 / WIDTH)
    cmb[3:4, :] = r2 * seo * (1.0 / WIDTH)

    for b in range(4):
        r = slice(b * 128, b * 128 + 128)
        tr = jnp.transpose(cmb[:, r])
        r2c = tr[:, 1:2]
        onorm = (attn_ref[r, :] - tr[:, 0:1]) * r2c
        u, dg = u_ref[r, :], dg_ref[r, :].astype(f32)
        gated[r, :] = (onorm * u).astype(bf16)
        du = (dg * onorm).astype(bf16).astype(f32)
        da = r2c * (dg * u - tr[:, 2:3] - onorm * tr[:, 3:4])
        for j in range(2):
            s = slice(j * 128, j * 128 + 128)
            dout[2 * j, r, :] = jnp.where(lane_lo, 0.0, pltpu.roll(da[:, s], 64, 1)).astype(bf16)
            dout[2 * j + 1, r, :] = jnp.where(lane_lo, 0.0, da[:, s]).astype(bf16)
            du_ref[2 * j, r, :] = du[:, s]
            du_ref[2 * j + 1, r, :] = pltpu.roll(du[:, s], 64, 1)

    for o in (2, 1, 3):
        t = lax.rem(cx + o, 4)
        rc(gated.at[pl.ds(al(t, 128), 128)], gfull.at[own], gt_s, gt_r, {"ctx": t}).start()
    sends.append(lambda: wait_bytes(gated.at[pl.ds(0, 384)], gt_s, gt_r).wait_send())
    flight["gt"] = lambda: wait_bytes(gfull.at[pl.ds(0, 384)], gt_s, gt_r).wait_recv()
    gfull[own, :] = gated[own, :]

    yy, zz = lax.div(chip, 4), lax.rem(chip, 4)
    base = core * 512

    def rows_at(start, count):
        return pl.ds(pl.multiple_of(start, count), count)

    def peer(axis, o):
        y2, z2 = (yy, lax.rem(zz + o, 4)) if axis == 0 else (lax.rem(yy + o, 4), zz)
        return lax.rem((zz if axis == 0 else yy) + o, 4), {"dp": (y2 * 4 + z2) * 2 + core}

    def ours(part):
        return (zz, yy) if part == 0 else (yy, zz)

    def begun(stage, p, ref):
        sends.append(lambda: wait_bytes(ref, ar_ss.at[stage, p], ar_rs.at[stage, p]).wait_send())
        flight["ar", stage, p] = lambda: wait_bytes(ref, ar_ss.at[stage, p], ar_rs.at[stage, p]).wait_recv()

    def to_core(stage, p, src, dst):
        rc(src, dst, ar_ss.at[stage, p], ar_rs.at[stage, p], {"dp": chip * 2 + other}).start()
        begun(stage, p, dst)

    def to_axis(stage, p, places, ref):
        @pl.loop(1, 4)
        def _(o):
            for part in range(2):
                axis = part if stage in (1, 4) else 1 - part
                t, dev = peer(axis, o)
                src, dst = places(part, t)
                rc(src, dst, ar_ss.at[stage, p], ar_rs.at[stage, p], dev).start()

        begun(stage, p, ref)

    def ar1(p):
        to_core(0, p, ar_src.at[p, rows_at(other * 512, 512)], ar_c.at[p])

    def ar2(p):
        arrive(("ar", 0, p))

        @pl.loop(0, 4)
        def _(b):
            r = rows_at(b * 128, 128)
            a = ar_src[p, rows_at(base + b * 128, 128), :].astype(f32)
            ar_h[p, r, :] = (a + ar_c[p, r, :].astype(f32)).astype(bf16)

        for part in range(2):
            mine = rows_at(part * 256 + ours(part)[0] * 64, 64)
            ar_r[p, mine, :] = ar_h[p, mine, :]

        def places(part, t):
            return (
                ar_h.at[p, rows_at(part * 256 + t * 64, 64)],
                ar_r.at[p, rows_at(part * 256 + ours(part)[0] * 64, 64)],
            )

        to_axis(1, p, places, ar_r.at[p, pl.ds(0, 384)])

    def ar3(p):
        arrive(("ar", 1, p))
        for part in range(2):
            acc = jnp.zeros((64, 256), f32)
            for k in range(4):
                acc = acc + ar_r[p, part * 256 + k * 64:part * 256 + k * 64 + 64, :].astype(f32)
            ar_q[p, part * 64:part * 64 + 64, :] = acc.astype(bf16)
            mine = rows_at(part * 64 + ours(part)[1] * 16, 16)
            ar_b[p, mine, :] = ar_q[p, mine, :]

        def places(part, t):
            return ar_q.at[p, rows_at(part * 64 + t * 16, 16)], ar_b.at[p, rows_at(part * 64 + ours(part)[1] * 16, 16)]

        to_axis(2, p, places, ar_b.at[p, pl.ds(0, 96)])

    def ar4(p):
        arrive(("ar", 2, p))
        for part in range(2):
            acc = jnp.zeros((16, 256), f32)
            for k in range(4):
                acc = acc + ar_b[p, part * 64 + k * 16:part * 64 + k * 16 + 16, :].astype(f32)
            first, second = ours(part)
            ar_f[p, rows_at(base + part * 256 + first * 64 + second * 16, 16), :] = acc.astype(bf16)

        def places(part, t):
            first, second = ours(part)
            ref = ar_f.at[p, rows_at(base + part * 256 + first * 64 + second * 16, 16)]
            return ref, ref

        to_axis(3, p, places, ar_f.at[p, pl.ds(0, 96)])

    def ar5(p):
        arrive(("ar", 3, p))

        def places(part, t):
            ref = ar_f.at[p, rows_at(base + part * 256 + ours(part)[0] * 64, 64)]
            return ref, ref

        to_axis(4, p, places, ar_f.at[p, pl.ds(0, 384)])

    def ar6(p):
        arrive(("ar", 4, p))
        ref = ar_f.at[p, rows_at(base, 512)]
        to_core(5, p, ref, ref)

    def backward(h):
        for b in range(4):
            r, n = slice(b * 128, b * 128 + 128), (b + 1) * 128
            dw = dot_nt(dout[h, r, :], uv[h, :n, :])
            ds = (dw * sl_ref[h, r, :n].astype(f32)).astype(bf16)
            ds_ref[r, :n] = ds
            dq_ref[r, :] = dot(ds, qk[h, :n, :])
        for b in range(4):
            r, c = slice(b * 128, b * 128 + 128), slice(b * 128, 512)
            dv = dot_tn(p_ref[h, c, r], dout[h, c, :])
            dk = dot_tn(ds_ref[c, r], qk[h, c, :])
            d1 = jnp.where(lane_lo, du_ref[h, r, :], dv)
            d2 = pltpu.roll(jnp.where(lane_lo, dk, dq_ref[r, :]), 64, 1)
            dpre[h, r, 0:128] = (d1 * slope[h, r, 0:128]).astype(bf16)
            dpre[h, r, 128:256] = (d2 * slope[h, r, 128:256]).astype(bf16)

    def piece(h):
        @pl.loop(0, 4)
        def _(q):
            acc = jnp.zeros((256, 256), f32)
            for b in range(4):
                acc = acc + dot(nrm_t[b, pl.ds(al(q, 256), 256), :], dpre[h, b * 128:b * 128 + 128, :])
            ar_src[h + 1, pl.ds(al(q, 256), 256), :] = acc.astype(bf16)

        ar1(h + 1)

    def dnorm(block, dst):
        rows = pl.ds(al(block, 128), 128)

        @pl.loop(0, 4)
        def _(cb):
            acc = jnp.zeros((128, 256), f32)
            for h in range(4):
                acc = acc + dot_nt(dpre[h, rows, :], w[h, pl.ds(al(cb, 256), 256), :])
            dst[:, pl.ds(al(cb, 256), 256)] = acc.astype(dst.dtype)

    lo, hi = pl.ds(0, 64), pl.ds(64, 64)

    def rs_go(src, dst, k, way):
        c = rc(src, dst, rs_s.at[k], rs_r.at[k], {"ctx": way})
        c.start()
        sends.append(c.wait_send)
        flight["rs", k] = c.wait_recv

    backward(0)
    piece(0)
    g_near()
    g_far()
    for cb in range(4):
        ar_src[0, cb * 256:cb * 256 + 256, :] = dot_tn(gated[...], gbuf[:, cb * 256:cb * 256 + 256]).astype(bf16)
    ar1(0)
    backward(1)
    piece(1)
    ar2(1)
    arrive("gt")
    for cb in range(4):
        s = slice(cb * 256, cb * 256 + 256)
        acc = xp[:, s].astype(f32)
        for c in range(4):
            acc = acc + dot(gfull[c * 128:c * 128 + 128, :], wo[c * 256:c * 256 + 256, s])
        yd[:, s] = acc.astype(bf16)
    pack_back(yd, send_y)
    a2a_start(2, send_y, recv_y)

    ar2(0)
    ar3(1)
    backward(2)
    piece(2)
    ar2(2)
    ar3(0)
    ar4(1)
    backward(3)

    to_far, to_right, to_left = rs_send.at[0], rs_send.at[1], rs_send.at[2]
    dnorm(opp, to_far)
    rs_go(to_far.at[lo], rs1.at[0], 0, right)
    rs_go(to_far.at[hi], rs1.at[1], 1, left)
    dnorm(right, to_right)
    rs_go(to_right.at[hi], rs2.at[0, hi], 2, right)
    dnorm(left, to_left)
    rs_go(to_left.at[lo], rs2.at[1, lo], 3, left)
    piece(3)
    ar2(3)
    ar3(2)
    ar4(0)
    ar5(1)
    arrive(("rs", 0))
    to_right[lo, :] = (to_right[lo, :].astype(f32) + rs1[0].astype(f32)).astype(bf16)
    rs_go(to_right.at[lo], rs2.at[0, lo], 4, right)
    arrive(("rs", 1))
    to_left[hi, :] = (to_left[hi, :].astype(f32) + rs1[1].astype(f32)).astype(bf16)
    rs_go(to_left.at[hi], rs2.at[1, hi], 5, left)
    ar2(4)
    ar3(3)
    ar4(2)
    ar5(0)
    ar6(1)
    dnorm(cx, rs_own)
    ar3(4)
    ar4(3)
    ar5(2)
    ar6(0)
    arrive(("rs", 2), ("rs", 3), ("rs", 4), ("rs", 5))
    dn = rs_own[...] + rs2[0].astype(f32) + rs2[1].astype(f32)
    xh2 = xhat[...]
    mean_d = jnp.mean(dn, axis=1, keepdims=True)
    mean_dx = jnp.mean(dn * xh2, axis=1, keepdims=True)
    dx = gbuf[own, :].astype(f32) + rstd_ref[:, 0:1] * (dn - mean_d - xh2 * mean_dx)
    yd[...] = dx.astype(bf16)
    pack_back(yd, send_d)
    a2a_start(3, send_d, recv_d)
    ar4(4)
    ar5(3)
    ar6(2)
    arrive(("a2a", 2))
    unpack_home(recv_y, y_out)
    ar5(4)
    ar6(3)
    ar6(4)
    arrive(("a2a", 3))
    for p in range(PIECES):
        arrive(("ar", 5, p))
    finish()


def last(scale, y, recv, pos_ref, ar, y_out, dx_out, proj, out):
    i = pl.program_id(0)
    y_out[...] = y[...]
    pos_l = jnp.broadcast_to(pos_ref[...], (ROWS, ROWS))
    pos_s = jnp.transpose(pos_l.astype(f32)).astype(i32)
    tgt_l, tgt_s = lax.shift_right_logical(pos_l, 9), lax.shift_right_logical(pos_s, 9)
    before = (tgt_l == tgt_s) & (iota((ROWS, ROWS), 1) < iota((ROWS, ROWS), 0))
    rank = jnp.sum(jnp.where(before, 1.0, 0.0), axis=1, keepdims=True).astype(i32)
    base = tgt_s[:, 0:1] * SLOTS
    lanes = iota((ROWS, 512), 1)
    for k in range(2):
        acc = jnp.zeros((ROWS, 128), f32)
        for L in range(3):
            v = rank + ((2 * i + k) * CAP - 16 * L)
            idx = jnp.where((v >= 0) & (v < 16), base + v, -1)
            acc = acc + dot(one(lanes == idx), recv[:, L * 128:L * 128 + 128])
        dx_out[:, k * 128:k * 128 + 128] = acc.astype(bf16)
    out[...] = ar[0].astype(f32) * scale
    for q in range(8):
        r = slice(q * 32, q * 32 + 32)
        proj[r] = jnp.swapaxes(ar[1:, r, :].astype(f32) * scale, 0, 1)


def shards(tokens, cotangent, packed_pos, segment_ids, w_proj, w_out):
    n_dp = lax.axis_size("dp")
    vmem, sem = pltpu.VMEM, pltpu.SemaphoreType.DMA
    scratch = [
        vmem((128, 1024), bf16), vmem((128, 1024), bf16), vmem((1024, 4, 256), bf16), vmem((4, 1024, 256), bf16),
        vmem((1024, 1024), bf16), sem((4,)),
        vmem((512, 512), bf16), vmem((512, 512), bf16),
        vmem((512, 384), bf16), vmem((512, 384), bf16),
        vmem((512, 384), bf16), vmem((512, 384), bf16),
        vmem((512, 384), bf16),
        vmem((8, 512), f32), vmem((128, 128), i32),
        vmem((128, 1024), bf16), vmem((128, 1024), f32), vmem((128, 128), f32),
        vmem((512, 1024), bf16), vmem((4, 1024, 128), bf16), vmem((512, 1024), bf16),
        vmem((512, 512), f32), vmem((4, 512, 256), f32),
        vmem((4, 512, 128), bf16), vmem((4, 512, 128), bf16),
        vmem((4, 512, 128), bf16), vmem((4, 512, 128), bf16),
        vmem((4, 512, 512), bf16), vmem((4, 512, 512), bf16),
        vmem((512, 512), bf16), vmem((512, 128), f32),
        vmem((512, 256), f32), vmem((512, 256), f32), vmem((512, 256), bf16),
        vmem((4, 8, 512), f32), vmem((128, 512), f32),
        vmem((512, 256), bf16), vmem((512, 256), bf16),
        vmem((4, 512, 128), bf16), vmem((4, 512, 128), f32), vmem((4, 512, 256), bf16),
        vmem((4, 128, 256), bf16),
        vmem((128, 1024), bf16),
        vmem((PIECES, 1024, 256), bf16), vmem((PIECES, 512, 256), bf16),
        vmem((PIECES, 512, 256), bf16), vmem((PIECES, 512, 256), bf16),
        vmem((PIECES, 128, 256), bf16), vmem((PIECES, 128, 256), bf16),
        vmem((3, 128, 1024), bf16), vmem((128, 1024), f32),
        vmem((2, 64, 1024), bf16), vmem((2, 128, 1024), bf16),
        sem((4,)), sem((4,)), sem((2,)), sem((2, 6)), sem, sem, sem, sem, sem, sem,
        sem((6, PIECES)), sem((6, PIECES)), sem((6,)), sem((6,)),
    ]
    spec, free = pl.BlockSpec(memory_space=pltpu.VMEM), pl.BlockSpec(memory_space=pl.ANY)
    pos = packed_pos.reshape(1, ROWS)
    y, dx, ar = pl.pallas_call(
        functools.partial(kernel, n_dp),
        out_shape=[
            jax.ShapeDtypeStruct((ROWS, WIDTH), bf16),
            jax.ShapeDtypeStruct((512, 384), bf16),
            jax.ShapeDtypeStruct((PIECES, 1024, 256), bf16),
        ],
        in_specs=[free, free, spec, spec, free, free],
        out_specs=[spec] * 3,
        scratch_shapes=scratch,
        compiler_params=pltpu.CompilerParams(
            collective_id=0, has_side_effects=True, vmem_limit_bytes=60 * 1024 * 1024
        ),
        cost_estimate=pl.CostEstimate(flops=6 * 10**9, bytes_accessed=12 * 10**6, transcendentals=3 * 10**6),
    )(tokens, cotangent, pos, segment_ids, w_proj, w_out)
    scale = (ROWS * 4 * n_dp) ** (-0.5)
    return pl.pallas_call(
        functools.partial(last, scale),
        grid=(4,),
        out_shape=[
            jax.ShapeDtypeStruct((ROWS, WIDTH), bf16),
            jax.ShapeDtypeStruct((ROWS, WIDTH), bf16),
            jax.ShapeDtypeStruct((1024, 4, 256), f32),
            jax.ShapeDtypeStruct((256, WIDTH), f32),
        ],
        in_specs=[
            pl.BlockSpec((32, WIDTH), lambda i: (i, 0)),
            pl.BlockSpec((512, 384), lambda i: (0, 0)),
            pl.BlockSpec((1, ROWS), lambda i: (0, 0)),
            pl.BlockSpec((PIECES, 256, 256), lambda i: (0, i, 0)),
        ],
        out_specs=[
            pl.BlockSpec((32, WIDTH), lambda i: (i, 0)),
            pl.BlockSpec((ROWS, 256), lambda i: (0, i)),
            pl.BlockSpec((256, 4, 256), lambda i: (i, 0, 0)),
            pl.BlockSpec((256, 256), lambda i: (0, i)),
        ],
        compiler_params=pltpu.CompilerParams(vmem_limit_bytes=40 * 1024 * 1024),
        cost_estimate=pl.CostEstimate(flops=10**8, bytes_accessed=10 * 10**6, transcendentals=0),
    )(y, dx, pos, ar)


def solution(mesh):
    return jax.shard_map(
        shards,
        mesh=mesh,
        in_specs=(
            P(("dp", "ctx"), None),
            P(("dp", "ctx"), None),
            P(("dp", "ctx")),
            P("dp", None),
            P(None, "ctx", None),
            P(),
        ),
        out_specs=(
            P(("dp", "ctx"), None),
            P(("dp", "ctx"), None),
            P(None, "ctx", None),
            P("ctx", None),
        ),
        check_vma=False,
    )
```

```python
import functools
import jax
import jax.numpy as jnp
from jax import lax
from jax.experimental import pallas as pl
from jax.experimental.pallas import tpu as pltpu
from jax.sharding import PartitionSpec as P

EPS = 1e-05
MESH = pl.DeviceIdType.MESH
bf16, f32, i32 = jnp.bfloat16, jnp.float32, jnp.int32
ROWS, WIDTH, GROUP, SLOTS = 128, 1024, 512, 16
CAP = 6
COMBOS = [(L, c) for L in range(3) for c in range(8) if c * CAP < 16 * L + 16 and c * CAP + CAP > 16 * L]
PIECES = 5


def dot(a, b):
    return lax.dot_general(a, b, (((1,), (0,)), ((), ())), preferred_element_type=f32)


def dot_nt(a, b):
    return lax.dot_general(a, b, (((1,), (1,)), ((), ())), preferred_element_type=f32)


def dot_tn(a, b):
    return lax.dot_general(a, b, (((0,), (0,)), ((), ())), preferred_element_type=f32)


def sigmoid(t):
    return 0.5 * jnp.tanh(0.5 * t) + 0.5


def iota(shape, axis):
    return lax.broadcasted_iota(i32, shape, axis)


def one(cond):
    return jnp.where(cond, 1.0, 0.0).astype(bf16)


def chunk(c):
    return pl.ds(c * 128, 128)


def kernel(
    n_dp,
    tok_h, cot_h, pos_ref, seg_ref, w_h, wo_h,
    y_out, recv_d, ar_f,
    tok, cot, w_raw, w, wo, in_s,
    send_x, recv_x, send_g, recv_g, send_y, recv_y, send_d,
    meta_t, rank_s, xp, xhat, rstd_ref, nrm, nrm_t, gbuf,
    msk, slope, uv, qk, kq, qz, p_ref, sl_ref, ds_ref, dq_ref,
    attn_ref, u_ref, dg_ref, st_all, cmb, gated, gfull, dout, du_ref, dpre, dg_send,
    yd, ar_src, ar_c, ar_h, ar_r, ar_q, ar_b, rs_send, rs_own, rs1, rs2,
    a2a_s, a2a_r, ag_s, ag_r, st_s, st_r, gt_s, gt_r, dg_s, dg_r, ar_ss, ar_rs, rs_s, rs_r,
):
    me, cx = lax.axis_index("dp"), lax.axis_index("ctx")
    core, chip = lax.rem(me, 2), lax.div(me, 2)
    other = 1 - core
    right, left, opp = lax.rem(cx + 1, 4), lax.rem(cx + 3, 4), lax.rem(cx + 2, 4)
    sends, flight = [], {}

    def rc(src, dst, ss, rs, dev):
        return pltpu.make_async_remote_copy(
            src_ref=src, dst_ref=dst, send_sem=ss, recv_sem=rs, device_id=dev, device_id_type=MESH
        )

    def wait_bytes(ref, ss, rs):
        return rc(ref, ref, ss, rs, {"ctx": right})

    def arrive(*keys):
        for key in keys:
            flight.pop(key)()

    def al(i, m):
        return pl.multiple_of(i * m, m)

    loads = [pltpu.make_async_copy(a, b, in_s.at[i]) for i, (a, b) in enumerate([(tok_h, tok), (cot_h, cot), (w_h, w_raw), (wo_h, wo)])]
    for c in loads:
        c.start()

    bar = pltpu.get_barrier_semaphore()

    @pl.loop(1, n_dp)
    def _(o):
        pl.semaphore_signal(bar, inc=1, device_id={"dp": lax.rem(me + o, n_dp)}, device_id_type=MESH)

    for o in range(1, 4):
        pl.semaphore_signal(bar, inc=1, device_id={"ctx": lax.rem(cx + o, 4)}, device_id_type=MESH)

    pos_l = jnp.broadcast_to(pos_ref[...], (ROWS, ROWS))
    pos_s = jnp.transpose(pos_l.astype(f32)).astype(i32)
    tgt_l, tgt_s = lax.shift_right_logical(pos_l, 9), lax.shift_right_logical(pos_s, 9)
    ii, jj = iota((ROWS, ROWS), 0), iota((ROWS, ROWS), 1)
    same = tgt_l == tgt_s
    rank_l = jnp.sum(jnp.where(same & (ii < jj), 1.0, 0.0), axis=0, keepdims=True).astype(i32)
    rank_c = jnp.sum(jnp.where(same & (jj < ii), 1.0, 0.0), axis=1, keepdims=True).astype(i32)
    tgt_row = tgt_l[:1] * SLOTS
    rank_s[...] = jnp.where(jj == 0, rank_c, tgt_s * SLOTS)
    row_no = (pos_s & (ROWS - 1)) + 1

    def pack_out(src, dst, with_meta):
        @pl.loop(0, 4)
        def _(rb):
            rows = pl.ds(al(rb, 128), 128)
            here = iota((128, ROWS), 0) + rb * 128
            meta = jnp.zeros((128, 128), f32)
            for L in range(3):
                acc = jnp.zeros((128, 128), f32)
                every = jnp.zeros((128, 128), f32)
                for c in [c for (l, c) in COMBOS if l == L]:
                    v = rank_l + (c * CAP - 16 * L)
                    idx = jnp.where((v >= 0) & (v < 16), tgt_row + v, -1)
                    hit = jnp.where(here == idx, 1.0, 0.0)
                    acc = acc + dot(hit.astype(bf16), src[:, c * 128:c * 128 + 128])
                    every = every + hit
                dst[rows, L * 128:L * 128 + 128] = acc.astype(bf16)
                if with_meta:
                    meta = meta + dot(every.astype(bf16), jnp.where(jj == L, row_no, 0).astype(f32).astype(bf16))
            if with_meta:
                dst[rows, 384:512] = meta.astype(bf16)

    def a2a_start(k, src, dst):
        mine = pl.ds(al(me, SLOTS), SLOTS)
        dst[mine, :] = src[mine, :]

        @pl.loop(1, n_dp)
        def _(o):
            t = lax.rem(me + o, n_dp)
            rc(src.at[pl.ds(al(t, SLOTS), SLOTS)], dst.at[mine], a2a_s.at[k], a2a_r.at[k], {"dp": t}).start()

        part = src.at[pl.ds(0, (n_dp - 1) * SLOTS)]
        sends.append(lambda: wait_bytes(part, a2a_s.at[k], a2a_r.at[k]).wait_send())
        come = dst.at[pl.ds(0, (n_dp - 1) * SLOTS)]
        flight["a2a", k] = lambda: wait_bytes(come, a2a_s.at[k], a2a_r.at[k]).wait_recv()

    def unpack_arrived(src, dst, rows):
        unit = iota((ROWS, 512), 1) & 15
        for c in range(8):
            acc = jnp.zeros((ROWS, 128), f32)
            for L in [l for (l, d) in COMBOS if d == c]:
                lo = c * CAP - 16 * L
                hit = (meta_t[L:L + 1, :] == (iota((ROWS, 512), 0) + 1).astype(f32)) & (unit >= lo) & (unit < lo + CAP)
                acc = acc + dot(one(hit), src[:, L * 128:L * 128 + 128])
            dst[rows, c * 128:c * 128 + 128] = acc.astype(bf16)

    def pack_back(src, dst):
        @pl.loop(0, 4)
        def _(rb):
            rows = pl.ds(al(rb, 128), 128)
            meta = recv_x[rows, 384:512].astype(f32)
            unit = iota((128, ROWS), 0) & 15
            lane = (iota((128, ROWS), 1) + 1).astype(f32)
            for L in range(3):
                acc = jnp.zeros((128, 128), f32)
                mine = meta[:, L:L + 1] == lane
                for c in [c for (l, c) in COMBOS if l == L]:
                    lo = c * CAP - 16 * L
                    acc = acc + dot(one(mine & (unit >= lo) & (unit < lo + CAP)), src[:, c * 128:c * 128 + 128])
                dst[rows, L * 128:L * 128 + 128] = acc.astype(bf16)

    def unpack_home(src, dst):
        rank, base = rank_s[:, 0:1], rank_s[:, 1:2]
        lanes = iota((ROWS, 512), 1)
        for c in range(8):
            acc = jnp.zeros((ROWS, 128), f32)
            for L in [l for (l, d) in COMBOS if d == c]:
                v = rank + (c * CAP - 16 * L)
                idx = jnp.where((v >= 0) & (v < 16), base + v, -1)
                acc = acc + dot(one(lanes == idx), src[:, L * 128:L * 128 + 128])
            dst[:, c * 128:c * 128 + 128] = acc.astype(bf16)

    def finish():
        for f in sends:
            f()

    loads[0].wait()
    pack_out(tok, send_x, True)
    pl.semaphore_wait(bar, n_dp - 1 + 3)
    a2a_start(0, send_x, recv_x)
    loads[1].wait()
    pack_out(cot, send_g, False)
    a2a_start(1, send_g, recv_g)

    seg_row = seg_ref[...]
    seg_col = jnp.transpose(jnp.broadcast_to(seg_row.astype(f32), (128, GROUP))).astype(i32)
    for b in range(4):
        sc = seg_col[b * 128:b * 128 + 128, 0:1]
        ok = (sc == seg_row) & (iota((128, GROUP), 1) <= iota((128, GROUP), 0) + b * 128)
        msk[b * 128:b * 128 + 128, :] = jnp.where(ok, 1.0, 0.0)
    cmb[...] = jnp.zeros_like(cmb)

    own = pl.ds(al(cx, 128), 128)
    loads[2].wait()

    @pl.loop(0, 16)
    def _(i):
        rows = pl.ds(al(i, 64), 64)
        w[:, rows, :] = jnp.swapaxes(w_raw[rows].astype(f32), 0, 1).astype(bf16)

    loads[3].wait()
    arrive(("a2a", 0))
    meta_t[...] = jnp.transpose(recv_x[:, 384:512].astype(f32))[:8]
    unpack_arrived(recv_x, xp, pl.ds(0, 128))
    xf = xp[...].astype(f32)
    mean = jnp.mean(xf, axis=1, keepdims=True)
    rstd = lax.rsqrt(jnp.mean((xf - mean) ** 2, axis=1, keepdims=True) + EPS)
    xh = (xf - mean) * rstd
    xhat[...] = xh
    rstd_ref[...] = jnp.broadcast_to(rstd, (ROWS, 128))
    nrm[own, :] = xh.astype(bf16)

    def half(b, k):
        return pl.ds(pl.multiple_of(b * 128 + k * 64, 64), 64)

    def ag(k, buf):
        def to(block, h, way, slot):
            ref = buf.at[half(block, h)]
            return rc(ref, ref, ag_s.at[k], ag_r.at[k, slot], {"ctx": way})

        def go(block, h, way, slot, source):
            to(block, h, way, slot).start()
            sends.append(to(block, h, way, slot).wait_send)
            flight["ag", k, slot] = to(source, h, way, slot).wait_recv

        def start():
            go(cx, 0, right, 0, left)
            go(cx, 1, left, 1, right)
            go(cx, 1, right, 2, left)
            go(cx, 0, left, 3, right)

        def forward():
            arrive(("ag", k, 0))
            go(left, 0, right, 4, opp)
            arrive(("ag", k, 1))
            go(right, 1, left, 5, opp)

        def near():
            arrive(("ag", k, 2), ("ag", k, 3))

        def far():
            arrive(("ag", k, 4), ("ag", k, 5))

        return start, forward, near, far

    lane_lo = iota((128, 128), 1) < 64

    def project(block):
        rows = pl.ds(al(block, 128), 128)
        for h in range(4):
            pre = dot(nrm[rows, :], w[h])
            sig = sigmoid(pre)
            act = pre * sig
            slope[h, rows, :] = sig + act * (1.0 - sig)
            uv[h, rows, :] = act[:, :128].astype(bf16)
            b = act[:, 128:].astype(bf16)
            qk[h, rows, :] = b
            bf = b.astype(f32)
            kq[h, rows, :] = pltpu.roll(bf, 64, 1).astype(bf16)
            qz[h, rows, :] = jnp.where(lane_lo, bf * 0.0625, 0.0).astype(bf16)

    def turn():
        for b in range(4):
            nrm_t[:, b * 128:b * 128 + 128] = jnp.transpose(nrm[b * 128:b * 128 + 128, :].astype(f32)).astype(bf16)

    n_start, n_forward, n_near, n_far = ag(0, nrm)
    g_start, g_forward, g_near, g_far = ag(1, gbuf)
    n_start()
    arrive(("a2a", 1))
    unpack_arrived(recv_g, gbuf, own)
    n_forward()
    for t in range(4):
        dg_send[t] = dot_nt(gbuf[own, :], wo[t * 256:t * 256 + 256, :]).astype(bf16)
    for o in (2, 1, 3):
        t = lax.rem(cx + o, 4)
        rc(dg_send.at[t], dg_ref.at[own], dg_s, dg_r, {"ctx": t}).start()
    sends.append(lambda: wait_bytes(dg_ref.at[pl.ds(0, 384)], dg_s, dg_r).wait_send())
    flight["dg"] = lambda: wait_bytes(dg_ref.at[pl.ds(0, 384)], dg_s, dg_r).wait_recv()
    dg_ref[own, :] = dg_send[cx]
    project(cx)
    n_near()
    project(left)
    project(right)
    n_far()
    g_start()
    project(opp)

    for j in range(2):
        for half_j in range(2):
            h = 2 * j + half_j
            for b in range(4):
                r, n = slice(b * 128, b * 128 + 128), (b + 1) * 128
                t = dot_nt(qz[h, r, :], kq[h, :n, :])
                th = jnp.tanh(t)
                m = msk[r, :n]
                up = 1.0 + th
                pw = t * up
                p = (pw * m).astype(bf16)
                p_ref[h, r, :n] = p
                sl_ref[h, r, :n] = ((up + pw * (1.0 - th)) * m).astype(bf16)
                pv = dot(p, uv[h, :n, :]).astype(bf16).astype(f32)
                u_here = uv[h, r, :].astype(f32)
                if half_j == 0:
                    attn_ref[r, j * 128:j * 128 + 128] = pltpu.roll(pv, 64, 1)
                    u_ref[r, j * 128:j * 128 + 128] = u_here
                else:
                    attn_ref[r, j * 128:j * 128 + 128] = jnp.where(lane_lo, attn_ref[r, j * 128:j * 128 + 128], pv)
                    u_ref[r, j * 128:j * 128 + 128] = jnp.where(
                        lane_lo, u_ref[r, j * 128:j * 128 + 128], pltpu.roll(u_here, 64, 1)
                    )

    g_forward()
    arrive("dg")

    @pl.loop(0, 4)
    def _(b):
        r = pl.ds(al(b, 128), 128)
        dg = dg_ref[r, :].astype(f32)
        a = attn_ref[r, :]
        m = jnp.mean(a, axis=1, keepdims=True)
        ac = a - m
        e = dg * u_ref[r, :]
        lane = iota((128, 128), 1)
        st = jnp.where(lane == 0, m, jnp.sum(ac * ac, axis=1, keepdims=True))
        st = jnp.where(lane == 2, jnp.sum(e, axis=1, keepdims=True), st)
        st = jnp.where(lane == 3, jnp.sum(e * ac, axis=1, keepdims=True), st)
        st_all[cx, :, pl.ds(al(b, 128), 128)] = jnp.transpose(st)[:8]

    for o in range(1, 4):
        rc(st_all.at[cx], st_all.at[cx], st_s, st_r, {"ctx": lax.rem(cx + o, 4)}).start()
    sends.append(lambda: wait_bytes(st_all.at[pl.ds(0, 3)], st_s, st_r).wait_send())
    flight["st"] = lambda: wait_bytes(st_all.at[pl.ds(0, 3)], st_s, st_r).wait_recv()
    turn()
    arrive("st")
    ms = [st_all[l, 0:1, :] for l in range(4)]
    m2 = (ms[0] + ms[1] + ms[2] + ms[3]) * 0.25
    sq, se, seo = 0.0, 0.0, 0.0
    for l in range(4):
        d = ms[l] - m2
        sq = sq + st_all[l, 1:2, :] + 256.0 * d * d
        se = se + st_all[l, 2:3, :]
        seo = seo + st_all[l, 3:4, :] + d * st_all[l, 2:3, :]
    r2 = lax.rsqrt(sq * (1.0 / WIDTH) + EPS)
    cmb[0:1, :] = m2
    cmb[1:2, :] = r2
    cmb[2:3, :] = se * (1.0 / WIDTH)
    cmb[3:4, :] = r2 * seo * (1.0 / WIDTH)

    for b in range(4):
        r = slice(b * 128, b * 128 + 128)
        tr = jnp.transpose(cmb[:, r])
        r2c = tr[:, 1:2]
        onorm = (attn_ref[r, :] - tr[:, 0:1]) * r2c
        u, dg = u_ref[r, :], dg_ref[r, :].astype(f32)
        gated[r, :] = (onorm * u).astype(bf16)
        du = (dg * onorm).astype(bf16).astype(f32)
        da = r2c * (dg * u - tr[:, 2:3] - onorm * tr[:, 3:4])
        for j in range(2):
            s = slice(j * 128, j * 128 + 128)
            dout[2 * j, r, :] = jnp.where(lane_lo, 0.0, pltpu.roll(da[:, s], 64, 1)).astype(bf16)
            dout[2 * j + 1, r, :] = jnp.where(lane_lo, 0.0, da[:, s]).astype(bf16)
            du_ref[2 * j, r, :] = du[:, s]
            du_ref[2 * j + 1, r, :] = pltpu.roll(du[:, s], 64, 1)

    for o in (2, 1, 3):
        t = lax.rem(cx + o, 4)
        rc(gated.at[pl.ds(al(t, 128), 128)], gfull.at[own], gt_s, gt_r, {"ctx": t}).start()
    sends.append(lambda: wait_bytes(gated.at[pl.ds(0, 384)], gt_s, gt_r).wait_send())
    flight["gt"] = lambda: wait_bytes(gfull.at[pl.ds(0, 384)], gt_s, gt_r).wait_recv()
    gfull[own, :] = gated[own, :]

    yy, zz = lax.div(chip, 4), lax.rem(chip, 4)
    base = core * 512

    def rows_at(start, count):
        return pl.ds(pl.multiple_of(start, count), count)

    def peer(axis, o):
        y2, z2 = (yy, lax.rem(zz + o, 4)) if axis == 0 else (lax.rem(yy + o, 4), zz)
        return lax.rem((zz if axis == 0 else yy) + o, 4), {"dp": (y2 * 4 + z2) * 2 + core}

    def ours(part):
        return (zz, yy) if part == 0 else (yy, zz)

    def begun(stage, p, ref):
        sends.append(lambda: wait_bytes(ref, ar_ss.at[stage, p], ar_rs.at[stage, p]).wait_send())
        flight["ar", stage, p] = lambda: wait_bytes(ref, ar_ss.at[stage, p], ar_rs.at[stage, p]).wait_recv()

    def to_core(stage, p, src, dst):
        rc(src, dst, ar_ss.at[stage, p], ar_rs.at[stage, p], {"dp": chip * 2 + other}).start()
        begun(stage, p, dst)

    def to_axis(stage, p, places, ref):
        @pl.loop(1, 4)
        def _(o):
            for part in range(2):
                axis = part if stage in (1, 4) else 1 - part
                t, dev = peer(axis, o)
                src, dst = places(part, t)
                rc(src, dst, ar_ss.at[stage, p], ar_rs.at[stage, p], dev).start()

        begun(stage, p, ref)

    def ar1(p):
        to_core(0, p, ar_src.at[p, rows_at(other * 512, 512)], ar_c.at[p])

    def ar2(p):
        arrive(("ar", 0, p))

        @pl.loop(0, 4)
        def _(b):
            r = rows_at(b * 128, 128)
            a = ar_src[p, rows_at(base + b * 128, 128), :].astype(f32)
            ar_h[p, r, :] = (a + ar_c[p, r, :].astype(f32)).astype(bf16)

        for part in range(2):
            mine = rows_at(part * 256 + ours(part)[0] * 64, 64)
            ar_r[p, mine, :] = ar_h[p, mine, :]

        def places(part, t):
            return (
                ar_h.at[p, rows_at(part * 256 + t * 64, 64)],
                ar_r.at[p, rows_at(part * 256 + ours(part)[0] * 64, 64)],
            )

        to_axis(1, p, places, ar_r.at[p, pl.ds(0, 384)])

    def ar3(p):
        arrive(("ar", 1, p))
        for part in range(2):
            acc = jnp.zeros((64, 256), f32)
            for k in range(4):
                acc = acc + ar_r[p, part * 256 + k * 64:part * 256 + k * 64 + 64, :].astype(f32)
            ar_q[p, part * 64:part * 64 + 64, :] = acc.astype(bf16)
            mine = rows_at(part * 64 + ours(part)[1] * 16, 16)
            ar_b[p, mine, :] = ar_q[p, mine, :]

        def places(part, t):
            return ar_q.at[p, rows_at(part * 64 + t * 16, 16)], ar_b.at[p, rows_at(part * 64 + ours(part)[1] * 16, 16)]

        to_axis(2, p, places, ar_b.at[p, pl.ds(0, 96)])

    def ar4(p):
        arrive(("ar", 2, p))
        for part in range(2):
            acc = jnp.zeros((16, 256), f32)
            for k in range(4):
                acc = acc + ar_b[p, part * 64 + k * 16:part * 64 + k * 16 + 16, :].astype(f32)
            first, second = ours(part)
            ar_f[p, rows_at(base + part * 256 + first * 64 + second * 16, 16), :] = acc.astype(bf16)

        def places(part, t):
            first, second = ours(part)
            ref = ar_f.at[p, rows_at(base + part * 256 + first * 64 + second * 16, 16)]
            return ref, ref

        to_axis(3, p, places, ar_f.at[p, pl.ds(0, 96)])

    def ar5(p):
        arrive(("ar", 3, p))

        def places(part, t):
            ref = ar_f.at[p, rows_at(base + part * 256 + ours(part)[0] * 64, 64)]
            return ref, ref

        to_axis(4, p, places, ar_f.at[p, pl.ds(0, 384)])

    def ar6(p):
        arrive(("ar", 4, p))
        ref = ar_f.at[p, rows_at(base, 512)]
        to_core(5, p, ref, ref)

    def backward(h):
        for b in range(4):
            r, n = slice(b * 128, b * 128 + 128), (b + 1) * 128
            dw = dot_nt(dout[h, r, :], uv[h, :n, :])
            ds = (dw * sl_ref[h, r, :n].astype(f32)).astype(bf16)
            ds_ref[r, :n] = ds
            dq_ref[r, :] = dot(ds, qk[h, :n, :])
        for b in range(4):
            r, c = slice(b * 128, b * 128 + 128), slice(b * 128, 512)
            dv = dot_tn(p_ref[h, c, r], dout[h, c, :])
            dk = dot_tn(ds_ref[c, r], qk[h, c, :])
            d1 = jnp.where(lane_lo, du_ref[h, r, :], dv)
            d2 = pltpu.roll(jnp.where(lane_lo, dk, dq_ref[r, :]), 64, 1) * 0.0625
            dpre[h, r, 0:128] = (d1 * slope[h, r, 0:128]).astype(bf16)
            dpre[h, r, 128:256] = (d2 * slope[h, r, 128:256]).astype(bf16)

    def piece(h):
        for q in range(4):
            acc = dot(nrm_t[q * 256:q * 256 + 256, :], dpre[h])
            ar_src[h + 1, q * 256:q * 256 + 256, :] = acc.astype(bf16)
        ar1(h + 1)

    def dnorm(block, dst):
        rows = pl.ds(al(block, 128), 128)

        @pl.loop(0, 4)
        def _(cb):
            acc = jnp.zeros((128, 256), f32)
            for h in range(4):
                acc = acc + dot_nt(dpre[h, rows, :], w[h, pl.ds(al(cb, 256), 256), :])
            dst[:, pl.ds(al(cb, 256), 256)] = acc.astype(dst.dtype)

    lo, hi = pl.ds(0, 64), pl.ds(64, 64)

    def rs_go(src, dst, k, way):
        c = rc(src, dst, rs_s.at[k], rs_r.at[k], {"ctx": way})
        c.start()
        sends.append(c.wait_send)
        flight["rs", k] = c.wait_recv

    backward(0)
    piece(0)
    g_near()
    g_far()
    for cb in range(4):
        ar_src[0, cb * 256:cb * 256 + 256, :] = dot_tn(gated[...], gbuf[:, cb * 256:cb * 256 + 256]).astype(bf16)
    ar1(0)
    backward(1)
    ar2(1)
    piece(1)
    ar2(0)
    backward(2)
    ar2(2)
    ar3(1)
    piece(2)
    ar3(0)
    backward(3)

    to_far, to_right, to_left = rs_send.at[0], rs_send.at[1], rs_send.at[2]
    dnorm(opp, to_far)
    rs_go(to_far.at[lo], rs1.at[0], 0, right)
    rs_go(to_far.at[hi], rs1.at[1], 1, left)
    dnorm(right, to_right)
    rs_go(to_right.at[hi], rs2.at[0, hi], 2, right)
    dnorm(left, to_left)
    rs_go(to_left.at[lo], rs2.at[1, lo], 3, left)
    piece(3)
    ar2(3)
    ar3(2)
    ar4(1)
    ar4(0)
    arrive(("rs", 0))
    to_right[lo, :] = (to_right[lo, :].astype(f32) + rs1[0].astype(f32)).astype(bf16)
    rs_go(to_right.at[lo], rs2.at[0, lo], 4, right)
    arrive(("rs", 1))
    to_left[hi, :] = (to_left[hi, :].astype(f32) + rs1[1].astype(f32)).astype(bf16)
    rs_go(to_left.at[hi], rs2.at[1, hi], 5, left)
    ar2(4)
    ar3(3)
    ar4(2)
    ar5(1)
    ar5(0)
    arrive("gt")
    for cb in range(4):
        s = slice(cb * 256, cb * 256 + 256)
        acc = xp[:, s].astype(f32)
        for c in range(4):
            acc = acc + dot(gfull[c * 128:c * 128 + 128, :], wo[c * 256:c * 256 + 256, s])
        yd[:, s] = acc.astype(bf16)
    pack_back(yd, send_y)
    a2a_start(2, send_y, recv_y)

    dnorm(cx, rs_own)
    ar3(4)
    ar4(3)
    ar5(2)
    ar6(1)
    ar6(0)
    arrive(("rs", 2), ("rs", 3), ("rs", 4), ("rs", 5))
    dn = rs_own[...] + rs2[0].astype(f32) + rs2[1].astype(f32)
    xh2 = xhat[...]
    mean_d = jnp.mean(dn, axis=1, keepdims=True)
    mean_dx = jnp.mean(dn * xh2, axis=1, keepdims=True)
    dx = gbuf[own, :].astype(f32) + rstd_ref[:, 0:1] * (dn - mean_d - xh2 * mean_dx)
    yd[...] = dx.astype(bf16)
    pack_back(yd, send_d)
    a2a_start(3, send_d, recv_d)
    ar4(4)
    ar5(3)
    ar6(2)
    arrive(("a2a", 2))
    unpack_home(recv_y, y_out)
    ar5(4)
    ar6(3)
    ar6(4)
    arrive(("a2a", 3))
    for p in range(PIECES):
        arrive(("ar", 5, p))
    finish()


def last(scale, y, recv, pos_ref, ar, y_out, dx_out, proj, out):
    i = pl.program_id(0)
    y_out[...] = y[...]
    pos_l = jnp.broadcast_to(pos_ref[...], (ROWS, ROWS))
    pos_s = jnp.transpose(pos_l.astype(f32)).astype(i32)
    tgt_l, tgt_s = lax.shift_right_logical(pos_l, 9), lax.shift_right_logical(pos_s, 9)
    before = (tgt_l == tgt_s) & (iota((ROWS, ROWS), 1) < iota((ROWS, ROWS), 0))
    rank = jnp.sum(jnp.where(before, 1.0, 0.0), axis=1, keepdims=True).astype(i32)
    base = tgt_s[:, 0:1] * SLOTS
    lanes = iota((ROWS, 512), 1)
    for k in range(2):
        acc = jnp.zeros((ROWS, 128), f32)
        for L in range(3):
            v = rank + ((2 * i + k) * CAP - 16 * L)
            idx = jnp.where((v >= 0) & (v < 16), base + v, -1)
            acc = acc + dot(one(lanes == idx), recv[:, L * 128:L * 128 + 128])
        dx_out[:, k * 128:k * 128 + 128] = acc.astype(bf16)
    out[...] = ar[0].astype(f32) * scale
    for q in range(8):
        r = slice(q * 32, q * 32 + 32)
        proj[r] = jnp.swapaxes(ar[1:, r, :].astype(f32) * scale, 0, 1)


def shards(tokens, cotangent, packed_pos, segment_ids, w_proj, w_out):
    n_dp = lax.axis_size("dp")
    vmem, sem = pltpu.VMEM, pltpu.SemaphoreType.DMA
    scratch = [
        vmem((128, 1024), bf16), vmem((128, 1024), bf16), vmem((1024, 4, 256), bf16), vmem((4, 1024, 256), bf16),
        vmem((1024, 1024), bf16), sem((4,)),
        vmem((512, 512), bf16), vmem((512, 512), bf16),
        vmem((512, 384), bf16), vmem((512, 384), bf16),
        vmem((512, 384), bf16), vmem((512, 384), bf16),
        vmem((512, 384), bf16),
        vmem((8, 512), f32), vmem((128, 128), i32),
        vmem((128, 1024), bf16), vmem((128, 1024), f32), vmem((128, 128), f32),
        vmem((512, 1024), bf16), vmem((1024, 512), bf16), vmem((512, 1024), bf16),
        vmem((512, 512), f32), vmem((4, 512, 256), f32),
        vmem((4, 512, 128), bf16), vmem((4, 512, 128), bf16),
        vmem((4, 512, 128), bf16), vmem((4, 512, 128), bf16),
        vmem((4, 512, 512), bf16), vmem((4, 512, 512), bf16),
        vmem((512, 512), bf16), vmem((512, 128), f32),
        vmem((512, 256), f32), vmem((512, 256), f32), vmem((512, 256), bf16),
        vmem((4, 8, 512), f32), vmem((128, 512), f32),
        vmem((512, 256), bf16), vmem((512, 256), bf16),
        vmem((4, 512, 128), bf16), vmem((4, 512, 128), f32), vmem((4, 512, 256), bf16),
        vmem((4, 128, 256), bf16),
        vmem((128, 1024), bf16),
        vmem((PIECES, 1024, 256), bf16), vmem((PIECES, 512, 256), bf16),
        vmem((PIECES, 512, 256), bf16), vmem((PIECES, 512, 256), bf16),
        vmem((PIECES, 128, 256), bf16), vmem((PIECES, 128, 256), bf16),
        vmem((3, 128, 1024), bf16), vmem((128, 1024), f32),
        vmem((2, 64, 1024), bf16), vmem((2, 128, 1024), bf16),
        sem((4,)), sem((4,)), sem((2,)), sem((2, 6)), sem, sem, sem, sem, sem, sem,
        sem((6, PIECES)), sem((6, PIECES)), sem((6,)), sem((6,)),
    ]
    spec, free = pl.BlockSpec(memory_space=pltpu.VMEM), pl.BlockSpec(memory_space=pl.ANY)
    pos = packed_pos.reshape(1, ROWS)
    y, dx, ar = pl.pallas_call(
        functools.partial(kernel, n_dp),
        out_shape=[
            jax.ShapeDtypeStruct((ROWS, WIDTH), bf16),
            jax.ShapeDtypeStruct((512, 384), bf16),
            jax.ShapeDtypeStruct((PIECES, 1024, 256), bf16),
        ],
        in_specs=[free, free, spec, spec, free, free],
        out_specs=[spec] * 3,
        scratch_shapes=scratch,
        compiler_params=pltpu.CompilerParams(
            collective_id=0, has_side_effects=True, vmem_limit_bytes=60 * 1024 * 1024
        ),
        cost_estimate=pl.CostEstimate(flops=6 * 10**9, bytes_accessed=12 * 10**6, transcendentals=3 * 10**6),
    )(tokens, cotangent, pos, segment_ids, w_proj, w_out)
    scale = (ROWS * 4 * n_dp) ** (-0.5)
    return pl.pallas_call(
        functools.partial(last, scale),
        grid=(4,),
        out_shape=[
            jax.ShapeDtypeStruct((ROWS, WIDTH), bf16),
            jax.ShapeDtypeStruct((ROWS, WIDTH), bf16),
            jax.ShapeDtypeStruct((1024, 4, 256), f32),
            jax.ShapeDtypeStruct((256, WIDTH), f32),
        ],
        in_specs=[
            pl.BlockSpec((32, WIDTH), lambda i: (i, 0)),
            pl.BlockSpec((512, 384), lambda i: (0, 0)),
            pl.BlockSpec((1, ROWS), lambda i: (0, 0)),
            pl.BlockSpec((PIECES, 256, 256), lambda i: (0, i, 0)),
        ],
        out_specs=[
            pl.BlockSpec((32, WIDTH), lambda i: (i, 0)),
            pl.BlockSpec((ROWS, 256), lambda i: (0, i)),
            pl.BlockSpec((256, 4, 256), lambda i: (i, 0, 0)),
            pl.BlockSpec((256, 256), lambda i: (0, i)),
        ],
        compiler_params=pltpu.CompilerParams(vmem_limit_bytes=60 * 1024 * 1024),
        cost_estimate=pl.CostEstimate(flops=10**8, bytes_accessed=10 * 10**6, transcendentals=0),
    )(y, dx, pos, ar)


def solution(mesh):
    return jax.shard_map(
        shards,
        mesh=mesh,
        in_specs=(
            P(("dp", "ctx"), None),
            P(("dp", "ctx"), None),
            P(("dp", "ctx")),
            P("dp", None),
            P(None, "ctx", None),
            P(),
        ),
        out_specs=(
            P(("dp", "ctx"), None),
            P(("dp", "ctx"), None),
            P(None, "ctx", None),
            P("ctx", None),
        ),
        check_vma=False,
    )
```

```python
import functools
import jax
import jax.numpy as jnp
from jax import lax
from jax.experimental import pallas as pl
from jax.experimental.pallas import tpu as pltpu
from jax.sharding import PartitionSpec as P

EPS = 1e-05
MESH = pl.DeviceIdType.MESH
bf16, f32, i32 = jnp.bfloat16, jnp.float32, jnp.int32
ROWS, WIDTH, GROUP, SLOTS = 128, 1024, 512, 16
CAP = 6
COMBOS = [(L, c) for L in range(3) for c in range(8) if c * CAP < 16 * L + 16 and c * CAP + CAP > 16 * L]
PIECES = 5


def dot(a, b):
    return lax.dot_general(a, b, (((1,), (0,)), ((), ())), preferred_element_type=f32)


def dot_nt(a, b):
    return lax.dot_general(a, b, (((1,), (1,)), ((), ())), preferred_element_type=f32)


def dot_tn(a, b):
    return lax.dot_general(a, b, (((0,), (0,)), ((), ())), preferred_element_type=f32)


def sigmoid(t):
    return 0.5 * jnp.tanh(0.5 * t) + 0.5


def iota(shape, axis):
    return lax.broadcasted_iota(i32, shape, axis)


def one(cond):
    return jnp.where(cond, 1.0, 0.0).astype(bf16)


def chunk(c):
    return pl.ds(c * 128, 128)


def kernel(
    n_dp,
    tok_h, cot_h, pos_ref, seg_ref, w_h, wo_h,
    y_out, recv_d, ar_f,
    tok, cot, w_raw, w, wo, in_s,
    send_x, recv_x, send_g, recv_g, send_y, recv_y, send_d,
    meta_t, rank_s, xp, xhat, rstd_ref, nrm, nrm_t, gbuf,
    msk, slope, uv, qk, kq, qz, p_ref, sl_ref, ds_ref, dq_ref,
    attn_ref, u_ref, dg_ref, st_all, cmb, gated, gfull, dout, du_ref, dpre, dg_send,
    yd, ar_src, ar_c, ar_h, ar_r, ar_q, ar_b, rs_send, rs_own, rs1, rs2,
    a2a_s, a2a_r, ag_s, ag_r, st_s, st_r, gt_s, gt_r, dg_s, dg_r, ar_ss, ar_rs, rs_s, rs_r,
):
    me, cx = lax.axis_index("dp"), lax.axis_index("ctx")
    core, chip = lax.rem(me, 2), lax.div(me, 2)
    other = 1 - core
    right, left, opp = lax.rem(cx + 1, 4), lax.rem(cx + 3, 4), lax.rem(cx + 2, 4)
    sends, flight = [], {}

    def rc(src, dst, ss, rs, dev):
        return pltpu.make_async_remote_copy(
            src_ref=src, dst_ref=dst, send_sem=ss, recv_sem=rs, device_id=dev, device_id_type=MESH
        )

    def wait_bytes(ref, ss, rs):
        return rc(ref, ref, ss, rs, {"ctx": right})

    def arrive(*keys):
        for key in keys:
            flight.pop(key)()

    def al(i, m):
        return pl.multiple_of(i * m, m)

    loads = [pltpu.make_async_copy(a, b, in_s.at[i]) for i, (a, b) in enumerate([(tok_h, tok), (cot_h, cot), (w_h, w_raw), (wo_h, wo)])]
    for c in loads:
        c.start()

    bar = pltpu.get_barrier_semaphore()

    @pl.loop(1, n_dp)
    def _(o):
        pl.semaphore_signal(bar, inc=1, device_id={"dp": lax.rem(me + o, n_dp)}, device_id_type=MESH)

    for o in range(1, 4):
        pl.semaphore_signal(bar, inc=1, device_id={"ctx": lax.rem(cx + o, 4)}, device_id_type=MESH)

    pos_l = jnp.broadcast_to(pos_ref[...], (ROWS, ROWS))
    pos_s = jnp.transpose(pos_l.astype(f32)).astype(i32)
    tgt_l, tgt_s = lax.shift_right_logical(pos_l, 9), lax.shift_right_logical(pos_s, 9)
    ii, jj = iota((ROWS, ROWS), 0), iota((ROWS, ROWS), 1)
    same = tgt_l == tgt_s
    rank_l = jnp.sum(jnp.where(same & (ii < jj), 1.0, 0.0), axis=0, keepdims=True).astype(i32)
    rank_c = jnp.sum(jnp.where(same & (jj < ii), 1.0, 0.0), axis=1, keepdims=True).astype(i32)
    tgt_row = tgt_l[:1] * SLOTS
    rank_s[...] = jnp.where(jj == 0, rank_c, tgt_s * SLOTS)
    row_no = (pos_s & (ROWS - 1)) + 1

    def pack_out(src, dst, with_meta):
        @pl.loop(0, 4)
        def _(rb):
            rows = pl.ds(al(rb, 128), 128)
            here = iota((128, ROWS), 0) + rb * 128
            meta = jnp.zeros((128, 128), f32)
            for L in range(3):
                acc = jnp.zeros((128, 128), f32)
                every = jnp.zeros((128, 128), f32)
                for c in [c for (l, c) in COMBOS if l == L]:
                    v = rank_l + (c * CAP - 16 * L)
                    idx = jnp.where((v >= 0) & (v < 16), tgt_row + v, -1)
                    hit = jnp.where(here == idx, 1.0, 0.0)
                    acc = acc + dot(hit.astype(bf16), src[:, c * 128:c * 128 + 128])
                    every = every + hit
                dst[rows, L * 128:L * 128 + 128] = acc.astype(bf16)
                if with_meta:
                    meta = meta + dot(every.astype(bf16), jnp.where(jj == L, row_no, 0).astype(f32).astype(bf16))
            if with_meta:
                dst[rows, 384:512] = meta.astype(bf16)

    def a2a_start(k, src, dst):
        mine = pl.ds(al(me, SLOTS), SLOTS)
        dst[mine, :] = src[mine, :]

        @pl.loop(1, n_dp)
        def _(o):
            t = lax.rem(me + o, n_dp)
            rc(src.at[pl.ds(al(t, SLOTS), SLOTS)], dst.at[mine], a2a_s.at[k], a2a_r.at[k], {"dp": t}).start()

        part = src.at[pl.ds(0, (n_dp - 1) * SLOTS)]
        sends.append(lambda: wait_bytes(part, a2a_s.at[k], a2a_r.at[k]).wait_send())
        come = dst.at[pl.ds(0, (n_dp - 1) * SLOTS)]
        flight["a2a", k] = lambda: wait_bytes(come, a2a_s.at[k], a2a_r.at[k]).wait_recv()

    def unpack_arrived(src, dst, rows):
        unit = iota((ROWS, 512), 1) & 15
        for c in range(8):
            acc = jnp.zeros((ROWS, 128), f32)
            for L in [l for (l, d) in COMBOS if d == c]:
                lo = c * CAP - 16 * L
                hit = (meta_t[L:L + 1, :] == (iota((ROWS, 512), 0) + 1).astype(f32)) & (unit >= lo) & (unit < lo + CAP)
                acc = acc + dot(one(hit), src[:, L * 128:L * 128 + 128])
            dst[rows, c * 128:c * 128 + 128] = acc.astype(bf16)

    def pack_back(src, dst):
        @pl.loop(0, 4)
        def _(rb):
            rows = pl.ds(al(rb, 128), 128)
            meta = recv_x[rows, 384:512].astype(f32)
            unit = iota((128, ROWS), 0) & 15
            lane = (iota((128, ROWS), 1) + 1).astype(f32)
            for L in range(3):
                acc = jnp.zeros((128, 128), f32)
                mine = meta[:, L:L + 1] == lane
                for c in [c for (l, c) in COMBOS if l == L]:
                    lo = c * CAP - 16 * L
                    acc = acc + dot(one(mine & (unit >= lo) & (unit < lo + CAP)), src[:, c * 128:c * 128 + 128])
                dst[rows, L * 128:L * 128 + 128] = acc.astype(bf16)

    def unpack_home(src, dst):
        rank, base = rank_s[:, 0:1], rank_s[:, 1:2]
        lanes = iota((ROWS, 512), 1)
        for c in range(8):
            acc = jnp.zeros((ROWS, 128), f32)
            for L in [l for (l, d) in COMBOS if d == c]:
                v = rank + (c * CAP - 16 * L)
                idx = jnp.where((v >= 0) & (v < 16), base + v, -1)
                acc = acc + dot(one(lanes == idx), src[:, L * 128:L * 128 + 128])
            dst[:, c * 128:c * 128 + 128] = acc.astype(bf16)

    def finish():
        for f in sends:
            f()

    loads[0].wait()
    pack_out(tok, send_x, True)
    pl.semaphore_wait(bar, n_dp - 1 + 3)
    a2a_start(0, send_x, recv_x)
    loads[1].wait()
    pack_out(cot, send_g, False)
    a2a_start(1, send_g, recv_g)

    seg_row = seg_ref[...]
    seg_col = jnp.transpose(jnp.broadcast_to(seg_row.astype(f32), (128, GROUP))).astype(i32)
    for b in range(4):
        sc = seg_col[b * 128:b * 128 + 128, 0:1]
        ok = (sc == seg_row) & (iota((128, GROUP), 1) <= iota((128, GROUP), 0) + b * 128)
        msk[b * 128:b * 128 + 128, :] = jnp.where(ok, 1.0, 0.0)
    cmb[...] = jnp.zeros_like(cmb)

    own = pl.ds(al(cx, 128), 128)
    loads[2].wait()

    @pl.loop(0, 16)
    def _(i):
        rows = pl.ds(al(i, 64), 64)
        w[:, rows, :] = jnp.swapaxes(w_raw[rows].astype(f32), 0, 1).astype(bf16)

    loads[3].wait()
    arrive(("a2a", 0))
    meta_t[...] = jnp.transpose(recv_x[:, 384:512].astype(f32))[:8]
    unpack_arrived(recv_x, xp, pl.ds(0, 128))
    xf = xp[...].astype(f32)
    mean = jnp.mean(xf, axis=1, keepdims=True)
    rstd = lax.rsqrt(jnp.mean((xf - mean) ** 2, axis=1, keepdims=True) + EPS)
    xh = (xf - mean) * rstd
    xhat[...] = xh
    rstd_ref[...] = jnp.broadcast_to(rstd, (ROWS, 128))
    nrm[own, :] = xh.astype(bf16)

    def half(b, k):
        return pl.ds(pl.multiple_of(b * 128 + k * 64, 64), 64)

    def ag(k, buf):
        def to(block, h, way, slot):
            ref = buf.at[half(block, h)]
            return rc(ref, ref, ag_s.at[k], ag_r.at[k, slot], {"ctx": way})

        def go(block, h, way, slot, source):
            to(block, h, way, slot).start()
            sends.append(to(block, h, way, slot).wait_send)
            flight["ag", k, slot] = to(source, h, way, slot).wait_recv

        def start():
            go(cx, 0, right, 0, left)
            go(cx, 1, left, 1, right)
            go(cx, 1, right, 2, left)
            go(cx, 0, left, 3, right)

        def forward():
            arrive(("ag", k, 0))
            go(left, 0, right, 4, opp)
            arrive(("ag", k, 1))
            go(right, 1, left, 5, opp)

        def near():
            arrive(("ag", k, 2), ("ag", k, 3))

        def far():
            arrive(("ag", k, 4), ("ag", k, 5))

        return start, forward, near, far

    lane_lo = iota((128, 128), 1) < 64

    def project(block):
        rows = pl.ds(al(block, 128), 128)
        for h in range(4):
            pre = dot(nrm[rows, :], w[h])
            sig = sigmoid(pre)
            act = pre * sig
            slope[h, rows, :] = sig + act * (1.0 - sig)
            uv[h, rows, :] = act[:, :128].astype(bf16)
            b = act[:, 128:].astype(bf16)
            qk[h, rows, :] = b
            bf = b.astype(f32)
            kq[h, rows, :] = pltpu.roll(bf, 64, 1).astype(bf16)
            qz[h, rows, :] = jnp.where(lane_lo, bf * 0.0625, 0.0).astype(bf16)

    def turn():
        for b in range(4):
            nrm_t[:, b * 128:b * 128 + 128] = jnp.transpose(nrm[b * 128:b * 128 + 128, :].astype(f32)).astype(bf16)

    n_start, n_forward, n_near, n_far = ag(0, nrm)
    g_start, g_forward, g_near, g_far = ag(1, gbuf)
    n_start()
    arrive(("a2a", 1))
    unpack_arrived(recv_g, gbuf, own)
    n_forward()
    for t in range(4):
        dg_send[t] = dot_nt(gbuf[own, :], wo[t * 256:t * 256 + 256, :]).astype(bf16)
    for o in (2, 1, 3):
        t = lax.rem(cx + o, 4)
        rc(dg_send.at[t], dg_ref.at[own], dg_s, dg_r, {"ctx": t}).start()
    sends.append(lambda: wait_bytes(dg_ref.at[pl.ds(0, 384)], dg_s, dg_r).wait_send())
    flight["dg"] = lambda: wait_bytes(dg_ref.at[pl.ds(0, 384)], dg_s, dg_r).wait_recv()
    dg_ref[own, :] = dg_send[cx]
    project(cx)
    n_near()
    project(left)
    project(right)
    n_far()
    project(opp)

    for j in range(2):
        for half_j in range(2):
            h = 2 * j + half_j
            for b in range(4):
                r, n = slice(b * 128, b * 128 + 128), (b + 1) * 128
                t = dot_nt(qz[h, r, :], kq[h, :n, :])
                th = jnp.tanh(t)
                m = msk[r, :n]
                up = 1.0 + th
                pw = t * up
                p = (pw * m).astype(bf16)
                p_ref[h, r, :n] = p
                sl_ref[h, r, :n] = ((up + pw * (1.0 - th)) * m).astype(bf16)
                pv = dot(p, uv[h, :n, :]).astype(bf16).astype(f32)
                u_here = uv[h, r, :].astype(f32)
                if half_j == 0:
                    attn_ref[r, j * 128:j * 128 + 128] = pltpu.roll(pv, 64, 1)
                    u_ref[r, j * 128:j * 128 + 128] = u_here
                else:
                    attn_ref[r, j * 128:j * 128 + 128] = jnp.where(lane_lo, attn_ref[r, j * 128:j * 128 + 128], pv)
                    u_ref[r, j * 128:j * 128 + 128] = jnp.where(
                        lane_lo, u_ref[r, j * 128:j * 128 + 128], pltpu.roll(u_here, 64, 1)
                    )

    arrive("dg")

    @pl.loop(0, 4)
    def _(b):
        r = pl.ds(al(b, 128), 128)
        dg = dg_ref[r, :].astype(f32)
        a = attn_ref[r, :]
        m = jnp.mean(a, axis=1, keepdims=True)
        ac = a - m
        e = dg * u_ref[r, :]
        lane = iota((128, 128), 1)
        st = jnp.where(lane == 0, m, jnp.sum(ac * ac, axis=1, keepdims=True))
        st = jnp.where(lane == 2, jnp.sum(e, axis=1, keepdims=True), st)
        st = jnp.where(lane == 3, jnp.sum(e * ac, axis=1, keepdims=True), st)
        st_all[cx, :, pl.ds(al(b, 128), 128)] = jnp.transpose(st)[:8]

    for o in range(1, 4):
        rc(st_all.at[cx], st_all.at[cx], st_s, st_r, {"ctx": lax.rem(cx + o, 4)}).start()
    sends.append(lambda: wait_bytes(st_all.at[pl.ds(0, 3)], st_s, st_r).wait_send())
    flight["st"] = lambda: wait_bytes(st_all.at[pl.ds(0, 3)], st_s, st_r).wait_recv()
    turn()
    arrive("st")
    g_start()
    ms = [st_all[l, 0:1, :] for l in range(4)]
    m2 = (ms[0] + ms[1] + ms[2] + ms[3]) * 0.25
    sq, se, seo = 0.0, 0.0, 0.0
    for l in range(4):
        d = ms[l] - m2
        sq = sq + st_all[l, 1:2, :] + 256.0 * d * d
        se = se + st_all[l, 2:3, :]
        seo = seo + st_all[l, 3:4, :] + d * st_all[l, 2:3, :]
    r2 = lax.rsqrt(sq * (1.0 / WIDTH) + EPS)
    cmb[0:1, :] = m2
    cmb[1:2, :] = r2
    cmb[2:3, :] = se * (1.0 / WIDTH)
    cmb[3:4, :] = r2 * seo * (1.0 / WIDTH)

    for b in range(4):
        r = slice(b * 128, b * 128 + 128)
        tr = jnp.transpose(cmb[:, r])
        r2c = tr[:, 1:2]
        onorm = (attn_ref[r, :] - tr[:, 0:1]) * r2c
        u, dg = u_ref[r, :], dg_ref[r, :].astype(f32)
        gated[r, :] = (onorm * u).astype(bf16)
        du = (dg * onorm).astype(bf16).astype(f32)
        da = r2c * (dg * u - tr[:, 2:3] - onorm * tr[:, 3:4])
        for j in range(2):
            s = slice(j * 128, j * 128 + 128)
            dout[2 * j, r, :] = jnp.where(lane_lo, 0.0, pltpu.roll(da[:, s], 64, 1)).astype(bf16)
            dout[2 * j + 1, r, :] = jnp.where(lane_lo, 0.0, da[:, s]).astype(bf16)
            du_ref[2 * j, r, :] = du[:, s]
            du_ref[2 * j + 1, r, :] = pltpu.roll(du[:, s], 64, 1)

    for o in (2, 1, 3):
        t = lax.rem(cx + o, 4)
        rc(gated.at[pl.ds(al(t, 128), 128)], gfull.at[own], gt_s, gt_r, {"ctx": t}).start()
    sends.append(lambda: wait_bytes(gated.at[pl.ds(0, 384)], gt_s, gt_r).wait_send())
    flight["gt"] = lambda: wait_bytes(gfull.at[pl.ds(0, 384)], gt_s, gt_r).wait_recv()
    gfull[own, :] = gated[own, :]

    yy, zz = lax.div(chip, 4), lax.rem(chip, 4)
    base = core * 512

    def rows_at(start, count):
        return pl.ds(pl.multiple_of(start, count), count)

    def peer(axis, o):
        y2, z2 = (yy, lax.rem(zz + o, 4)) if axis == 0 else (lax.rem(yy + o, 4), zz)
        return lax.rem((zz if axis == 0 else yy) + o, 4), {"dp": (y2 * 4 + z2) * 2 + core}

    def ours(part):
        return (zz, yy) if part == 0 else (yy, zz)

    def begun(stage, p, ref):
        sends.append(lambda: wait_bytes(ref, ar_ss.at[stage, p], ar_rs.at[stage, p]).wait_send())
        flight["ar", stage, p] = lambda: wait_bytes(ref, ar_ss.at[stage, p], ar_rs.at[stage, p]).wait_recv()

    def to_core(stage, p, src, dst):
        rc(src, dst, ar_ss.at[stage, p], ar_rs.at[stage, p], {"dp": chip * 2 + other}).start()
        begun(stage, p, dst)

    def to_axis(stage, p, places, ref):
        @pl.loop(1, 4)
        def _(o):
            for part in range(2):
                axis = part if stage in (1, 4) else 1 - part
                t, dev = peer(axis, o)
                src, dst = places(part, t)
                rc(src, dst, ar_ss.at[stage, p], ar_rs.at[stage, p], dev).start()

        begun(stage, p, ref)

    def ar1(p):
        to_core(0, p, ar_src.at[p, rows_at(other * 512, 512)], ar_c.at[p])

    def ar2(p):
        arrive(("ar", 0, p))

        @pl.loop(0, 4)
        def _(b):
            r = rows_at(b * 128, 128)
            a = ar_src[p, rows_at(base + b * 128, 128), :].astype(f32)
            ar_h[p, r, :] = (a + ar_c[p, r, :].astype(f32)).astype(bf16)

        for part in range(2):
            mine = rows_at(part * 256 + ours(part)[0] * 64, 64)
            ar_r[p, mine, :] = ar_h[p, mine, :]

        def places(part, t):
            return (
                ar_h.at[p, rows_at(part * 256 + t * 64, 64)],
                ar_r.at[p, rows_at(part * 256 + ours(part)[0] * 64, 64)],
            )

        to_axis(1, p, places, ar_r.at[p, pl.ds(0, 384)])

    def ar3(p):
        arrive(("ar", 1, p))
        for part in range(2):
            acc = jnp.zeros((64, 256), f32)
            for k in range(4):
                acc = acc + ar_r[p, part * 256 + k * 64:part * 256 + k * 64 + 64, :].astype(f32)
            ar_q[p, part * 64:part * 64 + 64, :] = acc.astype(bf16)
            mine = rows_at(part * 64 + ours(part)[1] * 16, 16)
            ar_b[p, mine, :] = ar_q[p, mine, :]

        def places(part, t):
            return ar_q.at[p, rows_at(part * 64 + t * 16, 16)], ar_b.at[p, rows_at(part * 64 + ours(part)[1] * 16, 16)]

        to_axis(2, p, places, ar_b.at[p, pl.ds(0, 96)])

    def ar4(p):
        arrive(("ar", 2, p))
        for part in range(2):
            acc = jnp.zeros((16, 256), f32)
            for k in range(4):
                acc = acc + ar_b[p, part * 64 + k * 16:part * 64 + k * 16 + 16, :].astype(f32)
            first, second = ours(part)
            ar_f[p, rows_at(base + part * 256 + first * 64 + second * 16, 16), :] = acc.astype(bf16)

        def places(part, t):
            first, second = ours(part)
            ref = ar_f.at[p, rows_at(base + part * 256 + first * 64 + second * 16, 16)]
            return ref, ref

        to_axis(3, p, places, ar_f.at[p, pl.ds(0, 96)])

    def ar5(p):
        arrive(("ar", 3, p))

        def places(part, t):
            ref = ar_f.at[p, rows_at(base + part * 256 + ours(part)[0] * 64, 64)]
            return ref, ref

        to_axis(4, p, places, ar_f.at[p, pl.ds(0, 384)])

    def ar6(p):
        arrive(("ar", 4, p))
        ref = ar_f.at[p, rows_at(base, 512)]
        to_core(5, p, ref, ref)

    def backward(h):
        for b in range(4):
            r, n = slice(b * 128, b * 128 + 128), (b + 1) * 128
            dw = dot_nt(dout[h, r, :], uv[h, :n, :])
            ds = (dw * sl_ref[h, r, :n].astype(f32)).astype(bf16)
            ds_ref[r, :n] = ds
            dq_ref[r, :] = dot(ds, qk[h, :n, :])
        for b in range(4):
            r, c = slice(b * 128, b * 128 + 128), slice(b * 128, 512)
            dv = dot_tn(p_ref[h, c, r], dout[h, c, :])
            dk = dot_tn(ds_ref[c, r], qk[h, c, :])
            d1 = jnp.where(lane_lo, du_ref[h, r, :], dv)
            d2 = pltpu.roll(jnp.where(lane_lo, dk, dq_ref[r, :]), 64, 1) * 0.0625
            dpre[h, r, 0:128] = (d1 * slope[h, r, 0:128]).astype(bf16)
            dpre[h, r, 128:256] = (d2 * slope[h, r, 128:256]).astype(bf16)

    def piece(h):
        for q in range(4):
            acc = dot(nrm_t[q * 256:q * 256 + 256, :], dpre[h])
            ar_src[h + 1, q * 256:q * 256 + 256, :] = acc.astype(bf16)
        ar1(h + 1)

    def dnorm(block, dst):
        rows = pl.ds(al(block, 128), 128)

        for cb in range(4):
            s = slice(cb * 256, cb * 256 + 256)
            acc = dot_nt(dpre[0, rows, :], w[0, s, :])
            for h in range(1, 4):
                acc = acc + dot_nt(dpre[h, rows, :], w[h, s, :])
            dst[:, s] = acc.astype(dst.dtype)

    lo, hi = pl.ds(0, 64), pl.ds(64, 64)

    def rs_go(src, dst, k, way):
        c = rc(src, dst, rs_s.at[k], rs_r.at[k], {"ctx": way})
        c.start()
        sends.append(c.wait_send)
        flight["rs", k] = c.wait_recv

    backward(0)
    piece(0)
    backward(1)
    ar2(1)
    piece(1)
    g_forward()
    backward(2)
    ar2(2)
    piece(2)
    ar3(1)
    backward(3)

    to_far, to_right, to_left = rs_send.at[0], rs_send.at[1], rs_send.at[2]
    dnorm(opp, to_far)
    rs_go(to_far.at[lo], rs1.at[0], 0, right)
    rs_go(to_far.at[hi], rs1.at[1], 1, left)
    dnorm(right, to_right)
    rs_go(to_right.at[hi], rs2.at[0, hi], 2, right)
    dnorm(left, to_left)
    rs_go(to_left.at[lo], rs2.at[1, lo], 3, left)
    piece(3)
    ar2(3)
    ar3(2)
    ar4(1)
    arrive(("rs", 0))
    to_right[lo, :] = (to_right[lo, :].astype(f32) + rs1[0].astype(f32)).astype(bf16)
    rs_go(to_right.at[lo], rs2.at[0, lo], 4, right)
    arrive(("rs", 1))
    to_left[hi, :] = (to_left[hi, :].astype(f32) + rs1[1].astype(f32)).astype(bf16)
    rs_go(to_left.at[hi], rs2.at[1, hi], 5, left)
    g_near()
    g_far()
    for cb in range(4):
        ar_src[0, cb * 256:cb * 256 + 256, :] = dot_tn(gated[...], gbuf[:, cb * 256:cb * 256 + 256]).astype(bf16)
    ar1(0)
    ar2(4)
    ar3(3)
    ar4(2)
    ar5(1)
    arrive("gt")
    for cb in range(4):
        s = slice(cb * 256, cb * 256 + 256)
        acc = xp[:, s].astype(f32)
        for c in range(4):
            acc = acc + dot(gfull[c * 128:c * 128 + 128, :], wo[c * 256:c * 256 + 256, s])
        yd[:, s] = acc.astype(bf16)
    pack_back(yd, send_y)
    a2a_start(2, send_y, recv_y)

    ar2(0)
    ar3(4)
    ar4(3)
    ar5(2)
    ar6(1)
    dnorm(cx, rs_own)
    ar3(0)
    ar4(4)
    ar5(3)
    ar6(2)
    arrive(("rs", 2), ("rs", 3), ("rs", 4), ("rs", 5))
    dn = rs_own[...] + rs2[0].astype(f32) + rs2[1].astype(f32)
    xh2 = xhat[...]
    mean_d = jnp.mean(dn, axis=1, keepdims=True)
    mean_dx = jnp.mean(dn * xh2, axis=1, keepdims=True)
    dx = gbuf[own, :].astype(f32) + rstd_ref[:, 0:1] * (dn - mean_d - xh2 * mean_dx)
    yd[...] = dx.astype(bf16)
    pack_back(yd, send_d)
    a2a_start(3, send_d, recv_d)
    ar4(0)
    ar5(4)
    ar6(3)
    arrive(("a2a", 2))
    unpack_home(recv_y, y_out)
    ar5(0)
    ar6(4)
    ar6(0)
    arrive(("a2a", 3))
    for p in range(PIECES):
        arrive(("ar", 5, p))
    finish()


def last(scale, y, recv, pos_ref, ar, y_out, dx_out, proj, out):
    i = pl.program_id(0)
    y_out[...] = y[...]
    pos_l = jnp.broadcast_to(pos_ref[...], (ROWS, ROWS))
    pos_s = jnp.transpose(pos_l.astype(f32)).astype(i32)
    tgt_l, tgt_s = lax.shift_right_logical(pos_l, 9), lax.shift_right_logical(pos_s, 9)
    before = (tgt_l == tgt_s) & (iota((ROWS, ROWS), 1) < iota((ROWS, ROWS), 0))
    rank = jnp.sum(jnp.where(before, 1.0, 0.0), axis=1, keepdims=True).astype(i32)
    base = tgt_s[:, 0:1] * SLOTS
    lanes = iota((ROWS, 512), 1)
    for k in range(2):
        acc = jnp.zeros((ROWS, 128), f32)
        for L in range(3):
            v = rank + ((2 * i + k) * CAP - 16 * L)
            idx = jnp.where((v >= 0) & (v < 16), base + v, -1)
            acc = acc + dot(one(lanes == idx), recv[:, L * 128:L * 128 + 128])
        dx_out[:, k * 128:k * 128 + 128] = acc.astype(bf16)
    out[...] = ar[0].astype(f32) * scale
    for q in range(8):
        r = slice(q * 32, q * 32 + 32)
        proj[r] = jnp.swapaxes(ar[1:, r, :].astype(f32) * scale, 0, 1)


def shards(tokens, cotangent, packed_pos, segment_ids, w_proj, w_out):
    n_dp = lax.axis_size("dp")
    vmem, sem = pltpu.VMEM, pltpu.SemaphoreType.DMA
    scratch = [
        vmem((128, 1024), bf16), vmem((128, 1024), bf16), vmem((1024, 4, 256), bf16), vmem((4, 1024, 256), bf16),
        vmem((1024, 1024), bf16), sem((4,)),
        vmem((512, 512), bf16), vmem((512, 512), bf16),
        vmem((512, 384), bf16), vmem((512, 384), bf16),
        vmem((512, 384), bf16), vmem((512, 384), bf16),
        vmem((512, 384), bf16),
        vmem((8, 512), f32), vmem((128, 128), i32),
        vmem((128, 1024), bf16), vmem((128, 1024), f32), vmem((128, 128), f32),
        vmem((512, 1024), bf16), vmem((1024, 512), bf16), vmem((512, 1024), bf16),
        vmem((512, 512), f32), vmem((4, 512, 256), f32),
        vmem((4, 512, 128), bf16), vmem((4, 512, 128), bf16),
        vmem((4, 512, 128), bf16), vmem((4, 512, 128), bf16),
        vmem((4, 512, 512), bf16), vmem((4, 512, 512), bf16),
        vmem((512, 512), bf16), vmem((512, 128), f32),
        vmem((512, 256), f32), vmem((512, 256), f32), vmem((512, 256), bf16),
        vmem((4, 8, 512), f32), vmem((128, 512), f32),
        vmem((512, 256), bf16), vmem((512, 256), bf16),
        vmem((4, 512, 128), bf16), vmem((4, 512, 128), f32), vmem((4, 512, 256), bf16),
        vmem((4, 128, 256), bf16),
        vmem((128, 1024), bf16),
        vmem((PIECES, 1024, 256), bf16), vmem((PIECES, 512, 256), bf16),
        vmem((PIECES, 512, 256), bf16), vmem((PIECES, 512, 256), bf16),
        vmem((PIECES, 128, 256), bf16), vmem((PIECES, 128, 256), bf16),
        vmem((3, 128, 1024), bf16), vmem((128, 1024), f32),
        vmem((2, 64, 1024), bf16), vmem((2, 128, 1024), bf16),
        sem((4,)), sem((4,)), sem((2,)), sem((2, 6)), sem, sem, sem, sem, sem, sem,
        sem((6, PIECES)), sem((6, PIECES)), sem((6,)), sem((6,)),
    ]
    spec, free = pl.BlockSpec(memory_space=pltpu.VMEM), pl.BlockSpec(memory_space=pl.ANY)
    pos = packed_pos.reshape(1, ROWS)
    y, dx, ar = pl.pallas_call(
        functools.partial(kernel, n_dp),
        out_shape=[
            jax.ShapeDtypeStruct((ROWS, WIDTH), bf16),
            jax.ShapeDtypeStruct((512, 384), bf16),
            jax.ShapeDtypeStruct((PIECES, 1024, 256), bf16),
        ],
        in_specs=[free, free, spec, spec, free, free],
        out_specs=[spec] * 3,
        scratch_shapes=scratch,
        compiler_params=pltpu.CompilerParams(
            collective_id=0, has_side_effects=True, vmem_limit_bytes=60 * 1024 * 1024
        ),
        cost_estimate=pl.CostEstimate(flops=6 * 10**9, bytes_accessed=12 * 10**6, transcendentals=3 * 10**6),
    )(tokens, cotangent, pos, segment_ids, w_proj, w_out)
    scale = (ROWS * 4 * n_dp) ** (-0.5)
    return pl.pallas_call(
        functools.partial(last, scale),
        grid=(4,),
        out_shape=[
            jax.ShapeDtypeStruct((ROWS, WIDTH), bf16),
            jax.ShapeDtypeStruct((ROWS, WIDTH), bf16),
            jax.ShapeDtypeStruct((1024, 4, 256), f32),
            jax.ShapeDtypeStruct((256, WIDTH), f32),
        ],
        in_specs=[
            pl.BlockSpec((32, WIDTH), lambda i: (i, 0)),
            pl.BlockSpec((512, 384), lambda i: (0, 0)),
            pl.BlockSpec((1, ROWS), lambda i: (0, 0)),
            pl.BlockSpec((PIECES, 256, 256), lambda i: (0, i, 0)),
        ],
        out_specs=[
            pl.BlockSpec((32, WIDTH), lambda i: (i, 0)),
            pl.BlockSpec((ROWS, 256), lambda i: (0, i)),
            pl.BlockSpec((256, 4, 256), lambda i: (i, 0, 0)),
            pl.BlockSpec((256, 256), lambda i: (0, i)),
        ],
        compiler_params=pltpu.CompilerParams(vmem_limit_bytes=60 * 1024 * 1024),
        cost_estimate=pl.CostEstimate(flops=10**8, bytes_accessed=10 * 10**6, transcendentals=0),
    )(y, dx, pos, ar)


def solution(mesh):
    return jax.shard_map(
        shards,
        mesh=mesh,
        in_specs=(
            P(("dp", "ctx"), None),
            P(("dp", "ctx"), None),
            P(("dp", "ctx")),
            P("dp", None),
            P(None, "ctx", None),
            P(),
        ),
        out_specs=(
            P(("dp", "ctx"), None),
            P(("dp", "ctx"), None),
            P(None, "ctx", None),
            P("ctx", None),
        ),
        check_vma=False,
    )
```

```python
import functools
import jax
import jax.numpy as jnp
from jax import lax
from jax.experimental import pallas as pl
from jax.experimental.pallas import tpu as pltpu
from jax.sharding import PartitionSpec as P

EPS = 1e-05
MESH = pl.DeviceIdType.MESH
bf16, f32, i32 = jnp.bfloat16, jnp.float32, jnp.int32
ROWS, WIDTH, GROUP, SLOTS = 128, 1024, 512, 16
CAP = 6
COMBOS = [(L, c) for L in range(3) for c in range(8) if c * CAP < 16 * L + 16 and c * CAP + CAP > 16 * L]
PIECES = 5


def dot(a, b):
    return lax.dot_general(a, b, (((1,), (0,)), ((), ())), preferred_element_type=f32)


def dot_nt(a, b):
    return lax.dot_general(a, b, (((1,), (1,)), ((), ())), preferred_element_type=f32)


def dot_tn(a, b):
    return lax.dot_general(a, b, (((0,), (0,)), ((), ())), preferred_element_type=f32)


def sigmoid(t):
    return 0.5 * jnp.tanh(0.5 * t) + 0.5


def iota(shape, axis):
    return lax.broadcasted_iota(i32, shape, axis)


def one(cond):
    return jnp.where(cond, 1.0, 0.0).astype(bf16)


def chunk(c):
    return pl.ds(c * 128, 128)


def kernel(
    n_dp,
    tok_h, cot_h, pos_ref, seg_ref, w_h, wo_h,
    y_hbm, recv_d, ar_hbm,
    y_out, ar_f, out_s,
    tok, cot, w_raw, w, wo, in_s,
    send_x, recv_x, send_g, recv_g, send_y, recv_y, send_d,
    meta_t, rank_s, xp, xhat, rstd_ref, nrm, nrm_t, gbuf,
    msk, slope, uv, qk, kq, qz, p_ref, sl_ref, ds_ref, dq_ref,
    attn_ref, u_ref, dg_ref, st_all, cmb, gated, gfull, dout, du_ref, dpre, dg_send,
    yd, ar_src, ar_c, ar_h, ar_r, ar_q, ar_b, rs_send, rs_own, rs1, rs2,
    a2a_s, a2a_r, ag_s, ag_r, st_s, st_r, gt_s, gt_r, dg_s, dg_r, ar_ss, ar_rs, rs_s, rs_r,
):
    me, cx = lax.axis_index("dp"), lax.axis_index("ctx")
    core, chip = lax.rem(me, 2), lax.div(me, 2)
    other = 1 - core
    right, left, opp = lax.rem(cx + 1, 4), lax.rem(cx + 3, 4), lax.rem(cx + 2, 4)
    sends, flight = [], {}

    def rc(src, dst, ss, rs, dev):
        return pltpu.make_async_remote_copy(
            src_ref=src, dst_ref=dst, send_sem=ss, recv_sem=rs, device_id=dev, device_id_type=MESH
        )

    def wait_bytes(ref, ss, rs):
        return rc(ref, ref, ss, rs, {"ctx": right})

    def arrive(*keys):
        for key in keys:
            flight.pop(key)()

    def al(i, m):
        return pl.multiple_of(i * m, m)

    loads = [pltpu.make_async_copy(a, b, in_s.at[i]) for i, (a, b) in enumerate([(tok_h, tok), (cot_h, cot), (w_h, w_raw), (wo_h, wo)])]
    for c in loads:
        c.start()

    bar = pltpu.get_barrier_semaphore()

    @pl.loop(1, n_dp)
    def _(o):
        pl.semaphore_signal(bar, inc=1, device_id={"dp": lax.rem(me + o, n_dp)}, device_id_type=MESH)

    for o in range(1, 4):
        pl.semaphore_signal(bar, inc=1, device_id={"ctx": lax.rem(cx + o, 4)}, device_id_type=MESH)

    pos_l = jnp.broadcast_to(pos_ref[...], (ROWS, ROWS))
    pos_s = jnp.transpose(pos_l.astype(f32)).astype(i32)
    tgt_l, tgt_s = lax.shift_right_logical(pos_l, 9), lax.shift_right_logical(pos_s, 9)
    ii, jj = iota((ROWS, ROWS), 0), iota((ROWS, ROWS), 1)
    same = tgt_l == tgt_s
    rank_l = jnp.sum(jnp.where(same & (ii < jj), 1.0, 0.0), axis=0, keepdims=True).astype(i32)
    rank_c = jnp.sum(jnp.where(same & (jj < ii), 1.0, 0.0), axis=1, keepdims=True).astype(i32)
    tgt_row = tgt_l[:1] * SLOTS
    rank_s[...] = jnp.where(jj == 0, rank_c, tgt_s * SLOTS)
    row_no = (pos_s & (ROWS - 1)) + 1

    def pack_out(src, dst, with_meta):
        @pl.loop(0, 4)
        def _(rb):
            rows = pl.ds(al(rb, 128), 128)
            here = iota((128, ROWS), 0) + rb * 128
            meta = jnp.zeros((128, 128), f32)
            for L in range(3):
                acc = jnp.zeros((128, 128), f32)
                every = jnp.zeros((128, 128), f32)
                for c in [c for (l, c) in COMBOS if l == L]:
                    v = rank_l + (c * CAP - 16 * L)
                    idx = jnp.where((v >= 0) & (v < 16), tgt_row + v, -1)
                    hit = jnp.where(here == idx, 1.0, 0.0)
                    acc = acc + dot(hit.astype(bf16), src[:, c * 128:c * 128 + 128])
                    every = every + hit
                dst[rows, L * 128:L * 128 + 128] = acc.astype(bf16)
                if with_meta:
                    meta = meta + dot(every.astype(bf16), jnp.where(jj == L, row_no, 0).astype(f32).astype(bf16))
            if with_meta:
                dst[rows, 384:512] = meta.astype(bf16)

    def a2a_start(k, src, dst):
        mine = pl.ds(al(me, SLOTS), SLOTS)
        dst[mine, :] = src[mine, :]

        @pl.loop(1, n_dp)
        def _(o):
            t = lax.rem(me + o, n_dp)
            rc(src.at[pl.ds(al(t, SLOTS), SLOTS)], dst.at[mine], a2a_s.at[k], a2a_r.at[k], {"dp": t}).start()

        part = src.at[pl.ds(0, (n_dp - 1) * SLOTS)]
        sends.append(lambda: wait_bytes(part, a2a_s.at[k], a2a_r.at[k]).wait_send())
        come = dst.at[pl.ds(0, (n_dp - 1) * SLOTS)]
        flight["a2a", k] = lambda: wait_bytes(come, a2a_s.at[k], a2a_r.at[k]).wait_recv()

    def unpack_arrived(src, dst, rows):
        unit = iota((ROWS, 512), 1) & 15
        for c in range(8):
            acc = jnp.zeros((ROWS, 128), f32)
            for L in [l for (l, d) in COMBOS if d == c]:
                lo = c * CAP - 16 * L
                hit = (meta_t[L:L + 1, :] == (iota((ROWS, 512), 0) + 1).astype(f32)) & (unit >= lo) & (unit < lo + CAP)
                acc = acc + dot(one(hit), src[:, L * 128:L * 128 + 128])
            dst[rows, c * 128:c * 128 + 128] = acc.astype(bf16)

    def pack_back(src, dst):
        @pl.loop(0, 4)
        def _(rb):
            rows = pl.ds(al(rb, 128), 128)
            meta = recv_x[rows, 384:512].astype(f32)
            unit = iota((128, ROWS), 0) & 15
            lane = (iota((128, ROWS), 1) + 1).astype(f32)
            for L in range(3):
                acc = jnp.zeros((128, 128), f32)
                mine = meta[:, L:L + 1] == lane
                for c in [c for (l, c) in COMBOS if l == L]:
                    lo = c * CAP - 16 * L
                    acc = acc + dot(one(mine & (unit >= lo) & (unit < lo + CAP)), src[:, c * 128:c * 128 + 128])
                dst[rows, L * 128:L * 128 + 128] = acc.astype(bf16)

    def unpack_home(src, dst):
        rank, base = rank_s[:, 0:1], rank_s[:, 1:2]
        lanes = iota((ROWS, 512), 1)
        for c in range(8):
            acc = jnp.zeros((ROWS, 128), f32)
            for L in [l for (l, d) in COMBOS if d == c]:
                v = rank + (c * CAP - 16 * L)
                idx = jnp.where((v >= 0) & (v < 16), base + v, -1)
                acc = acc + dot(one(lanes == idx), src[:, L * 128:L * 128 + 128])
            dst[:, c * 128:c * 128 + 128] = acc.astype(bf16)

    def finish():
        for f in sends:
            f()

    loads[0].wait()
    pack_out(tok, send_x, True)
    pl.semaphore_wait(bar, n_dp - 1 + 3)
    a2a_start(0, send_x, recv_x)
    loads[1].wait()
    pack_out(cot, send_g, False)
    a2a_start(1, send_g, recv_g)

    seg_row = seg_ref[...]
    seg_col = jnp.transpose(jnp.broadcast_to(seg_row.astype(f32), (128, GROUP))).astype(i32)
    for b in range(4):
        sc = seg_col[b * 128:b * 128 + 128, 0:1]
        ok = (sc == seg_row) & (iota((128, GROUP), 1) <= iota((128, GROUP), 0) + b * 128)
        msk[b * 128:b * 128 + 128, :] = jnp.where(ok, 1.0, 0.0)
    cmb[...] = jnp.zeros_like(cmb)

    own = pl.ds(al(cx, 128), 128)
    loads[2].wait()

    @pl.loop(0, 16)
    def _(i):
        rows = pl.ds(al(i, 64), 64)
        w[:, rows, :] = jnp.swapaxes(w_raw[rows].astype(f32), 0, 1).astype(bf16)

    loads[3].wait()
    arrive(("a2a", 0))
    meta_t[...] = jnp.transpose(recv_x[:, 384:512].astype(f32))[:8]
    unpack_arrived(recv_x, xp, pl.ds(0, 128))
    xf = xp[...].astype(f32)
    mean = jnp.mean(xf, axis=1, keepdims=True)
    rstd = lax.rsqrt(jnp.mean((xf - mean) ** 2, axis=1, keepdims=True) + EPS)
    xh = (xf - mean) * rstd
    xhat[...] = xh
    rstd_ref[...] = jnp.broadcast_to(rstd, (ROWS, 128))
    nrm[own, :] = xh.astype(bf16)

    def half(b, k):
        return pl.ds(pl.multiple_of(b * 128 + k * 64, 64), 64)

    def ag(k, buf):
        def to(block, h, way, slot):
            ref = buf.at[half(block, h)]
            return rc(ref, ref, ag_s.at[k], ag_r.at[k, slot], {"ctx": way})

        def go(block, h, way, slot, source):
            to(block, h, way, slot).start()
            sends.append(to(block, h, way, slot).wait_send)
            flight["ag", k, slot] = to(source, h, way, slot).wait_recv

        def start():
            go(cx, 0, right, 0, left)
            go(cx, 1, left, 1, right)
            go(cx, 1, right, 2, left)
            go(cx, 0, left, 3, right)

        def forward():
            arrive(("ag", k, 0))
            go(left, 0, right, 4, opp)
            arrive(("ag", k, 1))
            go(right, 1, left, 5, opp)

        def near():
            arrive(("ag", k, 2), ("ag", k, 3))

        def far():
            arrive(("ag", k, 4), ("ag", k, 5))

        return start, forward, near, far

    lane_lo = iota((128, 128), 1) < 64

    def project(block):
        rows = pl.ds(al(block, 128), 128)
        for h in range(4):
            pre = dot(nrm[rows, :], w[h])
            sig = sigmoid(pre)
            act = pre * sig
            slope[h, rows, :] = sig + act * (1.0 - sig)
            uv[h, rows, :] = act[:, :128].astype(bf16)
            b = act[:, 128:].astype(bf16)
            qk[h, rows, :] = b
            bf = b.astype(f32)
            kq[h, rows, :] = pltpu.roll(bf, 64, 1).astype(bf16)
            qz[h, rows, :] = jnp.where(lane_lo, bf * 0.0625, 0.0).astype(bf16)

    def turn():
        for b in range(4):
            nrm_t[:, b * 128:b * 128 + 128] = jnp.transpose(nrm[b * 128:b * 128 + 128, :].astype(f32)).astype(bf16)

    n_start, n_forward, n_near, n_far = ag(0, nrm)
    g_start, g_forward, g_near, g_far = ag(1, gbuf)
    n_start()
    arrive(("a2a", 1))
    unpack_arrived(recv_g, gbuf, own)
    n_forward()
    for t in range(4):
        dg_send[t] = dot_nt(gbuf[own, :], wo[t * 256:t * 256 + 256, :]).astype(bf16)
    for o in (2, 1, 3):
        t = lax.rem(cx + o, 4)
        rc(dg_send.at[t], dg_ref.at[own], dg_s, dg_r, {"ctx": t}).start()
    sends.append(lambda: wait_bytes(dg_ref.at[pl.ds(0, 384)], dg_s, dg_r).wait_send())
    flight["dg"] = lambda: wait_bytes(dg_ref.at[pl.ds(0, 384)], dg_s, dg_r).wait_recv()
    dg_ref[own, :] = dg_send[cx]
    project(cx)
    n_near()
    project(left)
    project(right)
    n_far()
    g_start()
    project(opp)

    for j in range(2):
        for half_j in range(2):
            h = 2 * j + half_j
            for b in range(4):
                r, n = slice(b * 128, b * 128 + 128), (b + 1) * 128
                t = dot_nt(qz[h, r, :], kq[h, :n, :])
                th = jnp.tanh(t)
                m = msk[r, :n]
                up = 1.0 + th
                pw = t * up
                p = (pw * m).astype(bf16)
                p_ref[h, r, :n] = p
                sl_ref[h, r, :n] = ((up + pw * (1.0 - th)) * m).astype(bf16)
                pv = dot(p, uv[h, :n, :]).astype(bf16).astype(f32)
                u_here = uv[h, r, :].astype(f32)
                if half_j == 0:
                    attn_ref[r, j * 128:j * 128 + 128] = pltpu.roll(pv, 64, 1)
                    u_ref[r, j * 128:j * 128 + 128] = u_here
                else:
                    attn_ref[r, j * 128:j * 128 + 128] = jnp.where(lane_lo, attn_ref[r, j * 128:j * 128 + 128], pv)
                    u_ref[r, j * 128:j * 128 + 128] = jnp.where(
                        lane_lo, u_ref[r, j * 128:j * 128 + 128], pltpu.roll(u_here, 64, 1)
                    )

    arrive("dg")

    @pl.loop(0, 4)
    def _(b):
        r = pl.ds(al(b, 128), 128)
        dg = dg_ref[r, :].astype(f32)
        a = attn_ref[r, :]
        m = jnp.mean(a, axis=1, keepdims=True)
        ac = a - m
        e = dg * u_ref[r, :]
        lane = iota((128, 128), 1)
        st = jnp.where(lane == 0, m, jnp.sum(ac * ac, axis=1, keepdims=True))
        st = jnp.where(lane == 2, jnp.sum(e, axis=1, keepdims=True), st)
        st = jnp.where(lane == 3, jnp.sum(e * ac, axis=1, keepdims=True), st)
        st_all[cx, :, pl.ds(al(b, 128), 128)] = jnp.transpose(st)[:8]

    for o in range(1, 4):
        rc(st_all.at[cx], st_all.at[cx], st_s, st_r, {"ctx": lax.rem(cx + o, 4)}).start()
    sends.append(lambda: wait_bytes(st_all.at[pl.ds(0, 3)], st_s, st_r).wait_send())
    flight["st"] = lambda: wait_bytes(st_all.at[pl.ds(0, 3)], st_s, st_r).wait_recv()
    turn()
    arrive("st")
    g_forward()
    ms = [st_all[l, 0:1, :] for l in range(4)]
    m2 = (ms[0] + ms[1] + ms[2] + ms[3]) * 0.25
    sq, se, seo = 0.0, 0.0, 0.0
    for l in range(4):
        d = ms[l] - m2
        sq = sq + st_all[l, 1:2, :] + 256.0 * d * d
        se = se + st_all[l, 2:3, :]
        seo = seo + st_all[l, 3:4, :] + d * st_all[l, 2:3, :]
    r2 = lax.rsqrt(sq * (1.0 / WIDTH) + EPS)
    cmb[0:1, :] = m2
    cmb[1:2, :] = r2
    cmb[2:3, :] = se * (1.0 / WIDTH)
    cmb[3:4, :] = r2 * seo * (1.0 / WIDTH)

    for b in range(4):
        r = slice(b * 128, b * 128 + 128)
        tr = jnp.transpose(cmb[:, r])
        r2c = tr[:, 1:2]
        onorm = (attn_ref[r, :] - tr[:, 0:1]) * r2c
        u, dg = u_ref[r, :], dg_ref[r, :].astype(f32)
        gated[r, :] = (onorm * u).astype(bf16)
        du = (dg * onorm).astype(bf16).astype(f32)
        da = r2c * (dg * u - tr[:, 2:3] - onorm * tr[:, 3:4])
        for j in range(2):
            s = slice(j * 128, j * 128 + 128)
            dout[2 * j, r, :] = jnp.where(lane_lo, 0.0, pltpu.roll(da[:, s], 64, 1)).astype(bf16)
            dout[2 * j + 1, r, :] = jnp.where(lane_lo, 0.0, da[:, s]).astype(bf16)
            du_ref[2 * j, r, :] = du[:, s]
            du_ref[2 * j + 1, r, :] = pltpu.roll(du[:, s], 64, 1)

    for o in (2, 1, 3):
        t = lax.rem(cx + o, 4)
        rc(gated.at[pl.ds(al(t, 128), 128)], gfull.at[own], gt_s, gt_r, {"ctx": t}).start()
    sends.append(lambda: wait_bytes(gated.at[pl.ds(0, 384)], gt_s, gt_r).wait_send())
    flight["gt"] = lambda: wait_bytes(gfull.at[pl.ds(0, 384)], gt_s, gt_r).wait_recv()
    gfull[own, :] = gated[own, :]

    yy, zz = lax.div(chip, 4), lax.rem(chip, 4)
    base = core * 512

    def rows_at(start, count):
        return pl.ds(pl.multiple_of(start, count), count)

    def peer(axis, o):
        y2, z2 = (yy, lax.rem(zz + o, 4)) if axis == 0 else (lax.rem(yy + o, 4), zz)
        return lax.rem((zz if axis == 0 else yy) + o, 4), {"dp": (y2 * 4 + z2) * 2 + core}

    def ours(part):
        return (zz, yy) if part == 0 else (yy, zz)

    def begun(stage, p, ref):
        sends.append(lambda: wait_bytes(ref, ar_ss.at[stage, p], ar_rs.at[stage, p]).wait_send())
        flight["ar", stage, p] = lambda: wait_bytes(ref, ar_ss.at[stage, p], ar_rs.at[stage, p]).wait_recv()

    def to_core(stage, p, src, dst):
        rc(src, dst, ar_ss.at[stage, p], ar_rs.at[stage, p], {"dp": chip * 2 + other}).start()
        begun(stage, p, dst)

    def to_axis(stage, p, places, ref):
        @pl.loop(1, 4)
        def _(o):
            for part in range(2):
                axis = part if stage in (1, 4) else 1 - part
                t, dev = peer(axis, o)
                src, dst = places(part, t)
                rc(src, dst, ar_ss.at[stage, p], ar_rs.at[stage, p], dev).start()

        begun(stage, p, ref)

    def ar1(p):
        to_core(0, p, ar_src.at[p, rows_at(other * 512, 512)], ar_c.at[p])

    def ar2(p):
        arrive(("ar", 0, p))

        @pl.loop(0, 4)
        def _(b):
            r = rows_at(b * 128, 128)
            a = ar_src[p, rows_at(base + b * 128, 128), :].astype(f32)
            ar_h[p, r, :] = (a + ar_c[p, r, :].astype(f32)).astype(bf16)

        for part in range(2):
            mine = rows_at(part * 256 + ours(part)[0] * 64, 64)
            ar_r[p, mine, :] = ar_h[p, mine, :]

        def places(part, t):
            return (
                ar_h.at[p, rows_at(part * 256 + t * 64, 64)],
                ar_r.at[p, rows_at(part * 256 + ours(part)[0] * 64, 64)],
            )

        to_axis(1, p, places, ar_r.at[p, pl.ds(0, 384)])

    def ar3(p):
        arrive(("ar", 1, p))
        for part in range(2):
            acc = jnp.zeros((64, 256), f32)
            for k in range(4):
                acc = acc + ar_r[p, part * 256 + k * 64:part * 256 + k * 64 + 64, :].astype(f32)
            ar_q[p, part * 64:part * 64 + 64, :] = acc.astype(bf16)
            mine = rows_at(part * 64 + ours(part)[1] * 16, 16)
            ar_b[p, mine, :] = ar_q[p, mine, :]

        def places(part, t):
            return ar_q.at[p, rows_at(part * 64 + t * 16, 16)], ar_b.at[p, rows_at(part * 64 + ours(part)[1] * 16, 16)]

        to_axis(2, p, places, ar_b.at[p, pl.ds(0, 96)])

    def ar4(p):
        arrive(("ar", 2, p))
        for part in range(2):
            acc = jnp.zeros((16, 256), f32)
            for k in range(4):
                acc = acc + ar_b[p, part * 64 + k * 16:part * 64 + k * 16 + 16, :].astype(f32)
            first, second = ours(part)
            ar_f[p, rows_at(base + part * 256 + first * 64 + second * 16, 16), :] = acc.astype(bf16)

        def places(part, t):
            first, second = ours(part)
            ref = ar_f.at[p, rows_at(base + part * 256 + first * 64 + second * 16, 16)]
            return ref, ref

        to_axis(3, p, places, ar_f.at[p, pl.ds(0, 96)])

    def ar5(p):
        arrive(("ar", 3, p))

        def places(part, t):
            ref = ar_f.at[p, rows_at(base + part * 256 + ours(part)[0] * 64, 64)]
            return ref, ref

        to_axis(4, p, places, ar_f.at[p, pl.ds(0, 384)])

    def ar6(p):
        arrive(("ar", 4, p))
        ref = ar_f.at[p, rows_at(base, 512)]
        to_core(5, p, ref, ref)

    stores = []

    def ar7(p):
        arrive(("ar", 5, p))
        stores.append(pltpu.make_async_copy(ar_f.at[p], ar_hbm.at[p], out_s.at[p]))
        stores[-1].start()

    def backward(h):
        for b in range(4):
            r, n = slice(b * 128, b * 128 + 128), (b + 1) * 128
            dw = dot_nt(dout[h, r, :], uv[h, :n, :])
            ds = (dw * sl_ref[h, r, :n].astype(f32)).astype(bf16)
            ds_ref[r, :n] = ds
            dq_ref[r, :] = dot(ds, qk[h, :n, :])
        for b in range(4):
            r, c = slice(b * 128, b * 128 + 128), slice(b * 128, 512)
            dv = dot_tn(p_ref[h, c, r], dout[h, c, :])
            dk = dot_tn(ds_ref[c, r], qk[h, c, :])
            d1 = jnp.where(lane_lo, du_ref[h, r, :], dv)
            d2 = pltpu.roll(jnp.where(lane_lo, dk, dq_ref[r, :]), 64, 1) * 0.0625
            dpre[h, r, 0:128] = (d1 * slope[h, r, 0:128]).astype(bf16)
            dpre[h, r, 128:256] = (d2 * slope[h, r, 128:256]).astype(bf16)

    def piece(h):
        for q in range(4):
            acc = dot(nrm_t[q * 256:q * 256 + 256, :], dpre[h])
            ar_src[h + 1, q * 256:q * 256 + 256, :] = acc.astype(bf16)
        ar1(h + 1)

    def dnorm(block, dst):
        rows = pl.ds(al(block, 128), 128)

        for cb in range(4):
            s = slice(cb * 256, cb * 256 + 256)
            acc = dot_nt(dpre[0, rows, :], w[0, s, :])
            for h in range(1, 4):
                acc = acc + dot_nt(dpre[h, rows, :], w[h, s, :])
            dst[:, s] = acc.astype(dst.dtype)

    lo, hi = pl.ds(0, 64), pl.ds(64, 64)

    def rs_go(src, dst, k, way):
        c = rc(src, dst, rs_s.at[k], rs_r.at[k], {"ctx": way})
        c.start()
        sends.append(c.wait_send)
        flight["rs", k] = c.wait_recv

    backward(0)
    piece(0)
    backward(1)
    ar2(1)
    piece(1)
    backward(2)
    ar2(2)
    piece(2)
    ar3(1)
    backward(3)

    to_far, to_right, to_left = rs_send.at[0], rs_send.at[1], rs_send.at[2]
    dnorm(opp, to_far)
    rs_go(to_far.at[lo], rs1.at[0], 0, right)
    rs_go(to_far.at[hi], rs1.at[1], 1, left)
    dnorm(right, to_right)
    rs_go(to_right.at[hi], rs2.at[0, hi], 2, right)
    dnorm(left, to_left)
    rs_go(to_left.at[lo], rs2.at[1, lo], 3, left)
    piece(3)
    ar2(3)
    ar3(2)
    ar4(1)
    arrive(("rs", 0))
    to_right[lo, :] = (to_right[lo, :].astype(f32) + rs1[0].astype(f32)).astype(bf16)
    rs_go(to_right.at[lo], rs2.at[0, lo], 4, right)
    arrive(("rs", 1))
    to_left[hi, :] = (to_left[hi, :].astype(f32) + rs1[1].astype(f32)).astype(bf16)
    rs_go(to_left.at[hi], rs2.at[1, hi], 5, left)
    g_near()
    g_far()
    for cb in range(4):
        ar_src[0, cb * 256:cb * 256 + 256, :] = dot_tn(gated[...], gbuf[:, cb * 256:cb * 256 + 256]).astype(bf16)
    ar1(0)
    ar2(4)
    ar3(3)
    ar4(2)
    ar5(1)
    arrive("gt")
    for cb in range(4):
        s = slice(cb * 256, cb * 256 + 256)
        acc = xp[:, s].astype(f32)
        for c in range(4):
            acc = acc + dot(gfull[c * 128:c * 128 + 128, :], wo[c * 256:c * 256 + 256, s])
        yd[:, s] = acc.astype(bf16)
    pack_back(yd, send_y)
    a2a_start(2, send_y, recv_y)

    ar2(0)
    ar3(4)
    ar4(3)
    ar5(2)
    ar6(1)
    dnorm(cx, rs_own)
    ar3(0)
    ar4(4)
    ar5(3)
    ar6(2)
    arrive(("rs", 2), ("rs", 3), ("rs", 4), ("rs", 5))
    dn = rs_own[...] + rs2[0].astype(f32) + rs2[1].astype(f32)
    xh2 = xhat[...]
    mean_d = jnp.mean(dn, axis=1, keepdims=True)
    mean_dx = jnp.mean(dn * xh2, axis=1, keepdims=True)
    dx = gbuf[own, :].astype(f32) + rstd_ref[:, 0:1] * (dn - mean_d - xh2 * mean_dx)
    yd[...] = dx.astype(bf16)
    pack_back(yd, send_d)
    a2a_start(3, send_d, recv_d)
    ar4(0)
    ar5(4)
    ar6(3)
    ar7(1)
    ar7(2)
    arrive(("a2a", 2))
    unpack_home(recv_y, y_out)
    stores.append(pltpu.make_async_copy(y_out, y_hbm, out_s.at[PIECES]))
    stores[-1].start()
    ar5(0)
    ar6(4)
    ar7(3)
    ar6(0)
    ar7(4)
    ar7(0)
    arrive(("a2a", 3))
    for c in stores:
        c.wait()
    finish()


def last(scale, y, recv, pos_ref, ar, y_out, dx_out, proj, out):
    i = pl.program_id(0)
    y_out[...] = y[...]
    pos_l = jnp.broadcast_to(pos_ref[...], (ROWS, ROWS))
    pos_s = jnp.transpose(pos_l.astype(f32)).astype(i32)
    tgt_l, tgt_s = lax.shift_right_logical(pos_l, 9), lax.shift_right_logical(pos_s, 9)
    before = (tgt_l == tgt_s) & (iota((ROWS, ROWS), 1) < iota((ROWS, ROWS), 0))
    rank = jnp.sum(jnp.where(before, 1.0, 0.0), axis=1, keepdims=True).astype(i32)
    base = tgt_s[:, 0:1] * SLOTS
    lanes = iota((ROWS, 512), 1)
    for k in range(2):
        acc = jnp.zeros((ROWS, 128), f32)
        for L in range(3):
            v = rank + ((2 * i + k) * CAP - 16 * L)
            idx = jnp.where((v >= 0) & (v < 16), base + v, -1)
            acc = acc + dot(one(lanes == idx), recv[:, L * 128:L * 128 + 128])
        dx_out[:, k * 128:k * 128 + 128] = acc.astype(bf16)
    out[...] = ar[0].astype(f32) * scale
    for q in range(8):
        r = slice(q * 32, q * 32 + 32)
        proj[r] = jnp.swapaxes(ar[1:, r, :].astype(f32) * scale, 0, 1)


def shards(tokens, cotangent, packed_pos, segment_ids, w_proj, w_out):
    n_dp = lax.axis_size("dp")
    vmem, sem = pltpu.VMEM, pltpu.SemaphoreType.DMA
    scratch = [
        vmem((128, 1024), bf16), vmem((PIECES, 1024, 256), bf16), sem((PIECES + 1,)),
        vmem((128, 1024), bf16), vmem((128, 1024), bf16), vmem((1024, 4, 256), bf16), vmem((4, 1024, 256), bf16),
        vmem((1024, 1024), bf16), sem((4,)),
        vmem((512, 512), bf16), vmem((512, 512), bf16),
        vmem((512, 384), bf16), vmem((512, 384), bf16),
        vmem((512, 384), bf16), vmem((512, 384), bf16),
        vmem((512, 384), bf16),
        vmem((8, 512), f32), vmem((128, 128), i32),
        vmem((128, 1024), bf16), vmem((128, 1024), f32), vmem((128, 128), f32),
        vmem((512, 1024), bf16), vmem((1024, 512), bf16), vmem((512, 1024), bf16),
        vmem((512, 512), f32), vmem((4, 512, 256), f32),
        vmem((4, 512, 128), bf16), vmem((4, 512, 128), bf16),
        vmem((4, 512, 128), bf16), vmem((4, 512, 128), bf16),
        vmem((4, 512, 512), bf16), vmem((4, 512, 512), bf16),
        vmem((512, 512), bf16), vmem((512, 128), f32),
        vmem((512, 256), f32), vmem((512, 256), f32), vmem((512, 256), bf16),
        vmem((4, 8, 512), f32), vmem((128, 512), f32),
        vmem((512, 256), bf16), vmem((512, 256), bf16),
        vmem((4, 512, 128), bf16), vmem((4, 512, 128), f32), vmem((4, 512, 256), bf16),
        vmem((4, 128, 256), bf16),
        vmem((128, 1024), bf16),
        vmem((PIECES, 1024, 256), bf16), vmem((PIECES, 512, 256), bf16),
        vmem((PIECES, 512, 256), bf16), vmem((PIECES, 512, 256), bf16),
        vmem((PIECES, 128, 256), bf16), vmem((PIECES, 128, 256), bf16),
        vmem((3, 128, 1024), bf16), vmem((128, 1024), f32),
        vmem((2, 64, 1024), bf16), vmem((2, 128, 1024), bf16),
        sem((4,)), sem((4,)), sem((2,)), sem((2, 6)), sem, sem, sem, sem, sem, sem,
        sem((6, PIECES)), sem((6, PIECES)), sem((6,)), sem((6,)),
    ]
    spec, free = pl.BlockSpec(memory_space=pltpu.VMEM), pl.BlockSpec(memory_space=pl.ANY)
    pos = packed_pos.reshape(1, ROWS)
    y, dx, ar = pl.pallas_call(
        functools.partial(kernel, n_dp),
        out_shape=[
            jax.ShapeDtypeStruct((ROWS, WIDTH), bf16),
            jax.ShapeDtypeStruct((512, 384), bf16),
            jax.ShapeDtypeStruct((PIECES, 1024, 256), bf16),
        ],
        in_specs=[free, free, spec, spec, free, free],
        out_specs=[free, spec, free],
        scratch_shapes=scratch,
        compiler_params=pltpu.CompilerParams(
            collective_id=0, has_side_effects=True, vmem_limit_bytes=44 * 1024 * 1024
        ),
        cost_estimate=pl.CostEstimate(flops=6 * 10**9, bytes_accessed=12 * 10**6, transcendentals=3 * 10**6),
    )(tokens, cotangent, pos, segment_ids, w_proj, w_out)
    scale = (ROWS * 4 * n_dp) ** (-0.5)
    return pl.pallas_call(
        functools.partial(last, scale),
        grid=(4,),
        out_shape=[
            jax.ShapeDtypeStruct((ROWS, WIDTH), bf16),
            jax.ShapeDtypeStruct((ROWS, WIDTH), bf16),
            jax.ShapeDtypeStruct((1024, 4, 256), f32),
            jax.ShapeDtypeStruct((256, WIDTH), f32),
        ],
        in_specs=[
            pl.BlockSpec((32, WIDTH), lambda i: (i, 0)),
            pl.BlockSpec((512, 384), lambda i: (0, 0)),
            pl.BlockSpec((1, ROWS), lambda i: (0, 0)),
            pl.BlockSpec((PIECES, 256, 256), lambda i: (0, i, 0)),
        ],
        out_specs=[
            pl.BlockSpec((32, WIDTH), lambda i: (i, 0)),
            pl.BlockSpec((ROWS, 256), lambda i: (0, i)),
            pl.BlockSpec((256, 4, 256), lambda i: (i, 0, 0)),
            pl.BlockSpec((256, 256), lambda i: (0, i)),
        ],
        compiler_params=pltpu.CompilerParams(vmem_limit_bytes=16 * 1024 * 1024),
        cost_estimate=pl.CostEstimate(flops=10**8, bytes_accessed=10 * 10**6, transcendentals=0),
    )(y, dx, pos, ar)


def solution(mesh):
    return jax.shard_map(
        shards,
        mesh=mesh,
        in_specs=(
            P(("dp", "ctx"), None),
            P(("dp", "ctx"), None),
            P(("dp", "ctx")),
            P("dp", None),
            P(None, "ctx", None),
            P(),
        ),
        out_specs=(
            P(("dp", "ctx"), None),
            P(("dp", "ctx"), None),
            P(None, "ctx", None),
            P("ctx", None),
        ),
        check_vma=False,
    )
```

```python
import functools
import jax
import jax.numpy as jnp
from jax import lax
from jax.experimental import pallas as pl
from jax.experimental.pallas import tpu as pltpu
from jax.sharding import PartitionSpec as P

EPS = 1e-05
MESH = pl.DeviceIdType.MESH
bf16, f32, i32 = jnp.bfloat16, jnp.float32, jnp.int32
ROWS, WIDTH, GROUP, SLOTS = 128, 1024, 512, 16
CAP = 6
COMBOS = [(L, c) for L in range(3) for c in range(8) if c * CAP < 16 * L + 16 and c * CAP + CAP > 16 * L]
PIECES = 5


def dot(a, b):
    return lax.dot_general(a, b, (((1,), (0,)), ((), ())), preferred_element_type=f32)


def dot_nt(a, b):
    return lax.dot_general(a, b, (((1,), (1,)), ((), ())), preferred_element_type=f32)


def dot_tn(a, b):
    return lax.dot_general(a, b, (((0,), (0,)), ((), ())), preferred_element_type=f32)


def sigmoid(t):
    return 0.5 * jnp.tanh(0.5 * t) + 0.5


def iota(shape, axis):
    return lax.broadcasted_iota(i32, shape, axis)


def one(cond):
    return jnp.where(cond, 1.0, 0.0).astype(bf16)


def chunk(c):
    return pl.ds(c * 128, 128)


def kernel(
    n_dp,
    tok_h, cot_h, pos_ref, seg_ref, w_h, wo_h,
    y_hbm, recv_d, ar_hbm,
    y_out, ar_f, out_s,
    tok, cot, w_raw, w, wo, in_s,
    send_x, recv_x, send_g, recv_g, send_y, recv_y, send_d,
    meta_t, rank_s, xp, xhat, rstd_ref, nrm, nrm_t, gbuf,
    msk, slope, uv, qk, kq, qz, p_ref, sl_ref, ds_ref, dq_ref,
    attn_ref, u_ref, dg_ref, st_all, cmb, gated, gfull, dout, du_ref, dpre, dg_send,
    yd, ar_src, ar_c, ar_h, ar_r, ar_q, ar_b, rs_send, rs_own, rs1, rs2,
    a2a_s, a2a_r, ag_s, ag_r, st_s, st_r, gt_s, gt_r, dg_s, dg_r, ar_ss, ar_rs, rs_s, rs_r,
):
    me, cx = lax.axis_index("dp"), lax.axis_index("ctx")
    core, chip = lax.rem(me, 2), lax.div(me, 2)
    other = 1 - core
    right, left, opp = lax.rem(cx + 1, 4), lax.rem(cx + 3, 4), lax.rem(cx + 2, 4)
    sends, flight = [], {}

    def rc(src, dst, ss, rs, dev):
        return pltpu.make_async_remote_copy(
            src_ref=src, dst_ref=dst, send_sem=ss, recv_sem=rs, device_id=dev, device_id_type=MESH
        )

    def wait_bytes(ref, ss, rs):
        return rc(ref, ref, ss, rs, {"ctx": right})

    def arrive(*keys):
        for key in keys:
            flight.pop(key)()

    def al(i, m):
        return pl.multiple_of(i * m, m)

    loads = [pltpu.make_async_copy(a, b, in_s.at[i]) for i, (a, b) in enumerate([(tok_h, tok), (cot_h, cot), (w_h, w_raw), (wo_h, wo)])]
    for c in loads:
        c.start()

    bar = pltpu.get_barrier_semaphore()

    @pl.loop(1, n_dp)
    def _(o):
        pl.semaphore_signal(bar, inc=1, device_id={"dp": lax.rem(me + o, n_dp)}, device_id_type=MESH)

    for o in range(1, 4):
        pl.semaphore_signal(bar, inc=1, device_id={"ctx": lax.rem(cx + o, 4)}, device_id_type=MESH)

    pos_l = jnp.broadcast_to(pos_ref[...], (ROWS, ROWS))
    pos_s = jnp.transpose(pos_l.astype(f32)).astype(i32)
    tgt_l, tgt_s = lax.shift_right_logical(pos_l, 9), lax.shift_right_logical(pos_s, 9)
    ii, jj = iota((ROWS, ROWS), 0), iota((ROWS, ROWS), 1)
    same = tgt_l == tgt_s
    rank_l = jnp.sum(jnp.where(same & (ii < jj), 1.0, 0.0), axis=0, keepdims=True).astype(i32)
    rank_c = jnp.sum(jnp.where(same & (jj < ii), 1.0, 0.0), axis=1, keepdims=True).astype(i32)
    tgt_row = tgt_l[:1] * SLOTS
    rank_s[...] = jnp.where(jj == 0, rank_c, tgt_s * SLOTS)
    row_no = (pos_s & (ROWS - 1)) + 1

    def pack_out(src, dst, with_meta):
        @pl.loop(0, 4)
        def _(rb):
            rows = pl.ds(al(rb, 128), 128)
            here = iota((128, ROWS), 0) + rb * 128
            meta = jnp.zeros((128, 128), f32)
            for L in range(3):
                acc = jnp.zeros((128, 128), f32)
                every = jnp.zeros((128, 128), f32)
                for c in [c for (l, c) in COMBOS if l == L]:
                    v = rank_l + (c * CAP - 16 * L)
                    idx = jnp.where((v >= 0) & (v < 16), tgt_row + v, -1)
                    hit = jnp.where(here == idx, 1.0, 0.0)
                    acc = acc + dot(hit.astype(bf16), src[:, c * 128:c * 128 + 128])
                    every = every + hit
                dst[rows, L * 128:L * 128 + 128] = acc.astype(bf16)
                if with_meta:
                    meta = meta + dot(every.astype(bf16), jnp.where(jj == L, row_no, 0).astype(f32).astype(bf16))
            if with_meta:
                dst[rows, 384:512] = meta.astype(bf16)

    def a2a_start(k, src, dst):
        mine = pl.ds(al(me, SLOTS), SLOTS)
        dst[mine, :] = src[mine, :]

        @pl.loop(1, n_dp)
        def _(o):
            t = lax.rem(me + o, n_dp)
            rc(src.at[pl.ds(al(t, SLOTS), SLOTS)], dst.at[mine], a2a_s.at[k], a2a_r.at[k], {"dp": t}).start()

        part = src.at[pl.ds(0, (n_dp - 1) * SLOTS)]
        sends.append(lambda: wait_bytes(part, a2a_s.at[k], a2a_r.at[k]).wait_send())
        come = dst.at[pl.ds(0, (n_dp - 1) * SLOTS)]
        flight["a2a", k] = lambda: wait_bytes(come, a2a_s.at[k], a2a_r.at[k]).wait_recv()

    def unpack_arrived(src, dst, rows):
        unit = iota((ROWS, 512), 1) & 15
        for c in range(8):
            acc = jnp.zeros((ROWS, 128), f32)
            for L in [l for (l, d) in COMBOS if d == c]:
                lo = c * CAP - 16 * L
                hit = (meta_t[L:L + 1, :] == (iota((ROWS, 512), 0) + 1).astype(f32)) & (unit >= lo) & (unit < lo + CAP)
                acc = acc + dot(one(hit), src[:, L * 128:L * 128 + 128])
            dst[rows, c * 128:c * 128 + 128] = acc.astype(bf16)

    def pack_back(src, dst):
        @pl.loop(0, 4)
        def _(rb):
            rows = pl.ds(al(rb, 128), 128)
            meta = recv_x[rows, 384:512].astype(f32)
            unit = iota((128, ROWS), 0) & 15
            lane = (iota((128, ROWS), 1) + 1).astype(f32)
            for L in range(3):
                acc = jnp.zeros((128, 128), f32)
                mine = meta[:, L:L + 1] == lane
                for c in [c for (l, c) in COMBOS if l == L]:
                    lo = c * CAP - 16 * L
                    acc = acc + dot(one(mine & (unit >= lo) & (unit < lo + CAP)), src[:, c * 128:c * 128 + 128])
                dst[rows, L * 128:L * 128 + 128] = acc.astype(bf16)

    def unpack_home(src, dst):
        rank, base = rank_s[:, 0:1], rank_s[:, 1:2]
        lanes = iota((ROWS, 512), 1)
        for c in range(8):
            acc = jnp.zeros((ROWS, 128), f32)
            for L in [l for (l, d) in COMBOS if d == c]:
                v = rank + (c * CAP - 16 * L)
                idx = jnp.where((v >= 0) & (v < 16), base + v, -1)
                acc = acc + dot(one(lanes == idx), src[:, L * 128:L * 128 + 128])
            dst[:, c * 128:c * 128 + 128] = acc.astype(bf16)

    def finish():
        for f in sends:
            f()

    loads[0].wait()
    pack_out(tok, send_x, True)
    pl.semaphore_wait(bar, n_dp - 1 + 3)
    a2a_start(0, send_x, recv_x)
    loads[1].wait()
    pack_out(cot, send_g, False)
    a2a_start(1, send_g, recv_g)

    seg_row = seg_ref[...]
    seg_col = jnp.transpose(jnp.broadcast_to(seg_row.astype(f32), (128, GROUP))).astype(i32)
    for b in range(4):
        sc = seg_col[b * 128:b * 128 + 128, 0:1]
        ok = (sc == seg_row) & (iota((128, GROUP), 1) <= iota((128, GROUP), 0) + b * 128)
        msk[b * 128:b * 128 + 128, :] = jnp.where(ok, 1.0, 0.0)
    cmb[...] = jnp.zeros_like(cmb)

    own = pl.ds(al(cx, 128), 128)
    loads[2].wait()

    @pl.loop(0, 16)
    def _(i):
        rows = pl.ds(al(i, 64), 64)
        w[:, rows, :] = jnp.swapaxes(w_raw[rows].astype(f32), 0, 1).astype(bf16)

    loads[3].wait()
    arrive(("a2a", 0))
    meta_t[...] = jnp.transpose(recv_x[:, 384:512].astype(f32))[:8]
    unpack_arrived(recv_x, xp, pl.ds(0, 128))
    xf = xp[...].astype(f32)
    mean = jnp.mean(xf, axis=1, keepdims=True)
    rstd = lax.rsqrt(jnp.mean((xf - mean) ** 2, axis=1, keepdims=True) + EPS)
    xh = (xf - mean) * rstd
    xhat[...] = xh
    rstd_ref[...] = jnp.broadcast_to(rstd, (ROWS, 128))
    nrm[own, :] = xh.astype(bf16)

    def half(b, k):
        return pl.ds(pl.multiple_of(b * 128 + k * 64, 64), 64)

    def ag(k, buf):
        def to(block, h, way, slot):
            ref = buf.at[half(block, h)]
            return rc(ref, ref, ag_s.at[k], ag_r.at[k, slot], {"ctx": way})

        def go(block, h, way, slot, source):
            to(block, h, way, slot).start()
            sends.append(to(block, h, way, slot).wait_send)
            flight["ag", k, slot] = to(source, h, way, slot).wait_recv

        def start():
            go(cx, 0, right, 0, left)
            go(cx, 1, left, 1, right)
            go(cx, 1, right, 2, left)
            go(cx, 0, left, 3, right)

        def forward():
            arrive(("ag", k, 0))
            go(left, 0, right, 4, opp)
            arrive(("ag", k, 1))
            go(right, 1, left, 5, opp)

        def near():
            arrive(("ag", k, 2), ("ag", k, 3))

        def far():
            arrive(("ag", k, 4), ("ag", k, 5))

        return start, forward, near, far

    lane_lo = iota((128, 128), 1) < 64

    def project(block):
        rows = pl.ds(al(block, 128), 128)
        for h in range(4):
            pre = dot(nrm[rows, :], w[h])
            sig = sigmoid(pre)
            act = pre * sig
            slope[h, rows, :] = sig + act * (1.0 - sig)
            uv[h, rows, :] = act[:, :128].astype(bf16)
            b = act[:, 128:].astype(bf16)
            qk[h, rows, :] = b
            bf = b.astype(f32)
            kq[h, rows, :] = pltpu.roll(bf, 64, 1).astype(bf16)
            qz[h, rows, :] = jnp.where(lane_lo, bf * 0.0625, 0.0).astype(bf16)

    def turn():
        for b in range(4):
            nrm_t[:, b * 128:b * 128 + 128] = jnp.transpose(nrm[b * 128:b * 128 + 128, :].astype(f32)).astype(bf16)

    n_start, n_forward, n_near, n_far = ag(0, nrm)
    g_start, g_forward, g_near, g_far = ag(1, gbuf)
    n_start()
    arrive(("a2a", 1))
    unpack_arrived(recv_g, gbuf, own)
    n_forward()
    for t in range(4):
        dg_send[t] = dot_nt(gbuf[own, :], wo[t * 256:t * 256 + 256, :]).astype(bf16)
    for o in (2, 1, 3):
        t = lax.rem(cx + o, 4)
        rc(dg_send.at[t], dg_ref.at[own], dg_s, dg_r, {"ctx": t}).start()
    sends.append(lambda: wait_bytes(dg_ref.at[pl.ds(0, 384)], dg_s, dg_r).wait_send())
    flight["dg"] = lambda: wait_bytes(dg_ref.at[pl.ds(0, 384)], dg_s, dg_r).wait_recv()
    dg_ref[own, :] = dg_send[cx]
    project(cx)
    n_near()
    project(left)
    project(right)
    n_far()
    g_start()
    project(opp)

    for j in range(2):
        for half_j in range(2):
            h = 2 * j + half_j
            for b in range(4):
                r, n = slice(b * 128, b * 128 + 128), (b + 1) * 128
                t = dot_nt(qz[h, r, :], kq[h, :n, :])
                th = jnp.tanh(t)
                m = msk[r, :n]
                up = 1.0 + th
                pw = t * up
                p = (pw * m).astype(bf16)
                p_ref[h, r, :n] = p
                sl_ref[h, r, :n] = ((up + pw * (1.0 - th)) * m).astype(bf16)
                pv = dot(p, uv[h, :n, :]).astype(bf16).astype(f32)
                u_here = uv[h, r, :].astype(f32)
                if half_j == 0:
                    attn_ref[r, j * 128:j * 128 + 128] = pltpu.roll(pv, 64, 1)
                    u_ref[r, j * 128:j * 128 + 128] = u_here
                else:
                    attn_ref[r, j * 128:j * 128 + 128] = jnp.where(lane_lo, attn_ref[r, j * 128:j * 128 + 128], pv)
                    u_ref[r, j * 128:j * 128 + 128] = jnp.where(
                        lane_lo, u_ref[r, j * 128:j * 128 + 128], pltpu.roll(u_here, 64, 1)
                    )

    arrive("dg")

    @pl.loop(0, 4)
    def _(b):
        r = pl.ds(al(b, 128), 128)
        dg = dg_ref[r, :].astype(f32)
        a = attn_ref[r, :]
        m = jnp.mean(a, axis=1, keepdims=True)
        ac = a - m
        e = dg * u_ref[r, :]
        lane = iota((128, 128), 1)
        st = jnp.where(lane == 0, m, jnp.sum(ac * ac, axis=1, keepdims=True))
        st = jnp.where(lane == 2, jnp.sum(e, axis=1, keepdims=True), st)
        st = jnp.where(lane == 3, jnp.sum(e * ac, axis=1, keepdims=True), st)
        st_all[cx, :, pl.ds(al(b, 128), 128)] = jnp.transpose(st)[:8]

    for o in range(1, 4):
        rc(st_all.at[cx], st_all.at[cx], st_s, st_r, {"ctx": lax.rem(cx + o, 4)}).start()
    sends.append(lambda: wait_bytes(st_all.at[pl.ds(0, 3)], st_s, st_r).wait_send())
    flight["st"] = lambda: wait_bytes(st_all.at[pl.ds(0, 3)], st_s, st_r).wait_recv()
    turn()
    arrive("st")
    g_forward()
    ms = [st_all[l, 0:1, :] for l in range(4)]
    m2 = (ms[0] + ms[1] + ms[2] + ms[3]) * 0.25
    sq, se, seo = 0.0, 0.0, 0.0
    for l in range(4):
        d = ms[l] - m2
        sq = sq + st_all[l, 1:2, :] + 256.0 * d * d
        se = se + st_all[l, 2:3, :]
        seo = seo + st_all[l, 3:4, :] + d * st_all[l, 2:3, :]
    r2 = lax.rsqrt(sq * (1.0 / WIDTH) + EPS)
    cmb[0:1, :] = m2
    cmb[1:2, :] = r2
    cmb[2:3, :] = se * (1.0 / WIDTH)
    cmb[3:4, :] = r2 * seo * (1.0 / WIDTH)

    for b in range(4):
        r = slice(b * 128, b * 128 + 128)
        tr = jnp.transpose(cmb[:, r])
        r2c = tr[:, 1:2]
        onorm = (attn_ref[r, :] - tr[:, 0:1]) * r2c
        u, dg = u_ref[r, :], dg_ref[r, :].astype(f32)
        gated[r, :] = (onorm * u).astype(bf16)
        du = (dg * onorm).astype(bf16).astype(f32)
        da = r2c * (dg * u - tr[:, 2:3] - onorm * tr[:, 3:4])
        for j in range(2):
            s = slice(j * 128, j * 128 + 128)
            dout[2 * j, r, :] = jnp.where(lane_lo, 0.0, pltpu.roll(da[:, s], 64, 1)).astype(bf16)
            dout[2 * j + 1, r, :] = jnp.where(lane_lo, 0.0, da[:, s]).astype(bf16)
            du_ref[2 * j, r, :] = du[:, s]
            du_ref[2 * j + 1, r, :] = pltpu.roll(du[:, s], 64, 1)

    for o in (2, 1, 3):
        t = lax.rem(cx + o, 4)
        rc(gated.at[pl.ds(al(t, 128), 128)], gfull.at[own], gt_s, gt_r, {"ctx": t}).start()
    sends.append(lambda: wait_bytes(gated.at[pl.ds(0, 384)], gt_s, gt_r).wait_send())
    flight["gt"] = lambda: wait_bytes(gfull.at[pl.ds(0, 384)], gt_s, gt_r).wait_recv()
    gfull[own, :] = gated[own, :]

    yy, zz = lax.div(chip, 4), lax.rem(chip, 4)
    base = core * 512

    def rows_at(start, count):
        return pl.ds(pl.multiple_of(start, count), count)

    def peer(axis, o):
        y2, z2 = (yy, lax.rem(zz + o, 4)) if axis == 0 else (lax.rem(yy + o, 4), zz)
        return lax.rem((zz if axis == 0 else yy) + o, 4), {"dp": (y2 * 4 + z2) * 2 + core}

    def ours(part):
        return (zz, yy) if part == 0 else (yy, zz)

    def begun(stage, p, ref):
        sends.append(lambda: wait_bytes(ref, ar_ss.at[stage, p], ar_rs.at[stage, p]).wait_send())
        flight["ar", stage, p] = lambda: wait_bytes(ref, ar_ss.at[stage, p], ar_rs.at[stage, p]).wait_recv()

    def to_core(stage, p, src, dst):
        rc(src, dst, ar_ss.at[stage, p], ar_rs.at[stage, p], {"dp": chip * 2 + other}).start()
        begun(stage, p, dst)

    def to_axis(stage, p, places, ref):
        @pl.loop(1, 4)
        def _(o):
            for part in range(2):
                axis = part if stage in (1, 4) else 1 - part
                t, dev = peer(axis, o)
                src, dst = places(part, t)
                rc(src, dst, ar_ss.at[stage, p], ar_rs.at[stage, p], dev).start()

        begun(stage, p, ref)

    def ar1(p):
        to_core(0, p, ar_src.at[p, rows_at(other * 512, 512)], ar_c.at[p])

    def ar2(p):
        arrive(("ar", 0, p))

        @pl.loop(0, 4)
        def _(b):
            r = rows_at(b * 128, 128)
            a = ar_src[p, rows_at(base + b * 128, 128), :].astype(f32)
            ar_h[p, r, :] = (a + ar_c[p, r, :].astype(f32)).astype(bf16)

        for part in range(2):
            mine = rows_at(part * 256 + ours(part)[0] * 64, 64)
            ar_r[p, mine, :] = ar_h[p, mine, :]

        def places(part, t):
            return (
                ar_h.at[p, rows_at(part * 256 + t * 64, 64)],
                ar_r.at[p, rows_at(part * 256 + ours(part)[0] * 64, 64)],
            )

        to_axis(1, p, places, ar_r.at[p, pl.ds(0, 384)])

    def ar3(p):
        arrive(("ar", 1, p))
        for part in range(2):
            acc = jnp.zeros((64, 256), f32)
            for k in range(4):
                acc = acc + ar_r[p, part * 256 + k * 64:part * 256 + k * 64 + 64, :].astype(f32)
            ar_q[p, part * 64:part * 64 + 64, :] = acc.astype(bf16)
            mine = rows_at(part * 64 + ours(part)[1] * 16, 16)
            ar_b[p, mine, :] = ar_q[p, mine, :]

        def places(part, t):
            return ar_q.at[p, rows_at(part * 64 + t * 16, 16)], ar_b.at[p, rows_at(part * 64 + ours(part)[1] * 16, 16)]

        to_axis(2, p, places, ar_b.at[p, pl.ds(0, 96)])

    def ar4(p):
        arrive(("ar", 2, p))
        for part in range(2):
            acc = jnp.zeros((16, 256), f32)
            for k in range(4):
                acc = acc + ar_b[p, part * 64 + k * 16:part * 64 + k * 16 + 16, :].astype(f32)
            first, second = ours(part)
            ar_f[p, rows_at(base + part * 256 + first * 64 + second * 16, 16), :] = acc.astype(bf16)

        def places(part, t):
            first, second = ours(part)
            ref = ar_f.at[p, rows_at(base + part * 256 + first * 64 + second * 16, 16)]
            return ref, ref

        to_axis(3, p, places, ar_f.at[p, pl.ds(0, 96)])

    def ar5(p):
        arrive(("ar", 3, p))

        def places(part, t):
            ref = ar_f.at[p, rows_at(base + part * 256 + ours(part)[0] * 64, 64)]
            return ref, ref

        to_axis(4, p, places, ar_f.at[p, pl.ds(0, 384)])

    def ar6(p):
        arrive(("ar", 4, p))
        ref = ar_f.at[p, rows_at(base, 512)]
        to_core(5, p, ref, ref)

    stores = []

    def ar7(p):
        arrive(("ar", 5, p))
        stores.append(pltpu.make_async_copy(ar_f.at[p], ar_hbm.at[p], out_s.at[p]))
        stores[-1].start()

    def backward(h):
        for b in range(4):
            r, n = slice(b * 128, b * 128 + 128), (b + 1) * 128
            dw = dot_nt(dout[h, r, :], uv[h, :n, :])
            ds = (dw * sl_ref[h, r, :n].astype(f32)).astype(bf16)
            ds_ref[r, :n] = ds
            dq_ref[r, :] = dot(ds, qk[h, :n, :])
        for b in range(4):
            r, c = slice(b * 128, b * 128 + 128), slice(b * 128, 512)
            dv = dot_tn(p_ref[h, c, r], dout[h, c, :])
            dk = dot_tn(ds_ref[c, r], qk[h, c, :])
            d1 = jnp.where(lane_lo, du_ref[h, r, :], dv)
            d2 = pltpu.roll(jnp.where(lane_lo, dk, dq_ref[r, :]), 64, 1) * 0.0625
            dpre[h, r, 0:128] = (d1 * slope[h, r, 0:128]).astype(bf16)
            dpre[h, r, 128:256] = (d2 * slope[h, r, 128:256]).astype(bf16)

    def piece(h):
        for q in range(4):
            acc = dot(nrm_t[q * 256:q * 256 + 256, :], dpre[h])
            ar_src[h + 1, q * 256:q * 256 + 256, :] = acc.astype(bf16)
        ar1(h + 1)

    def dnorm(block, dst):
        rows = pl.ds(al(block, 128), 128)

        for cb in range(4):
            s = slice(cb * 256, cb * 256 + 256)
            acc = dot_nt(dpre[0, rows, :], w[0, s, :])
            for h in range(1, 4):
                acc = acc + dot_nt(dpre[h, rows, :], w[h, s, :])
            dst[:, s] = acc.astype(dst.dtype)

    lo, hi = pl.ds(0, 64), pl.ds(64, 64)

    def rs_go(src, dst, k, way):
        c = rc(src, dst, rs_s.at[k], rs_r.at[k], {"ctx": way})
        c.start()
        sends.append(c.wait_send)
        flight["rs", k] = c.wait_recv

    backward(0)
    piece(0)
    backward(1)
    ar2(1)
    piece(1)
    g_near()
    g_far()
    for cb in range(4):
        ar_src[0, cb * 256:cb * 256 + 256, :] = dot_tn(gated[...], gbuf[:, cb * 256:cb * 256 + 256]).astype(bf16)
    ar1(0)
    ar2(2)
    backward(2)
    ar3(1)
    ar2(0)
    piece(2)
    ar3(2)
    backward(3)
    ar2(3)
    ar4(1)
    ar3(0)
    piece(3)

    to_far, to_right, to_left = rs_send.at[0], rs_send.at[1], rs_send.at[2]
    dnorm(opp, to_far)
    rs_go(to_far.at[lo], rs1.at[0], 0, right)
    rs_go(to_far.at[hi], rs1.at[1], 1, left)
    ar5(1)
    ar4(2)
    dnorm(right, to_right)
    rs_go(to_right.at[hi], rs2.at[0, hi], 2, right)
    ar2(4)
    ar3(3)
    dnorm(left, to_left)
    rs_go(to_left.at[lo], rs2.at[1, lo], 3, left)
    ar4(0)
    ar5(2)
    arrive(("rs", 0))
    to_right[lo, :] = (to_right[lo, :].astype(f32) + rs1[0].astype(f32)).astype(bf16)
    rs_go(to_right.at[lo], rs2.at[0, lo], 4, right)
    arrive(("rs", 1))
    to_left[hi, :] = (to_left[hi, :].astype(f32) + rs1[1].astype(f32)).astype(bf16)
    rs_go(to_left.at[hi], rs2.at[1, hi], 5, left)
    ar3(4)
    ar4(3)
    ar5(0)
    ar6(1)
    arrive("gt")
    for cb in range(4):
        s = slice(cb * 256, cb * 256 + 256)
        acc = xp[:, s].astype(f32)
        for c in range(4):
            acc = acc + dot(gfull[c * 128:c * 128 + 128, :], wo[c * 256:c * 256 + 256, s])
        yd[:, s] = acc.astype(bf16)
    pack_back(yd, send_y)
    a2a_start(2, send_y, recv_y)

    ar4(4)
    ar5(3)
    ar6(2)
    dnorm(cx, rs_own)
    ar5(4)
    ar6(0)
    ar7(1)
    arrive(("rs", 2), ("rs", 3), ("rs", 4), ("rs", 5))
    dn = rs_own[...] + rs2[0].astype(f32) + rs2[1].astype(f32)
    xh2 = xhat[...]
    mean_d = jnp.mean(dn, axis=1, keepdims=True)
    mean_dx = jnp.mean(dn * xh2, axis=1, keepdims=True)
    dx = gbuf[own, :].astype(f32) + rstd_ref[:, 0:1] * (dn - mean_d - xh2 * mean_dx)
    yd[...] = dx.astype(bf16)
    pack_back(yd, send_d)
    a2a_start(3, send_d, recv_d)
    ar6(3)
    ar7(2)
    arrive(("a2a", 2))
    unpack_home(recv_y, y_out)
    stores.append(pltpu.make_async_copy(y_out, y_hbm, out_s.at[PIECES]))
    stores[-1].start()
    ar6(4)
    ar7(0)
    ar7(3)
    ar7(4)
    arrive(("a2a", 3))
    for c in stores:
        c.wait()
    finish()


def last(scale, y, recv, pos_ref, ar, y_out, dx_out, proj, out):
    i = pl.program_id(0)
    y_out[...] = y[...]
    pos_l = jnp.broadcast_to(pos_ref[...], (ROWS, ROWS))
    pos_s = jnp.transpose(pos_l.astype(f32)).astype(i32)
    tgt_l, tgt_s = lax.shift_right_logical(pos_l, 9), lax.shift_right_logical(pos_s, 9)
    before = (tgt_l == tgt_s) & (iota((ROWS, ROWS), 1) < iota((ROWS, ROWS), 0))
    rank = jnp.sum(jnp.where(before, 1.0, 0.0), axis=1, keepdims=True).astype(i32)
    base = tgt_s[:, 0:1] * SLOTS
    lanes = iota((ROWS, 512), 1)
    for k in range(2):
        acc = jnp.zeros((ROWS, 128), f32)
        for L in range(3):
            v = rank + ((2 * i + k) * CAP - 16 * L)
            idx = jnp.where((v >= 0) & (v < 16), base + v, -1)
            acc = acc + dot(one(lanes == idx), recv[:, L * 128:L * 128 + 128])
        dx_out[:, k * 128:k * 128 + 128] = acc.astype(bf16)
    out[...] = ar[0].astype(f32) * scale
    for q in range(8):
        r = slice(q * 32, q * 32 + 32)
        proj[r] = jnp.swapaxes(ar[1:, r, :].astype(f32) * scale, 0, 1)


def shards(tokens, cotangent, packed_pos, segment_ids, w_proj, w_out):
    n_dp = lax.axis_size("dp")
    vmem, sem = pltpu.VMEM, pltpu.SemaphoreType.DMA
    scratch = [
        vmem((128, 1024), bf16), vmem((PIECES, 1024, 256), bf16), sem((PIECES + 1,)),
        vmem((128, 1024), bf16), vmem((128, 1024), bf16), vmem((1024, 4, 256), bf16), vmem((4, 1024, 256), bf16),
        vmem((1024, 1024), bf16), sem((4,)),
        vmem((512, 512), bf16), vmem((512, 512), bf16),
        vmem((512, 384), bf16), vmem((512, 384), bf16),
        vmem((512, 384), bf16), vmem((512, 384), bf16),
        vmem((512, 384), bf16),
        vmem((8, 512), f32), vmem((128, 128), i32),
        vmem((128, 1024), bf16), vmem((128, 1024), f32), vmem((128, 128), f32),
        vmem((512, 1024), bf16), vmem((1024, 512), bf16), vmem((512, 1024), bf16),
        vmem((512, 512), f32), vmem((4, 512, 256), f32),
        vmem((4, 512, 128), bf16), vmem((4, 512, 128), bf16),
        vmem((4, 512, 128), bf16), vmem((4, 512, 128), bf16),
        vmem((4, 512, 512), bf16), vmem((4, 512, 512), bf16),
        vmem((512, 512), bf16), vmem((512, 128), f32),
        vmem((512, 256), f32), vmem((512, 256), f32), vmem((512, 256), bf16),
        vmem((4, 8, 512), f32), vmem((128, 512), f32),
        vmem((512, 256), bf16), vmem((512, 256), bf16),
        vmem((4, 512, 128), bf16), vmem((4, 512, 128), f32), vmem((4, 512, 256), bf16),
        vmem((4, 128, 256), bf16),
        vmem((128, 1024), bf16),
        vmem((PIECES, 1024, 256), bf16), vmem((PIECES, 512, 256), bf16),
        vmem((PIECES, 512, 256), bf16), vmem((PIECES, 512, 256), bf16),
        vmem((PIECES, 128, 256), bf16), vmem((PIECES, 128, 256), bf16),
        vmem((3, 128, 1024), bf16), vmem((128, 1024), f32),
        vmem((2, 64, 1024), bf16), vmem((2, 128, 1024), bf16),
        sem((4,)), sem((4,)), sem((2,)), sem((2, 6)), sem, sem, sem, sem, sem, sem,
        sem((6, PIECES)), sem((6, PIECES)), sem((6,)), sem((6,)),
    ]
    spec, free = pl.BlockSpec(memory_space=pltpu.VMEM), pl.BlockSpec(memory_space=pl.ANY)
    pos = packed_pos.reshape(1, ROWS)
    y, dx, ar = pl.pallas_call(
        functools.partial(kernel, n_dp),
        out_shape=[
            jax.ShapeDtypeStruct((ROWS, WIDTH), bf16),
            jax.ShapeDtypeStruct((512, 384), bf16),
            jax.ShapeDtypeStruct((PIECES, 1024, 256), bf16),
        ],
        in_specs=[free, free, spec, spec, free, free],
        out_specs=[free, spec, free],
        scratch_shapes=scratch,
        compiler_params=pltpu.CompilerParams(
            collective_id=0, has_side_effects=True, vmem_limit_bytes=60 * 1024 * 1024
        ),
        cost_estimate=pl.CostEstimate(flops=6 * 10**9, bytes_accessed=12 * 10**6, transcendentals=3 * 10**6),
    )(tokens, cotangent, pos, segment_ids, w_proj, w_out)
    scale = (ROWS * 4 * n_dp) ** (-0.5)
    return pl.pallas_call(
        functools.partial(last, scale),
        grid=(4,),
        out_shape=[
            jax.ShapeDtypeStruct((ROWS, WIDTH), bf16),
            jax.ShapeDtypeStruct((ROWS, WIDTH), bf16),
            jax.ShapeDtypeStruct((1024, 4, 256), f32),
            jax.ShapeDtypeStruct((256, WIDTH), f32),
        ],
        in_specs=[
            pl.BlockSpec((32, WIDTH), lambda i: (i, 0)),
            pl.BlockSpec((512, 384), lambda i: (0, 0)),
            pl.BlockSpec((1, ROWS), lambda i: (0, 0)),
            pl.BlockSpec((PIECES, 256, 256), lambda i: (0, i, 0)),
        ],
        out_specs=[
            pl.BlockSpec((32, WIDTH), lambda i: (i, 0)),
            pl.BlockSpec((ROWS, 256), lambda i: (0, i)),
            pl.BlockSpec((256, 4, 256), lambda i: (i, 0, 0)),
            pl.BlockSpec((256, 256), lambda i: (0, i)),
        ],
        compiler_params=pltpu.CompilerParams(vmem_limit_bytes=60 * 1024 * 1024),
        cost_estimate=pl.CostEstimate(flops=10**8, bytes_accessed=10 * 10**6, transcendentals=0),
    )(y, dx, pos, ar)


def solution(mesh):
    return jax.shard_map(
        shards,
        mesh=mesh,
        in_specs=(
            P(("dp", "ctx"), None),
            P(("dp", "ctx"), None),
            P(("dp", "ctx")),
            P("dp", None),
            P(None, "ctx", None),
            P(),
        ),
        out_specs=(
            P(("dp", "ctx"), None),
            P(("dp", "ctx"), None),
            P(None, "ctx", None),
            P("ctx", None),
        ),
        check_vma=False,
    )
```

```python
import functools
import jax
import jax.numpy as jnp
from jax import lax
from jax.experimental import pallas as pl
from jax.experimental.pallas import tpu as pltpu
from jax.sharding import PartitionSpec as P

EPS = 1e-05
MESH = pl.DeviceIdType.MESH
bf16, f32, i32 = jnp.bfloat16, jnp.float32, jnp.int32
ROWS, WIDTH, GROUP, SLOTS = 128, 1024, 512, 16
CAP = 6
COMBOS = [(L, c) for L in range(3) for c in range(8) if c * CAP < 16 * L + 16 and c * CAP + CAP > 16 * L]
PIECES = 5


def dot(a, b):
    return lax.dot_general(a, b, (((1,), (0,)), ((), ())), preferred_element_type=f32)


def dot_nt(a, b):
    return lax.dot_general(a, b, (((1,), (1,)), ((), ())), preferred_element_type=f32)


def dot_tn(a, b):
    return lax.dot_general(a, b, (((0,), (0,)), ((), ())), preferred_element_type=f32)


def sigmoid(t):
    return 0.5 * jnp.tanh(0.5 * t) + 0.5


def iota(shape, axis):
    return lax.broadcasted_iota(i32, shape, axis)


def one(cond):
    return jnp.where(cond, 1.0, 0.0).astype(bf16)


def chunk(c):
    return pl.ds(c * 128, 128)


def kernel(
    n_dp,
    tok_h, cot_h, pos_ref, seg_ref, w_h, wo_h,
    y_hbm, recv_d, ar_hbm,
    y_out, ar_f, out_s,
    tok, cot, w_raw, w, wo, in_s,
    send_x, recv_x, send_g, recv_g, send_y, recv_y, send_d,
    meta_t, rank_s, xp, xhat, rstd_ref, nrm, nrm_t, gbuf,
    msk, slope, uv, qk, kq, qz, p_ref, sl_ref, ds_ref, dq_ref,
    attn_ref, u_ref, dg_ref, st_all, cmb, gated, gfull, dout, du_ref, dpre, dg_send,
    yd, ar_src, ar_c, ar_h, ar_r, ar_q, ar_b, rs_send, rs_own, rs1, rs2,
    a2a_s, a2a_r, ag_s, ag_r, st_s, st_r, gt_s, gt_r, dg_s, dg_r, ar_ss, ar_rs, rs_s, rs_r,
):
    me, cx = lax.axis_index("dp"), lax.axis_index("ctx")
    core, chip = lax.rem(me, 2), lax.div(me, 2)
    other = 1 - core
    right, left, opp = lax.rem(cx + 1, 4), lax.rem(cx + 3, 4), lax.rem(cx + 2, 4)
    sends, flight = [], {}

    def rc(src, dst, ss, rs, dev):
        return pltpu.make_async_remote_copy(
            src_ref=src, dst_ref=dst, send_sem=ss, recv_sem=rs, device_id=dev, device_id_type=MESH
        )

    def wait_bytes(ref, ss, rs):
        return rc(ref, ref, ss, rs, {"ctx": right})

    def arrive(*keys):
        for key in keys:
            flight.pop(key)()

    def al(i, m):
        return pl.multiple_of(i * m, m)

    loads = [pltpu.make_async_copy(a, b, in_s.at[i]) for i, (a, b) in enumerate([(tok_h, tok), (cot_h, cot), (w_h, w_raw), (wo_h, wo)])]
    for c in loads:
        c.start()

    bar = pltpu.get_barrier_semaphore()

    @pl.loop(1, n_dp)
    def _(o):
        pl.semaphore_signal(bar, inc=1, device_id={"dp": lax.rem(me + o, n_dp)}, device_id_type=MESH)

    for o in range(1, 4):
        pl.semaphore_signal(bar, inc=1, device_id={"ctx": lax.rem(cx + o, 4)}, device_id_type=MESH)

    pos_l = jnp.broadcast_to(pos_ref[...], (ROWS, ROWS))
    pos_s = jnp.transpose(pos_l.astype(f32)).astype(i32)
    tgt_l, tgt_s = lax.shift_right_logical(pos_l, 9), lax.shift_right_logical(pos_s, 9)
    ii, jj = iota((ROWS, ROWS), 0), iota((ROWS, ROWS), 1)
    same = tgt_l == tgt_s
    rank_l = jnp.sum(jnp.where(same & (ii < jj), 1.0, 0.0), axis=0, keepdims=True).astype(i32)
    rank_c = jnp.sum(jnp.where(same & (jj < ii), 1.0, 0.0), axis=1, keepdims=True).astype(i32)
    tgt_row = tgt_l[:1] * SLOTS
    rank_s[...] = jnp.where(jj == 0, rank_c, tgt_s * SLOTS)
    row_no = (pos_s & (ROWS - 1)) + 1

    def pack_out(src, dst, with_meta):
        @pl.loop(0, 4)
        def _(rb):
            rows = pl.ds(al(rb, 128), 128)
            here = iota((128, ROWS), 0) + rb * 128
            meta = jnp.zeros((128, 128), f32)
            for L in range(3):
                acc = jnp.zeros((128, 128), f32)
                every = jnp.zeros((128, 128), f32)
                for c in [c for (l, c) in COMBOS if l == L]:
                    v = rank_l + (c * CAP - 16 * L)
                    idx = jnp.where((v >= 0) & (v < 16), tgt_row + v, -1)
                    hit = jnp.where(here == idx, 1.0, 0.0)
                    acc = acc + dot(hit.astype(bf16), src[:, c * 128:c * 128 + 128])
                    every = every + hit
                dst[rows, L * 128:L * 128 + 128] = acc.astype(bf16)
                if with_meta:
                    meta = meta + dot(every.astype(bf16), jnp.where(jj == L, row_no, 0).astype(f32).astype(bf16))
            if with_meta:
                dst[rows, 384:512] = meta.astype(bf16)

    def a2a_start(k, src, dst):
        mine = pl.ds(al(me, SLOTS), SLOTS)
        dst[mine, :] = src[mine, :]

        @pl.loop(1, n_dp)
        def _(o):
            t = lax.rem(me + o, n_dp)
            rc(src.at[pl.ds(al(t, SLOTS), SLOTS)], dst.at[mine], a2a_s.at[k], a2a_r.at[k], {"dp": t}).start()

        part = src.at[pl.ds(0, (n_dp - 1) * SLOTS)]
        sends.append(lambda: wait_bytes(part, a2a_s.at[k], a2a_r.at[k]).wait_send())
        come = dst.at[pl.ds(0, (n_dp - 1) * SLOTS)]
        flight["a2a", k] = lambda: wait_bytes(come, a2a_s.at[k], a2a_r.at[k]).wait_recv()

    def unpack_arrived(src, dst, rows):
        unit = iota((ROWS, 512), 1) & 15
        for c in range(8):
            acc = jnp.zeros((ROWS, 128), f32)
            for L in [l for (l, d) in COMBOS if d == c]:
                lo = c * CAP - 16 * L
                hit = (meta_t[L:L + 1, :] == (iota((ROWS, 512), 0) + 1).astype(f32)) & (unit >= lo) & (unit < lo + CAP)
                acc = acc + dot(one(hit), src[:, L * 128:L * 128 + 128])
            dst[rows, c * 128:c * 128 + 128] = acc.astype(bf16)

    def pack_back(src, dst):
        @pl.loop(0, 4)
        def _(rb):
            rows = pl.ds(al(rb, 128), 128)
            meta = recv_x[rows, 384:512].astype(f32)
            unit = iota((128, ROWS), 0) & 15
            lane = (iota((128, ROWS), 1) + 1).astype(f32)
            for L in range(3):
                acc = jnp.zeros((128, 128), f32)
                mine = meta[:, L:L + 1] == lane
                for c in [c for (l, c) in COMBOS if l == L]:
                    lo = c * CAP - 16 * L
                    acc = acc + dot(one(mine & (unit >= lo) & (unit < lo + CAP)), src[:, c * 128:c * 128 + 128])
                dst[rows, L * 128:L * 128 + 128] = acc.astype(bf16)

    def unpack_home(src, dst):
        rank, base = rank_s[:, 0:1], rank_s[:, 1:2]
        lanes = iota((ROWS, 512), 1)
        for c in range(8):
            acc = jnp.zeros((ROWS, 128), f32)
            for L in [l for (l, d) in COMBOS if d == c]:
                v = rank + (c * CAP - 16 * L)
                idx = jnp.where((v >= 0) & (v < 16), base + v, -1)
                acc = acc + dot(one(lanes == idx), src[:, L * 128:L * 128 + 128])
            dst[:, c * 128:c * 128 + 128] = acc.astype(bf16)

    def finish():
        for f in sends:
            f()

    loads[0].wait()
    pack_out(tok, send_x, True)
    pl.semaphore_wait(bar, n_dp - 1 + 3)
    a2a_start(0, send_x, recv_x)
    loads[1].wait()
    pack_out(cot, send_g, False)

    seg_row = seg_ref[...]
    seg_col = jnp.transpose(jnp.broadcast_to(seg_row.astype(f32), (128, GROUP))).astype(i32)
    for b in range(4):
        sc = seg_col[b * 128:b * 128 + 128, 0:1]
        ok = (sc == seg_row) & (iota((128, GROUP), 1) <= iota((128, GROUP), 0) + b * 128)
        msk[b * 128:b * 128 + 128, :] = jnp.where(ok, 1.0, 0.0)
    cmb[...] = jnp.zeros_like(cmb)

    own = pl.ds(al(cx, 128), 128)
    loads[2].wait()

    @pl.loop(0, 16)
    def _(i):
        rows = pl.ds(al(i, 64), 64)
        w[:, rows, :] = jnp.swapaxes(w_raw[rows].astype(f32), 0, 1).astype(bf16)

    loads[3].wait()
    arrive(("a2a", 0))
    meta_t[...] = jnp.transpose(recv_x[:, 384:512].astype(f32))[:8]
    unpack_arrived(recv_x, xp, pl.ds(0, 128))
    xf = xp[...].astype(f32)
    mean = jnp.mean(xf, axis=1, keepdims=True)
    rstd = lax.rsqrt(jnp.mean((xf - mean) ** 2, axis=1, keepdims=True) + EPS)
    xh = (xf - mean) * rstd
    xhat[...] = xh
    rstd_ref[...] = jnp.broadcast_to(rstd, (ROWS, 128))
    nrm[own, :] = xh.astype(bf16)

    def half(b, k):
        return pl.ds(pl.multiple_of(b * 128 + k * 64, 64), 64)

    def ag(k, buf):
        def to(block, h, way, slot):
            ref = buf.at[half(block, h)]
            return rc(ref, ref, ag_s.at[k], ag_r.at[k, slot], {"ctx": way})

        def go(block, h, way, slot, source):
            to(block, h, way, slot).start()
            sends.append(to(block, h, way, slot).wait_send)
            flight["ag", k, slot] = to(source, h, way, slot).wait_recv

        def start():
            go(cx, 0, right, 0, left)
            go(cx, 1, left, 1, right)
            go(cx, 1, right, 2, left)
            go(cx, 0, left, 3, right)

        def forward():
            arrive(("ag", k, 0))
            go(left, 0, right, 4, opp)
            arrive(("ag", k, 1))
            go(right, 1, left, 5, opp)

        def near():
            arrive(("ag", k, 2), ("ag", k, 3))

        def far():
            arrive(("ag", k, 4), ("ag", k, 5))

        return start, forward, near, far

    lane_lo = iota((128, 128), 1) < 64

    def project(block):
        rows = pl.ds(al(block, 128), 128)
        for h in range(4):
            pre = dot(nrm[rows, :], w[h])
            sig = sigmoid(pre)
            act = pre * sig
            slope[h, rows, :] = sig + act * (1.0 - sig)
            uv[h, rows, :] = act[:, :128].astype(bf16)
            b = act[:, 128:].astype(bf16)
            qk[h, rows, :] = b
            bf = b.astype(f32)
            kq[h, rows, :] = pltpu.roll(bf, 64, 1).astype(bf16)
            qz[h, rows, :] = jnp.where(lane_lo, bf * 0.0625, 0.0).astype(bf16)

    def turn():
        for b in range(4):
            nrm_t[:, b * 128:b * 128 + 128] = jnp.transpose(nrm[b * 128:b * 128 + 128, :].astype(f32)).astype(bf16)

    n_start, n_forward, n_near, n_far = ag(0, nrm)
    g_start, g_forward, g_near, g_far = ag(1, gbuf)
    n_start()
    a2a_start(1, send_g, recv_g)
    project(cx)
    n_forward()
    n_near()
    project(left)
    project(right)
    arrive(("a2a", 1))
    unpack_arrived(recv_g, gbuf, own)
    for t in range(4):
        dg_send[t] = dot_nt(gbuf[own, :], wo[t * 256:t * 256 + 256, :]).astype(bf16)
    for o in (2, 1, 3):
        t = lax.rem(cx + o, 4)
        rc(dg_send.at[t], dg_ref.at[own], dg_s, dg_r, {"ctx": t}).start()
    sends.append(lambda: wait_bytes(dg_ref.at[pl.ds(0, 384)], dg_s, dg_r).wait_send())
    flight["dg"] = lambda: wait_bytes(dg_ref.at[pl.ds(0, 384)], dg_s, dg_r).wait_recv()
    dg_ref[own, :] = dg_send[cx]
    n_far()
    g_start()
    project(opp)

    for j in range(2):
        for half_j in range(2):
            h = 2 * j + half_j
            for b in range(4):
                r, n = slice(b * 128, b * 128 + 128), (b + 1) * 128
                t = dot_nt(qz[h, r, :], kq[h, :n, :])
                th = jnp.tanh(t)
                m = msk[r, :n]
                up = 1.0 + th
                pw = t * up
                p = (pw * m).astype(bf16)
                p_ref[h, r, :n] = p
                sl_ref[h, r, :n] = ((up + pw * (1.0 - th)) * m).astype(bf16)
                pv = dot(p, uv[h, :n, :]).astype(bf16).astype(f32)
                u_here = uv[h, r, :].astype(f32)
                if half_j == 0:
                    attn_ref[r, j * 128:j * 128 + 128] = pltpu.roll(pv, 64, 1)
                    u_ref[r, j * 128:j * 128 + 128] = u_here
                else:
                    attn_ref[r, j * 128:j * 128 + 128] = jnp.where(lane_lo, attn_ref[r, j * 128:j * 128 + 128], pv)
                    u_ref[r, j * 128:j * 128 + 128] = jnp.where(
                        lane_lo, u_ref[r, j * 128:j * 128 + 128], pltpu.roll(u_here, 64, 1)
                    )

    arrive("dg")

    @pl.loop(0, 4)
    def _(b):
        r = pl.ds(al(b, 128), 128)
        dg = dg_ref[r, :].astype(f32)
        a = attn_ref[r, :]
        m = jnp.mean(a, axis=1, keepdims=True)
        ac = a - m
        e = dg * u_ref[r, :]
        lane = iota((128, 128), 1)
        st = jnp.where(lane == 0, m, jnp.sum(ac * ac, axis=1, keepdims=True))
        st = jnp.where(lane == 2, jnp.sum(e, axis=1, keepdims=True), st)
        st = jnp.where(lane == 3, jnp.sum(e * ac, axis=1, keepdims=True), st)
        st_all[cx, :, pl.ds(al(b, 128), 128)] = jnp.transpose(st)[:8]

    for o in range(1, 4):
        rc(st_all.at[cx], st_all.at[cx], st_s, st_r, {"ctx": lax.rem(cx + o, 4)}).start()
    sends.append(lambda: wait_bytes(st_all.at[pl.ds(0, 3)], st_s, st_r).wait_send())
    flight["st"] = lambda: wait_bytes(st_all.at[pl.ds(0, 3)], st_s, st_r).wait_recv()
    turn()
    arrive("st")
    g_forward()
    ms = [st_all[l, 0:1, :] for l in range(4)]
    m2 = (ms[0] + ms[1] + ms[2] + ms[3]) * 0.25
    sq, se, seo = 0.0, 0.0, 0.0
    for l in range(4):
        d = ms[l] - m2
        sq = sq + st_all[l, 1:2, :] + 256.0 * d * d
        se = se + st_all[l, 2:3, :]
        seo = seo + st_all[l, 3:4, :] + d * st_all[l, 2:3, :]
    r2 = lax.rsqrt(sq * (1.0 / WIDTH) + EPS)
    cmb[0:1, :] = m2
    cmb[1:2, :] = r2
    cmb[2:3, :] = se * (1.0 / WIDTH)
    cmb[3:4, :] = r2 * seo * (1.0 / WIDTH)

    for b in range(4):
        r = slice(b * 128, b * 128 + 128)
        tr = jnp.transpose(cmb[:, r])
        r2c = tr[:, 1:2]
        onorm = (attn_ref[r, :] - tr[:, 0:1]) * r2c
        u, dg = u_ref[r, :], dg_ref[r, :].astype(f32)
        gated[r, :] = (onorm * u).astype(bf16)
        du = (dg * onorm).astype(bf16).astype(f32)
        da = r2c * (dg * u - tr[:, 2:3] - onorm * tr[:, 3:4])
        for j in range(2):
            s = slice(j * 128, j * 128 + 128)
            dout[2 * j, r, :] = jnp.where(lane_lo, 0.0, pltpu.roll(da[:, s], 64, 1)).astype(bf16)
            dout[2 * j + 1, r, :] = jnp.where(lane_lo, 0.0, da[:, s]).astype(bf16)
            du_ref[2 * j, r, :] = du[:, s]
            du_ref[2 * j + 1, r, :] = pltpu.roll(du[:, s], 64, 1)

    for o in (2, 1, 3):
        t = lax.rem(cx + o, 4)
        rc(gated.at[pl.ds(al(t, 128), 128)], gfull.at[own], gt_s, gt_r, {"ctx": t}).start()
    sends.append(lambda: wait_bytes(gated.at[pl.ds(0, 384)], gt_s, gt_r).wait_send())
    flight["gt"] = lambda: wait_bytes(gfull.at[pl.ds(0, 384)], gt_s, gt_r).wait_recv()
    gfull[own, :] = gated[own, :]

    yy, zz = lax.div(chip, 4), lax.rem(chip, 4)
    base = core * 512

    def rows_at(start, count):
        return pl.ds(pl.multiple_of(start, count), count)

    def peer(axis, o):
        y2, z2 = (yy, lax.rem(zz + o, 4)) if axis == 0 else (lax.rem(yy + o, 4), zz)
        return lax.rem((zz if axis == 0 else yy) + o, 4), {"dp": (y2 * 4 + z2) * 2 + core}

    def ours(part):
        return (zz, yy) if part == 0 else (yy, zz)

    def begun(stage, p, ref):
        sends.append(lambda: wait_bytes(ref, ar_ss.at[stage, p], ar_rs.at[stage, p]).wait_send())
        flight["ar", stage, p] = lambda: wait_bytes(ref, ar_ss.at[stage, p], ar_rs.at[stage, p]).wait_recv()

    def to_core(stage, p, src, dst):
        rc(src, dst, ar_ss.at[stage, p], ar_rs.at[stage, p], {"dp": chip * 2 + other}).start()
        begun(stage, p, dst)

    def to_axis(stage, p, places, ref):
        @pl.loop(1, 4)
        def _(o):
            for part in range(2):
                axis = part if stage in (1, 4) else 1 - part
                t, dev = peer(axis, o)
                src, dst = places(part, t)
                rc(src, dst, ar_ss.at[stage, p], ar_rs.at[stage, p], dev).start()

        begun(stage, p, ref)

    def ar1(p):
        to_core(0, p, ar_src.at[p, rows_at(other * 512, 512)], ar_c.at[p])

    def ar2(p):
        arrive(("ar", 0, p))

        @pl.loop(0, 4)
        def _(b):
            r = rows_at(b * 128, 128)
            a = ar_src[p, rows_at(base + b * 128, 128), :].astype(f32)
            ar_h[p, r, :] = (a + ar_c[p, r, :].astype(f32)).astype(bf16)

        for part in range(2):
            mine = rows_at(part * 256 + ours(part)[0] * 64, 64)
            ar_r[p, mine, :] = ar_h[p, mine, :]

        def places(part, t):
            return (
                ar_h.at[p, rows_at(part * 256 + t * 64, 64)],
                ar_r.at[p, rows_at(part * 256 + ours(part)[0] * 64, 64)],
            )

        to_axis(1, p, places, ar_r.at[p, pl.ds(0, 384)])

    def ar3(p):
        arrive(("ar", 1, p))
        for part in range(2):
            acc = jnp.zeros((64, 256), f32)
            for k in range(4):
                acc = acc + ar_r[p, part * 256 + k * 64:part * 256 + k * 64 + 64, :].astype(f32)
            ar_q[p, part * 64:part * 64 + 64, :] = acc.astype(bf16)
            mine = rows_at(part * 64 + ours(part)[1] * 16, 16)
            ar_b[p, mine, :] = ar_q[p, mine, :]

        def places(part, t):
            return ar_q.at[p, rows_at(part * 64 + t * 16, 16)], ar_b.at[p, rows_at(part * 64 + ours(part)[1] * 16, 16)]

        to_axis(2, p, places, ar_b.at[p, pl.ds(0, 96)])

    def ar4(p):
        arrive(("ar", 2, p))
        for part in range(2):
            acc = jnp.zeros((16, 256), f32)
            for k in range(4):
                acc = acc + ar_b[p, part * 64 + k * 16:part * 64 + k * 16 + 16, :].astype(f32)
            first, second = ours(part)
            ar_f[p, rows_at(base + part * 256 + first * 64 + second * 16, 16), :] = acc.astype(bf16)

        def places(part, t):
            first, second = ours(part)
            ref = ar_f.at[p, rows_at(base + part * 256 + first * 64 + second * 16, 16)]
            return ref, ref

        to_axis(3, p, places, ar_f.at[p, pl.ds(0, 96)])

    def ar5(p):
        arrive(("ar", 3, p))

        def places(part, t):
            ref = ar_f.at[p, rows_at(base + part * 256 + ours(part)[0] * 64, 64)]
            return ref, ref

        to_axis(4, p, places, ar_f.at[p, pl.ds(0, 384)])

    def ar6(p):
        arrive(("ar", 4, p))
        ref = ar_f.at[p, rows_at(base, 512)]
        to_core(5, p, ref, ref)

    stores = []

    def ar7(p):
        arrive(("ar", 5, p))
        stores.append(pltpu.make_async_copy(ar_f.at[p], ar_hbm.at[p], out_s.at[p]))
        stores[-1].start()

    def backward(h):
        for b in range(4):
            r, n = slice(b * 128, b * 128 + 128), (b + 1) * 128
            dw = dot_nt(dout[h, r, :], uv[h, :n, :])
            ds = (dw * sl_ref[h, r, :n].astype(f32)).astype(bf16)
            ds_ref[r, :n] = ds
            dq_ref[r, :] = dot(ds, qk[h, :n, :])
        for b in range(4):
            r, c = slice(b * 128, b * 128 + 128), slice(b * 128, 512)
            dv = dot_tn(p_ref[h, c, r], dout[h, c, :])
            dk = dot_tn(ds_ref[c, r], qk[h, c, :])
            d1 = jnp.where(lane_lo, du_ref[h, r, :], dv)
            d2 = pltpu.roll(jnp.where(lane_lo, dk, dq_ref[r, :]), 64, 1) * 0.0625
            dpre[h, r, 0:128] = (d1 * slope[h, r, 0:128]).astype(bf16)
            dpre[h, r, 128:256] = (d2 * slope[h, r, 128:256]).astype(bf16)

    def piece(h):
        for q in range(4):
            acc = dot(nrm_t[q * 256:q * 256 + 256, :], dpre[h])
            ar_src[h + 1, q * 256:q * 256 + 256, :] = acc.astype(bf16)
        ar1(h + 1)

    def dnorm(block, dst):
        rows = pl.ds(al(block, 128), 128)

        for cb in range(4):
            s = slice(cb * 256, cb * 256 + 256)
            acc = dot_nt(dpre[0, rows, :], w[0, s, :])
            for h in range(1, 4):
                acc = acc + dot_nt(dpre[h, rows, :], w[h, s, :])
            dst[:, s] = acc.astype(dst.dtype)

    lo, hi = pl.ds(0, 64), pl.ds(64, 64)

    def rs_go(src, dst, k, way):
        c = rc(src, dst, rs_s.at[k], rs_r.at[k], {"ctx": way})
        c.start()
        sends.append(c.wait_send)
        flight["rs", k] = c.wait_recv

    backward(0)
    piece(0)
    backward(1)
    ar2(1)
    piece(1)
    g_near()
    g_far()
    for cb in range(4):
        ar_src[0, cb * 256:cb * 256 + 256, :] = dot_tn(gated[...], gbuf[:, cb * 256:cb * 256 + 256]).astype(bf16)
    ar1(0)
    ar2(2)
    backward(2)
    ar3(1)
    ar2(0)
    piece(2)
    ar3(2)
    backward(3)
    ar2(3)
    ar4(1)
    ar3(0)
    piece(3)

    to_far, to_right, to_left = rs_send.at[0], rs_send.at[1], rs_send.at[2]
    dnorm(opp, to_far)
    rs_go(to_far.at[lo], rs1.at[0], 0, right)
    rs_go(to_far.at[hi], rs1.at[1], 1, left)
    ar5(1)
    ar4(2)
    dnorm(right, to_right)
    rs_go(to_right.at[hi], rs2.at[0, hi], 2, right)
    ar2(4)
    ar3(3)
    dnorm(left, to_left)
    rs_go(to_left.at[lo], rs2.at[1, lo], 3, left)
    ar4(0)
    ar5(2)
    arrive(("rs", 0))
    to_right[lo, :] = (to_right[lo, :].astype(f32) + rs1[0].astype(f32)).astype(bf16)
    rs_go(to_right.at[lo], rs2.at[0, lo], 4, right)
    arrive(("rs", 1))
    to_left[hi, :] = (to_left[hi, :].astype(f32) + rs1[1].astype(f32)).astype(bf16)
    rs_go(to_left.at[hi], rs2.at[1, hi], 5, left)
    ar3(4)
    ar4(3)
    ar5(0)
    ar6(1)
    arrive("gt")
    for cb in range(4):
        s = slice(cb * 256, cb * 256 + 256)
        acc = xp[:, s].astype(f32)
        for c in range(4):
            acc = acc + dot(gfull[c * 128:c * 128 + 128, :], wo[c * 256:c * 256 + 256, s])
        yd[:, s] = acc.astype(bf16)
    pack_back(yd, send_y)
    a2a_start(2, send_y, recv_y)

    ar4(4)
    ar5(3)
    ar6(2)
    dnorm(cx, rs_own)
    ar5(4)
    ar6(0)
    ar7(1)
    arrive(("rs", 2), ("rs", 3), ("rs", 4), ("rs", 5))
    dn = rs_own[...] + rs2[0].astype(f32) + rs2[1].astype(f32)
    xh2 = xhat[...]
    mean_d = jnp.mean(dn, axis=1, keepdims=True)
    mean_dx = jnp.mean(dn * xh2, axis=1, keepdims=True)
    dx = gbuf[own, :].astype(f32) + rstd_ref[:, 0:1] * (dn - mean_d - xh2 * mean_dx)
    yd[...] = dx.astype(bf16)
    pack_back(yd, send_d)
    a2a_start(3, send_d, recv_d)
    ar6(3)
    ar7(2)
    arrive(("a2a", 2))
    unpack_home(recv_y, y_out)
    stores.append(pltpu.make_async_copy(y_out, y_hbm, out_s.at[PIECES]))
    stores[-1].start()
    ar6(4)
    ar7(0)
    ar7(3)
    ar7(4)
    arrive(("a2a", 3))
    for c in stores:
        c.wait()
    finish()


def last(scale, y, recv, pos_ref, ar, y_out, dx_out, proj, out):
    i = pl.program_id(0)
    y_out[...] = y[...]
    pos_l = jnp.broadcast_to(pos_ref[...], (ROWS, ROWS))
    pos_s = jnp.transpose(pos_l.astype(f32)).astype(i32)
    tgt_l, tgt_s = lax.shift_right_logical(pos_l, 9), lax.shift_right_logical(pos_s, 9)
    before = (tgt_l == tgt_s) & (iota((ROWS, ROWS), 1) < iota((ROWS, ROWS), 0))
    rank = jnp.sum(jnp.where(before, 1.0, 0.0), axis=1, keepdims=True).astype(i32)
    base = tgt_s[:, 0:1] * SLOTS
    lanes = iota((ROWS, 512), 1)
    for k in range(2):
        acc = jnp.zeros((ROWS, 128), f32)
        for L in range(3):
            v = rank + ((2 * i + k) * CAP - 16 * L)
            idx = jnp.where((v >= 0) & (v < 16), base + v, -1)
            acc = acc + dot(one(lanes == idx), recv[:, L * 128:L * 128 + 128])
        dx_out[:, k * 128:k * 128 + 128] = acc.astype(bf16)
    out[...] = ar[0].astype(f32) * scale
    for q in range(8):
        r = slice(q * 32, q * 32 + 32)
        proj[r] = jnp.swapaxes(ar[1:, r, :].astype(f32) * scale, 0, 1)


def shards(tokens, cotangent, packed_pos, segment_ids, w_proj, w_out):
    n_dp = lax.axis_size("dp")
    vmem, sem = pltpu.VMEM, pltpu.SemaphoreType.DMA
    scratch = [
        vmem((128, 1024), bf16), vmem((PIECES, 1024, 256), bf16), sem((PIECES + 1,)),
        vmem((128, 1024), bf16), vmem((128, 1024), bf16), vmem((1024, 4, 256), bf16), vmem((4, 1024, 256), bf16),
        vmem((1024, 1024), bf16), sem((4,)),
        vmem((512, 512), bf16), vmem((512, 512), bf16),
        vmem((512, 384), bf16), vmem((512, 384), bf16),
        vmem((512, 384), bf16), vmem((512, 384), bf16),
        vmem((512, 384), bf16),
        vmem((8, 512), f32), vmem((128, 128), i32),
        vmem((128, 1024), bf16), vmem((128, 1024), f32), vmem((128, 128), f32),
        vmem((512, 1024), bf16), vmem((1024, 512), bf16), vmem((512, 1024), bf16),
        vmem((512, 512), f32), vmem((4, 512, 256), f32),
        vmem((4, 512, 128), bf16), vmem((4, 512, 128), bf16),
        vmem((4, 512, 128), bf16), vmem((4, 512, 128), bf16),
        vmem((4, 512, 512), bf16), vmem((4, 512, 512), bf16),
        vmem((512, 512), bf16), vmem((512, 128), f32),
        vmem((512, 256), f32), vmem((512, 256), f32), vmem((512, 256), bf16),
        vmem((4, 8, 512), f32), vmem((128, 512), f32),
        vmem((512, 256), bf16), vmem((512, 256), bf16),
        vmem((4, 512, 128), bf16), vmem((4, 512, 128), f32), vmem((4, 512, 256), bf16),
        vmem((4, 128, 256), bf16),
        vmem((128, 1024), bf16),
        vmem((PIECES, 1024, 256), bf16), vmem((PIECES, 512, 256), bf16),
        vmem((PIECES, 512, 256), bf16), vmem((PIECES, 512, 256), bf16),
        vmem((PIECES, 128, 256), bf16), vmem((PIECES, 128, 256), bf16),
        vmem((3, 128, 1024), bf16), vmem((128, 1024), f32),
        vmem((2, 64, 1024), bf16), vmem((2, 128, 1024), bf16),
        sem((4,)), sem((4,)), sem((2,)), sem((2, 6)), sem, sem, sem, sem, sem, sem,
        sem((6, PIECES)), sem((6, PIECES)), sem((6,)), sem((6,)),
    ]
    spec, free = pl.BlockSpec(memory_space=pltpu.VMEM), pl.BlockSpec(memory_space=pl.ANY)
    pos = packed_pos.reshape(1, ROWS)
    y, dx, ar = pl.pallas_call(
        functools.partial(kernel, n_dp),
        out_shape=[
            jax.ShapeDtypeStruct((ROWS, WIDTH), bf16),
            jax.ShapeDtypeStruct((512, 384), bf16),
            jax.ShapeDtypeStruct((PIECES, 1024, 256), bf16),
        ],
        in_specs=[free, free, spec, spec, free, free],
        out_specs=[free, spec, free],
        scratch_shapes=scratch,
        compiler_params=pltpu.CompilerParams(
            collective_id=0, has_side_effects=True, vmem_limit_bytes=60 * 1024 * 1024
        ),
        cost_estimate=pl.CostEstimate(flops=6 * 10**9, bytes_accessed=12 * 10**6, transcendentals=3 * 10**6),
    )(tokens, cotangent, pos, segment_ids, w_proj, w_out)
    scale = (ROWS * 4 * n_dp) ** (-0.5)
    return pl.pallas_call(
        functools.partial(last, scale),
        grid=(4,),
        out_shape=[
            jax.ShapeDtypeStruct((ROWS, WIDTH), bf16),
            jax.ShapeDtypeStruct((ROWS, WIDTH), bf16),
            jax.ShapeDtypeStruct((1024, 4, 256), f32),
            jax.ShapeDtypeStruct((256, WIDTH), f32),
        ],
        in_specs=[
            pl.BlockSpec((32, WIDTH), lambda i: (i, 0)),
            pl.BlockSpec((512, 384), lambda i: (0, 0)),
            pl.BlockSpec((1, ROWS), lambda i: (0, 0)),
            pl.BlockSpec((PIECES, 256, 256), lambda i: (0, i, 0)),
        ],
        out_specs=[
            pl.BlockSpec((32, WIDTH), lambda i: (i, 0)),
            pl.BlockSpec((ROWS, 256), lambda i: (0, i)),
            pl.BlockSpec((256, 4, 256), lambda i: (i, 0, 0)),
            pl.BlockSpec((256, 256), lambda i: (0, i)),
        ],
        compiler_params=pltpu.CompilerParams(vmem_limit_bytes=60 * 1024 * 1024),
        cost_estimate=pl.CostEstimate(flops=10**8, bytes_accessed=10 * 10**6, transcendentals=0),
    )(y, dx, pos, ar)


def solution(mesh):
    return jax.shard_map(
        shards,
        mesh=mesh,
        in_specs=(
            P(("dp", "ctx"), None),
            P(("dp", "ctx"), None),
            P(("dp", "ctx")),
            P("dp", None),
            P(None, "ctx", None),
            P(),
        ),
        out_specs=(
            P(("dp", "ctx"), None),
            P(("dp", "ctx"), None),
            P(None, "ctx", None),
            P("ctx", None),
        ),
        check_vma=False,
    )
```

```python
import functools
import jax
import jax.numpy as jnp
from jax import lax
from jax.experimental import pallas as pl
from jax.experimental.pallas import tpu as pltpu
from jax.sharding import PartitionSpec as P

EPS = 1e-05
MESH = pl.DeviceIdType.MESH
bf16, f32, i32 = jnp.bfloat16, jnp.float32, jnp.int32
ROWS, WIDTH, GROUP, SLOTS = 128, 1024, 512, 16
CAP = 6
COMBOS = [(L, c) for L in range(3) for c in range(8) if c * CAP < 16 * L + 16 and c * CAP + CAP > 16 * L]
PIECES = 5


def dot(a, b):
    return lax.dot_general(a, b, (((1,), (0,)), ((), ())), preferred_element_type=f32)


def dot_nt(a, b):
    return lax.dot_general(a, b, (((1,), (1,)), ((), ())), preferred_element_type=f32)


def dot_tn(a, b):
    return lax.dot_general(a, b, (((0,), (0,)), ((), ())), preferred_element_type=f32)


def sigmoid(t):
    return 0.5 * jnp.tanh(0.5 * t) + 0.5


def iota(shape, axis):
    return lax.broadcasted_iota(i32, shape, axis)


def one(cond):
    return jnp.where(cond, 1.0, 0.0).astype(bf16)


def chunk(c):
    return pl.ds(c * 128, 128)


def kernel(
    n_dp,
    tok_h, cot_h, pos_ref, seg_ref, w_h, wo_h,
    y_hbm, recv_d, ar_hbm,
    y_out, ar_f, out_s,
    tok, cot, w_raw, w, wo, in_s,
    send_x, recv_x, send_g, recv_g, send_y, recv_y, send_d,
    meta_t, rank_s, xp, xhat, rstd_ref, nrm, nrm_t, gbuf,
    msk, slope, uv, qk, kq, qz, p_ref, sl_ref, ds_ref, dq_ref,
    attn_ref, u_ref, dg_ref, st_all, cmb, gated, gfull, dout, du_ref, dpre, dg_send,
    yd, ar_src, ar_c, ar_h, ar_r, ar_q, ar_b, rs_send, rs_own, rs1, rs2,
    a2a_s, a2a_r, ag_s, ag_r, st_s, st_r, gt_s, gt_r, dg_s, dg_r, ar_ss, ar_rs, rs_s, rs_r,
):
    me, cx = lax.axis_index("dp"), lax.axis_index("ctx")
    core, chip = lax.rem(me, 2), lax.div(me, 2)
    other = 1 - core
    right, left, opp = lax.rem(cx + 1, 4), lax.rem(cx + 3, 4), lax.rem(cx + 2, 4)
    sends, flight = [], {}

    def rc(src, dst, ss, rs, dev):
        return pltpu.make_async_remote_copy(
            src_ref=src, dst_ref=dst, send_sem=ss, recv_sem=rs, device_id=dev, device_id_type=MESH
        )

    def wait_bytes(ref, ss, rs):
        return rc(ref, ref, ss, rs, {"ctx": right})

    def arrive(*keys):
        for key in keys:
            flight.pop(key)()

    def al(i, m):
        return pl.multiple_of(i * m, m)

    loads = [pltpu.make_async_copy(a, b, in_s.at[i]) for i, (a, b) in enumerate([(tok_h, tok), (cot_h, cot), (w_h, w_raw), (wo_h, wo)])]
    for c in loads:
        c.start()

    bar = pltpu.get_barrier_semaphore()

    @pl.loop(1, n_dp)
    def _(o):
        pl.semaphore_signal(bar, inc=1, device_id={"dp": lax.rem(me + o, n_dp)}, device_id_type=MESH)

    for o in range(1, 4):
        pl.semaphore_signal(bar, inc=1, device_id={"ctx": lax.rem(cx + o, 4)}, device_id_type=MESH)

    pos_l = jnp.broadcast_to(pos_ref[...], (ROWS, ROWS))
    pos_s = jnp.transpose(pos_l.astype(f32)).astype(i32)
    tgt_l, tgt_s = lax.shift_right_logical(pos_l, 9), lax.shift_right_logical(pos_s, 9)
    ii, jj = iota((ROWS, ROWS), 0), iota((ROWS, ROWS), 1)
    same = tgt_l == tgt_s
    rank_l = jnp.sum(jnp.where(same & (ii < jj), 1.0, 0.0), axis=0, keepdims=True).astype(i32)
    rank_c = jnp.sum(jnp.where(same & (jj < ii), 1.0, 0.0), axis=1, keepdims=True).astype(i32)
    tgt_row = tgt_l[:1] * SLOTS
    rank_s[...] = jnp.where(jj == 0, rank_c, tgt_s * SLOTS)
    row_no = (pos_s & (ROWS - 1)) + 1

    def pack_out(src, dst, with_meta):
        @pl.loop(0, 4)
        def _(rb):
            rows = pl.ds(al(rb, 128), 128)
            here = iota((128, ROWS), 0) + rb * 128
            meta = jnp.zeros((128, 128), f32)
            for L in range(3):
                acc = jnp.zeros((128, 128), f32)
                every = jnp.zeros((128, 128), f32)
                for c in [c for (l, c) in COMBOS if l == L]:
                    v = rank_l + (c * CAP - 16 * L)
                    idx = jnp.where((v >= 0) & (v < 16), tgt_row + v, -1)
                    hit = jnp.where(here == idx, 1.0, 0.0)
                    acc = acc + dot(hit.astype(bf16), src[:, c * 128:c * 128 + 128])
                    every = every + hit
                dst[rows, L * 128:L * 128 + 128] = acc.astype(bf16)
                if with_meta:
                    meta = meta + dot(every.astype(bf16), jnp.where(jj == L, row_no, 0).astype(f32).astype(bf16))
            if with_meta:
                dst[rows, 384:512] = meta.astype(bf16)

    def a2a_start(k, src, dst):
        mine = pl.ds(al(me, SLOTS), SLOTS)
        dst[mine, :] = src[mine, :]

        @pl.loop(1, n_dp)
        def _(o):
            t = lax.rem(me + o, n_dp)
            rc(src.at[pl.ds(al(t, SLOTS), SLOTS)], dst.at[mine], a2a_s.at[k], a2a_r.at[k], {"dp": t}).start()

        part = src.at[pl.ds(0, (n_dp - 1) * SLOTS)]
        sends.append(lambda: wait_bytes(part, a2a_s.at[k], a2a_r.at[k]).wait_send())
        come = dst.at[pl.ds(0, (n_dp - 1) * SLOTS)]
        flight["a2a", k] = lambda: wait_bytes(come, a2a_s.at[k], a2a_r.at[k]).wait_recv()

    def unpack_arrived(src, dst, rows):
        unit = iota((ROWS, 512), 1) & 15
        for c in range(8):
            acc = jnp.zeros((ROWS, 128), f32)
            for L in [l for (l, d) in COMBOS if d == c]:
                lo = c * CAP - 16 * L
                hit = (meta_t[L:L + 1, :] == (iota((ROWS, 512), 0) + 1).astype(f32)) & (unit >= lo) & (unit < lo + CAP)
                acc = acc + dot(one(hit), src[:, L * 128:L * 128 + 128])
            dst[rows, c * 128:c * 128 + 128] = acc.astype(bf16)

    def pack_back(src, dst):
        @pl.loop(0, 4)
        def _(rb):
            rows = pl.ds(al(rb, 128), 128)
            meta = recv_x[rows, 384:512].astype(f32)
            unit = iota((128, ROWS), 0) & 15
            lane = (iota((128, ROWS), 1) + 1).astype(f32)
            for L in range(3):
                acc = jnp.zeros((128, 128), f32)
                mine = meta[:, L:L + 1] == lane
                for c in [c for (l, c) in COMBOS if l == L]:
                    lo = c * CAP - 16 * L
                    acc = acc + dot(one(mine & (unit >= lo) & (unit < lo + CAP)), src[:, c * 128:c * 128 + 128])
                dst[rows, L * 128:L * 128 + 128] = acc.astype(bf16)

    def unpack_home(src, dst):
        rank, base = rank_s[:, 0:1], rank_s[:, 1:2]
        lanes = iota((ROWS, 512), 1)
        for c in range(8):
            acc = jnp.zeros((ROWS, 128), f32)
            for L in [l for (l, d) in COMBOS if d == c]:
                v = rank + (c * CAP - 16 * L)
                idx = jnp.where((v >= 0) & (v < 16), base + v, -1)
                acc = acc + dot(one(lanes == idx), src[:, L * 128:L * 128 + 128])
            dst[:, c * 128:c * 128 + 128] = acc.astype(bf16)

    def finish():
        for f in sends:
            f()

    loads[0].wait()
    pack_out(tok, send_x, True)
    pl.semaphore_wait(bar, n_dp - 1 + 3)
    a2a_start(0, send_x, recv_x)
    loads[1].wait()
    pack_out(cot, send_g, False)

    seg_row = seg_ref[...]
    seg_col = jnp.transpose(jnp.broadcast_to(seg_row.astype(f32), (128, GROUP))).astype(i32)
    for b in range(4):
        sc = seg_col[b * 128:b * 128 + 128, 0:1]
        ok = (sc == seg_row) & (iota((128, GROUP), 1) <= iota((128, GROUP), 0) + b * 128)
        msk[b * 128:b * 128 + 128, :] = jnp.where(ok, 1.0, 0.0)
    cmb[...] = jnp.zeros_like(cmb)

    own = pl.ds(al(cx, 128), 128)
    loads[2].wait()

    @pl.loop(0, 16)
    def _(i):
        rows = pl.ds(al(i, 64), 64)
        w[:, rows, :] = jnp.swapaxes(w_raw[rows].astype(f32), 0, 1).astype(bf16)

    loads[3].wait()
    arrive(("a2a", 0))
    meta_t[...] = jnp.transpose(recv_x[:, 384:512].astype(f32))[:8]
    unpack_arrived(recv_x, xp, pl.ds(0, 128))
    xf = xp[...].astype(f32)
    mean = jnp.mean(xf, axis=1, keepdims=True)
    rstd = lax.rsqrt(jnp.mean((xf - mean) ** 2, axis=1, keepdims=True) + EPS)
    xh = (xf - mean) * rstd
    xhat[...] = xh
    rstd_ref[...] = jnp.broadcast_to(rstd, (ROWS, 128))
    nrm[own, :] = xh.astype(bf16)

    def half(b, k):
        return pl.ds(pl.multiple_of(b * 128 + k * 64, 64), 64)

    def ag(k, buf):
        def to(block, h, way, slot):
            ref = buf.at[half(block, h)]
            return rc(ref, ref, ag_s.at[k], ag_r.at[k, slot], {"ctx": way})

        def go(block, h, way, slot, source):
            to(block, h, way, slot).start()
            sends.append(to(block, h, way, slot).wait_send)
            flight["ag", k, slot] = to(source, h, way, slot).wait_recv

        def start():
            go(cx, 0, right, 0, left)
            go(cx, 1, left, 1, right)
            go(cx, 1, right, 2, left)
            go(cx, 0, left, 3, right)

        def forward():
            arrive(("ag", k, 0))
            go(left, 0, right, 4, opp)
            arrive(("ag", k, 1))
            go(right, 1, left, 5, opp)

        def near():
            arrive(("ag", k, 2), ("ag", k, 3))

        def far():
            arrive(("ag", k, 4), ("ag", k, 5))

        return start, forward, near, far

    lane_lo = iota((128, 128), 1) < 64

    def project(block):
        rows = pl.ds(al(block, 128), 128)
        for h in range(4):
            pre = dot(nrm[rows, :], w[h])
            sig = sigmoid(pre)
            act = pre * sig
            slope[h, rows, :] = sig + act * (1.0 - sig)
            uv[h, rows, :] = act[:, :128].astype(bf16)
            b = act[:, 128:].astype(bf16)
            qk[h, rows, :] = b
            bf = b.astype(f32)
            kq[h, rows, :] = pltpu.roll(bf, 64, 1).astype(bf16)
            qz[h, rows, :] = jnp.where(lane_lo, bf * 0.0625, 0.0).astype(bf16)

    def turn():
        for b in range(4):
            nrm_t[:, b * 128:b * 128 + 128] = jnp.transpose(nrm[b * 128:b * 128 + 128, :].astype(f32)).astype(bf16)

    n_start, n_forward, n_near, n_far = ag(0, nrm)
    g_start, g_forward, g_near, g_far = ag(1, gbuf)
    n_start()
    a2a_start(1, send_g, recv_g)
    project(cx)
    n_forward()
    n_near()
    project(left)
    project(right)
    arrive(("a2a", 1))
    unpack_arrived(recv_g, gbuf, own)
    for t in range(4):
        dg_send[t] = dot_nt(gbuf[own, :], wo[t * 256:t * 256 + 256, :]).astype(bf16)
    for o in (2, 1, 3):
        t = lax.rem(cx + o, 4)
        rc(dg_send.at[t], dg_ref.at[own], dg_s, dg_r, {"ctx": t}).start()
    sends.append(lambda: wait_bytes(dg_ref.at[pl.ds(0, 384)], dg_s, dg_r).wait_send())
    flight["dg"] = lambda: wait_bytes(dg_ref.at[pl.ds(0, 384)], dg_s, dg_r).wait_recv()
    dg_ref[own, :] = dg_send[cx]
    n_far()
    g_start()
    project(opp)

    for j in range(2):
        for half_j in range(2):
            h = 2 * j + half_j
            for b in range(4):
                r, n = slice(b * 128, b * 128 + 128), (b + 1) * 128
                t = dot_nt(qz[h, r, :], kq[h, :n, :])
                th = jnp.tanh(t)
                m = msk[r, :n]
                up = 1.0 + th
                pw = t * up
                p = (pw * m).astype(bf16)
                p_ref[h, r, :n] = p
                sl_ref[h, r, :n] = ((up + pw * (1.0 - th)) * m).astype(bf16)
                pv = dot(p, uv[h, :n, :]).astype(bf16).astype(f32)
                u_here = uv[h, r, :].astype(f32)
                if half_j == 0:
                    attn_ref[r, j * 128:j * 128 + 128] = pltpu.roll(pv, 64, 1)
                    u_ref[r, j * 128:j * 128 + 128] = u_here
                else:
                    attn_ref[r, j * 128:j * 128 + 128] = jnp.where(lane_lo, attn_ref[r, j * 128:j * 128 + 128], pv)
                    u_ref[r, j * 128:j * 128 + 128] = jnp.where(
                        lane_lo, u_ref[r, j * 128:j * 128 + 128], pltpu.roll(u_here, 64, 1)
                    )

    arrive("dg")

    @pl.loop(0, 4)
    def _(b):
        r = pl.ds(al(b, 128), 128)
        dg = dg_ref[r, :].astype(f32)
        a = attn_ref[r, :]
        m = jnp.mean(a, axis=1, keepdims=True)
        ac = a - m
        e = dg * u_ref[r, :]
        lane = iota((128, 128), 1)
        st = jnp.where(lane == 0, m, jnp.sum(ac * ac, axis=1, keepdims=True))
        st = jnp.where(lane == 2, jnp.sum(e, axis=1, keepdims=True), st)
        st = jnp.where(lane == 3, jnp.sum(e * ac, axis=1, keepdims=True), st)
        st_all[cx, :, pl.ds(al(b, 128), 128)] = jnp.transpose(st)[:8]

    for o in range(1, 4):
        rc(st_all.at[cx], st_all.at[cx], st_s, st_r, {"ctx": lax.rem(cx + o, 4)}).start()
    sends.append(lambda: wait_bytes(st_all.at[pl.ds(0, 3)], st_s, st_r).wait_send())
    flight["st"] = lambda: wait_bytes(st_all.at[pl.ds(0, 3)], st_s, st_r).wait_recv()
    turn()
    arrive("st")
    g_forward()
    ms = [st_all[l, 0:1, :] for l in range(4)]
    m2 = (ms[0] + ms[1] + ms[2] + ms[3]) * 0.25
    sq, se, seo = 0.0, 0.0, 0.0
    for l in range(4):
        d = ms[l] - m2
        sq = sq + st_all[l, 1:2, :] + 256.0 * d * d
        se = se + st_all[l, 2:3, :]
        seo = seo + st_all[l, 3:4, :] + d * st_all[l, 2:3, :]
    r2 = lax.rsqrt(sq * (1.0 / WIDTH) + EPS)
    cmb[0:1, :] = m2
    cmb[1:2, :] = r2
    cmb[2:3, :] = se * (1.0 / WIDTH)
    cmb[3:4, :] = r2 * seo * (1.0 / WIDTH)

    for b in range(4):
        r = slice(b * 128, b * 128 + 128)
        tr = jnp.transpose(cmb[:, r])
        r2c = tr[:, 1:2]
        onorm = (attn_ref[r, :] - tr[:, 0:1]) * r2c
        u, dg = u_ref[r, :], dg_ref[r, :].astype(f32)
        gated[r, :] = (onorm * u).astype(bf16)
        du = (dg * onorm).astype(bf16).astype(f32)
        da = r2c * (dg * u - tr[:, 2:3] - onorm * tr[:, 3:4])
        for j in range(2):
            s = slice(j * 128, j * 128 + 128)
            dout[2 * j, r, :] = jnp.where(lane_lo, 0.0, pltpu.roll(da[:, s], 64, 1)).astype(bf16)
            dout[2 * j + 1, r, :] = jnp.where(lane_lo, 0.0, da[:, s]).astype(bf16)
            du_ref[2 * j, r, :] = du[:, s]
            du_ref[2 * j + 1, r, :] = pltpu.roll(du[:, s], 64, 1)

    for o in (2, 1, 3):
        t = lax.rem(cx + o, 4)
        rc(gated.at[pl.ds(al(t, 128), 128)], gfull.at[own], gt_s, gt_r, {"ctx": t}).start()
    sends.append(lambda: wait_bytes(gated.at[pl.ds(0, 384)], gt_s, gt_r).wait_send())
    flight["gt"] = lambda: wait_bytes(gfull.at[pl.ds(0, 384)], gt_s, gt_r).wait_recv()
    gfull[own, :] = gated[own, :]

    yy, zz = lax.div(chip, 4), lax.rem(chip, 4)
    base = core * 512

    def rows_at(start, count):
        return pl.ds(pl.multiple_of(start, count), count)

    def peer(axis, o):
        y2, z2 = (yy, lax.rem(zz + o, 4)) if axis == 0 else (lax.rem(yy + o, 4), zz)
        return lax.rem((zz if axis == 0 else yy) + o, 4), {"dp": (y2 * 4 + z2) * 2 + core}

    def ours(part):
        return (zz, yy) if part == 0 else (yy, zz)

    def begun(stage, p, ref):
        sends.append(lambda: wait_bytes(ref, ar_ss.at[stage, p], ar_rs.at[stage, p]).wait_send())
        flight["ar", stage, p] = lambda: wait_bytes(ref, ar_ss.at[stage, p], ar_rs.at[stage, p]).wait_recv()

    def to_core(stage, p, src, dst):
        rc(src, dst, ar_ss.at[stage, p], ar_rs.at[stage, p], {"dp": chip * 2 + other}).start()
        begun(stage, p, dst)

    def to_axis(stage, p, places, ref):
        @pl.loop(1, 4)
        def _(o):
            for part in range(2):
                axis = part if stage in (1, 4) else 1 - part
                t, dev = peer(axis, o)
                src, dst = places(part, t)
                rc(src, dst, ar_ss.at[stage, p], ar_rs.at[stage, p], dev).start()

        begun(stage, p, ref)

    def ar1(p):
        to_core(0, p, ar_src.at[p, rows_at(other * 512, 512)], ar_c.at[p])

    def ar2(p):
        arrive(("ar", 0, p))

        @pl.loop(0, 4)
        def _(b):
            r = rows_at(b * 128, 128)
            a = ar_src[p, rows_at(base + b * 128, 128), :].astype(f32)
            ar_h[p, r, :] = (a + ar_c[p, r, :].astype(f32)).astype(bf16)

        for part in range(2):
            mine = rows_at(part * 256 + ours(part)[0] * 64, 64)
            ar_r[p, mine, :] = ar_h[p, mine, :]

        def places(part, t):
            return (
                ar_h.at[p, rows_at(part * 256 + t * 64, 64)],
                ar_r.at[p, rows_at(part * 256 + ours(part)[0] * 64, 64)],
            )

        to_axis(1, p, places, ar_r.at[p, pl.ds(0, 384)])

    def ar3(p):
        arrive(("ar", 1, p))
        for part in range(2):
            acc = jnp.zeros((64, 256), f32)
            for k in range(4):
                acc = acc + ar_r[p, part * 256 + k * 64:part * 256 + k * 64 + 64, :].astype(f32)
            ar_q[p, part * 64:part * 64 + 64, :] = acc.astype(bf16)
            mine = rows_at(part * 64 + ours(part)[1] * 16, 16)
            ar_b[p, mine, :] = ar_q[p, mine, :]

        def places(part, t):
            return ar_q.at[p, rows_at(part * 64 + t * 16, 16)], ar_b.at[p, rows_at(part * 64 + ours(part)[1] * 16, 16)]

        to_axis(2, p, places, ar_b.at[p, pl.ds(0, 96)])

    def ar4(p):
        arrive(("ar", 2, p))
        for part in range(2):
            acc = jnp.zeros((16, 256), f32)
            for k in range(4):
                acc = acc + ar_b[p, part * 64 + k * 16:part * 64 + k * 16 + 16, :].astype(f32)
            first, second = ours(part)
            ar_f[p, rows_at(base + part * 256 + first * 64 + second * 16, 16), :] = acc.astype(bf16)

        def places(part, t):
            first, second = ours(part)
            ref = ar_f.at[p, rows_at(base + part * 256 + first * 64 + second * 16, 16)]
            return ref, ref

        to_axis(3, p, places, ar_f.at[p, pl.ds(0, 96)])

    def ar5(p):
        arrive(("ar", 3, p))

        def places(part, t):
            ref = ar_f.at[p, rows_at(base + part * 256 + ours(part)[0] * 64, 64)]
            return ref, ref

        to_axis(4, p, places, ar_f.at[p, pl.ds(0, 384)])

    def ar6(p):
        arrive(("ar", 4, p))
        ref = ar_f.at[p, rows_at(base, 512)]
        to_core(5, p, ref, ref)

    stores = []

    def ar7(p):
        arrive(("ar", 5, p))
        stores.append(pltpu.make_async_copy(ar_f.at[p], ar_hbm.at[p], out_s.at[p]))
        stores[-1].start()

    def backward(h):
        for b in range(4):
            r, n = slice(b * 128, b * 128 + 128), (b + 1) * 128
            dw = dot_nt(dout[h, r, :], uv[h, :n, :])
            ds = (dw * sl_ref[h, r, :n].astype(f32)).astype(bf16)
            ds_ref[r, :n] = ds
            dq_ref[r, :] = dot(ds, qk[h, :n, :])
        for b in range(4):
            r, c = slice(b * 128, b * 128 + 128), slice(b * 128, 512)
            dv = dot_tn(p_ref[h, c, r], dout[h, c, :])
            dk = dot_tn(ds_ref[c, r], qk[h, c, :])
            d1 = jnp.where(lane_lo, du_ref[h, r, :], dv)
            d2 = pltpu.roll(jnp.where(lane_lo, dk, dq_ref[r, :]), 64, 1) * 0.0625
            dpre[h, r, 0:128] = (d1 * slope[h, r, 0:128]).astype(bf16)
            dpre[h, r, 128:256] = (d2 * slope[h, r, 128:256]).astype(bf16)

    def piece(h):
        for q in range(4):
            acc = dot(nrm_t[q * 256:q * 256 + 256, :], dpre[h])
            ar_src[h + 1, q * 256:q * 256 + 256, :] = acc.astype(bf16)
        ar1(h + 1)

    def dnorm(block, dst):
        rows = pl.ds(al(block, 128), 128)

        for cb in range(4):
            s = slice(cb * 256, cb * 256 + 256)
            acc = dot_nt(dpre[0, rows, :], w[0, s, :])
            for h in range(1, 4):
                acc = acc + dot_nt(dpre[h, rows, :], w[h, s, :])
            dst[:, s] = acc.astype(dst.dtype)

    lo, hi = pl.ds(0, 64), pl.ds(64, 64)

    def rs_go(src, dst, k, way):
        c = rc(src, dst, rs_s.at[k], rs_r.at[k], {"ctx": way})
        c.start()
        sends.append(c.wait_send)
        flight["rs", k] = c.wait_recv

    backward(0)
    piece(0)
    backward(1)
    ar2(1)
    piece(1)
    g_near()
    g_far()
    for cb in range(4):
        ar_src[0, cb * 256:cb * 256 + 256, :] = dot_tn(gated[...], gbuf[:, cb * 256:cb * 256 + 256]).astype(bf16)
    ar1(0)
    ar2(2)
    backward(2)
    ar3(1)
    ar2(0)
    piece(2)
    ar3(2)
    backward(3)
    ar2(3)
    ar4(1)
    ar3(0)
    piece(3)

    to_far, to_right, to_left = rs_send.at[0], rs_send.at[1], rs_send.at[2]
    dnorm(opp, to_far)
    rs_go(to_far.at[lo], rs1.at[0], 0, right)
    rs_go(to_far.at[hi], rs1.at[1], 1, left)
    ar5(1)
    ar4(2)
    dnorm(right, to_right)
    rs_go(to_right.at[hi], rs2.at[0, hi], 2, right)
    ar2(4)
    ar3(3)
    dnorm(left, to_left)
    rs_go(to_left.at[lo], rs2.at[1, lo], 3, left)
    ar4(0)
    ar5(2)
    arrive(("rs", 0))
    to_right[lo, :] = (to_right[lo, :].astype(f32) + rs1[0].astype(f32)).astype(bf16)
    rs_go(to_right.at[lo], rs2.at[0, lo], 4, right)
    arrive(("rs", 1))
    to_left[hi, :] = (to_left[hi, :].astype(f32) + rs1[1].astype(f32)).astype(bf16)
    rs_go(to_left.at[hi], rs2.at[1, hi], 5, left)
    ar3(4)
    ar4(3)
    ar5(0)
    ar6(1)
    arrive("gt")
    for cb in range(4):
        s = slice(cb * 256, cb * 256 + 256)
        acc = xp[:, s].astype(f32)
        for c in range(4):
            acc = acc + dot(gfull[c * 128:c * 128 + 128, :], wo[c * 256:c * 256 + 256, s])
        yd[:, s] = acc.astype(bf16)
    pack_back(yd, send_y)

    ar4(4)
    ar5(3)
    ar6(2)
    dnorm(cx, rs_own)
    ar5(4)
    a2a_start(2, send_y, recv_y)
    ar6(0)
    ar7(1)
    arrive(("rs", 2), ("rs", 3), ("rs", 4), ("rs", 5))
    dn = rs_own[...] + rs2[0].astype(f32) + rs2[1].astype(f32)
    xh2 = xhat[...]
    mean_d = jnp.mean(dn, axis=1, keepdims=True)
    mean_dx = jnp.mean(dn * xh2, axis=1, keepdims=True)
    dx = gbuf[own, :].astype(f32) + rstd_ref[:, 0:1] * (dn - mean_d - xh2 * mean_dx)
    yd[...] = dx.astype(bf16)
    pack_back(yd, send_d)
    a2a_start(3, send_d, recv_d)
    ar6(3)
    ar7(2)
    arrive(("a2a", 2))
    unpack_home(recv_y, y_out)
    stores.append(pltpu.make_async_copy(y_out, y_hbm, out_s.at[PIECES]))
    stores[-1].start()
    ar6(4)
    ar7(0)
    ar7(3)
    ar7(4)
    arrive(("a2a", 3))
    for c in stores:
        c.wait()
    finish()


def last(scale, y, recv, pos_ref, ar, y_out, dx_out, proj, out):
    i = pl.program_id(0)
    y_out[...] = y[...]
    pos_l = jnp.broadcast_to(pos_ref[...], (ROWS, ROWS))
    pos_s = jnp.transpose(pos_l.astype(f32)).astype(i32)
    tgt_l, tgt_s = lax.shift_right_logical(pos_l, 9), lax.shift_right_logical(pos_s, 9)
    before = (tgt_l == tgt_s) & (iota((ROWS, ROWS), 1) < iota((ROWS, ROWS), 0))
    rank = jnp.sum(jnp.where(before, 1.0, 0.0), axis=1, keepdims=True).astype(i32)
    base = tgt_s[:, 0:1] * SLOTS
    lanes = iota((ROWS, 512), 1)
    for k in range(2):
        acc = jnp.zeros((ROWS, 128), f32)
        for L in range(3):
            v = rank + ((2 * i + k) * CAP - 16 * L)
            idx = jnp.where((v >= 0) & (v < 16), base + v, -1)
            acc = acc + dot(one(lanes == idx), recv[:, L * 128:L * 128 + 128])
        dx_out[:, k * 128:k * 128 + 128] = acc.astype(bf16)
    out[...] = ar[0].astype(f32) * scale
    for q in range(8):
        r = slice(q * 32, q * 32 + 32)
        proj[r] = jnp.swapaxes(ar[1:, r, :].astype(f32) * scale, 0, 1)


def shards(tokens, cotangent, packed_pos, segment_ids, w_proj, w_out):
    n_dp = lax.axis_size("dp")
    vmem, sem = pltpu.VMEM, pltpu.SemaphoreType.DMA
    scratch = [
        vmem((128, 1024), bf16), vmem((PIECES, 1024, 256), bf16), sem((PIECES + 1,)),
        vmem((128, 1024), bf16), vmem((128, 1024), bf16), vmem((1024, 4, 256), bf16), vmem((4, 1024, 256), bf16),
        vmem((1024, 1024), bf16), sem((4,)),
        vmem((512, 512), bf16), vmem((512, 512), bf16),
        vmem((512, 384), bf16), vmem((512, 384), bf16),
        vmem((512, 384), bf16), vmem((512, 384), bf16),
        vmem((512, 384), bf16),
        vmem((8, 512), f32), vmem((128, 128), i32),
        vmem((128, 1024), bf16), vmem((128, 1024), f32), vmem((128, 128), f32),
        vmem((512, 1024), bf16), vmem((1024, 512), bf16), vmem((512, 1024), bf16),
        vmem((512, 512), f32), vmem((4, 512, 256), f32),
        vmem((4, 512, 128), bf16), vmem((4, 512, 128), bf16),
        vmem((4, 512, 128), bf16), vmem((4, 512, 128), bf16),
        vmem((4, 512, 512), bf16), vmem((4, 512, 512), bf16),
        vmem((512, 512), bf16), vmem((512, 128), f32),
        vmem((512, 256), f32), vmem((512, 256), f32), vmem((512, 256), bf16),
        vmem((4, 8, 512), f32), vmem((128, 512), f32),
        vmem((512, 256), bf16), vmem((512, 256), bf16),
        vmem((4, 512, 128), bf16), vmem((4, 512, 128), f32), vmem((4, 512, 256), bf16),
        vmem((4, 128, 256), bf16),
        vmem((128, 1024), bf16),
        vmem((PIECES, 1024, 256), bf16), vmem((PIECES, 512, 256), bf16),
        vmem((PIECES, 512, 256), bf16), vmem((PIECES, 512, 256), bf16),
        vmem((PIECES, 128, 256), bf16), vmem((PIECES, 128, 256), bf16),
        vmem((3, 128, 1024), bf16), vmem((128, 1024), f32),
        vmem((2, 64, 1024), bf16), vmem((2, 128, 1024), bf16),
        sem((4,)), sem((4,)), sem((2,)), sem((2, 6)), sem, sem, sem, sem, sem, sem,
        sem((6, PIECES)), sem((6, PIECES)), sem((6,)), sem((6,)),
    ]
    spec, free = pl.BlockSpec(memory_space=pltpu.VMEM), pl.BlockSpec(memory_space=pl.ANY)
    pos = packed_pos.reshape(1, ROWS)
    y, dx, ar = pl.pallas_call(
        functools.partial(kernel, n_dp),
        out_shape=[
            jax.ShapeDtypeStruct((ROWS, WIDTH), bf16),
            jax.ShapeDtypeStruct((512, 384), bf16),
            jax.ShapeDtypeStruct((PIECES, 1024, 256), bf16),
        ],
        in_specs=[free, free, spec, spec, free, free],
        out_specs=[free, spec, free],
        scratch_shapes=scratch,
        compiler_params=pltpu.CompilerParams(
            collective_id=0, has_side_effects=True, vmem_limit_bytes=60 * 1024 * 1024
        ),
        cost_estimate=pl.CostEstimate(flops=6 * 10**9, bytes_accessed=12 * 10**6, transcendentals=3 * 10**6),
    )(tokens, cotangent, pos, segment_ids, w_proj, w_out)
    scale = (ROWS * 4 * n_dp) ** (-0.5)
    return pl.pallas_call(
        functools.partial(last, scale),
        grid=(4,),
        out_shape=[
            jax.ShapeDtypeStruct((ROWS, WIDTH), bf16),
            jax.ShapeDtypeStruct((ROWS, WIDTH), bf16),
            jax.ShapeDtypeStruct((1024, 4, 256), f32),
            jax.ShapeDtypeStruct((256, WIDTH), f32),
        ],
        in_specs=[
            pl.BlockSpec((32, WIDTH), lambda i: (i, 0)),
            pl.BlockSpec((512, 384), lambda i: (0, 0)),
            pl.BlockSpec((1, ROWS), lambda i: (0, 0)),
            pl.BlockSpec((PIECES, 256, 256), lambda i: (0, i, 0)),
        ],
        out_specs=[
            pl.BlockSpec((32, WIDTH), lambda i: (i, 0)),
            pl.BlockSpec((ROWS, 256), lambda i: (0, i)),
            pl.BlockSpec((256, 4, 256), lambda i: (i, 0, 0)),
            pl.BlockSpec((256, 256), lambda i: (0, i)),
        ],
        compiler_params=pltpu.CompilerParams(vmem_limit_bytes=60 * 1024 * 1024),
        cost_estimate=pl.CostEstimate(flops=10**8, bytes_accessed=10 * 10**6, transcendentals=0),
    )(y, dx, pos, ar)


def solution(mesh):
    return jax.shard_map(
        shards,
        mesh=mesh,
        in_specs=(
            P(("dp", "ctx"), None),
            P(("dp", "ctx"), None),
            P(("dp", "ctx")),
            P("dp", None),
            P(None, "ctx", None),
            P(),
        ),
        out_specs=(
            P(("dp", "ctx"), None),
            P(("dp", "ctx"), None),
            P(None, "ctx", None),
            P("ctx", None),
        ),
        check_vma=False,
    )
```
